256 devices in a mesh: slab: 16 (over z, y_hi), pencil: 16 (over x, y_lo, core).
Axes of the slice: x: 4, y: 4 (y_hi: 2, y_lo: 2; y = y_hi * 2 + y_lo), z: 8, core: 2. Of those that a mesh axis runs over, the one named last changes fastest.
Arguments:
- layer_input: bfloat16 [32, 64, 256, 256], P(None, 'slab', 'pencil'), may hold values from -6 to 6
- pre_activation: bfloat16 [32, 64, 256, 256], P(None, 'slab', 'pencil'), may hold values from -6 to 6
- coefficient: bfloat16 [64, 256, 256], P('slab', 'pencil'), may hold values from 0.5 to 2.5
- source: bfloat16 [64, 256, 256], P('slab', 'pencil'), may hold values from -6 to 6
- projection: float32 [32], replicated, may hold values from -1 to 1
- pointwise: bfloat16 [32, 32], replicated, may hold values from -1 to 1
- spectral_weight: bfloat16 [2, 32, 32, 32, 512], P(None, 'slab', 'pencil'), may hold values from -12 to 12
Outputs:
- input_grad: bfloat16 [32, 64, 256, 256], P(None, 'slab', 'pencil')
- weight_grad: bfloat16 [2, 32, 32, 32, 512], P(None, 'slab', 'pencil')
The draws below stay inside these ranges and needn't reach their ends.
All inputs are finite; a program needn't handle non-finite values.
Results may differ from the reference program's by a relative error of at most 0.0013.
Values sent between devices are 32-bit elements; how exact they have to be, the bound alone decides.
No kernel may reach another device: no remote copies, remote signals or barrier semaphores. Data moves between devices by JAX's collectives and lax.ppermute only.
A program may use at most 128 MiB of HBM per device.

```python
import jax
import jax.numpy as jnp
from jax import lax

C = 32
NZ = 256
MX = 16
MY = 16
MZ = 16
CX = 4
KX = 32
KY = 32
NX = 64
NY = 256
N_SLAB = 16


def level_of(own_key, dims, cuts, smallest, high):
    def one(position, parts):
        steps = jax.random.uniform(jax.random.fold_in(jax.random.fold_in(own_key, 6), position), (parts,), jnp.float32, smallest / len(cuts), high / len(cuts))
        return jnp.repeat(jnp.exp(steps), dims[position] // parts).reshape((-1,) + (1,) * (len(dims) - position - 1))

    loudness = one(*cuts[0])
    for cut in cuts[1:]:
        loudness = loudness * one(*cut)
    return loudness


def noise(stream_key, shape, deviation, bound, shards=(), held_as=jnp.bfloat16):
    loudness = level_of(stream_key, shape, shards, -0.22, 0.18) if shards else 1.0
    result = jax.random.normal(stream_key, shape, jnp.float32) * deviation * loudness
    return jnp.minimum(jnp.maximum(result, -bound), bound).astype(held_as)


def setup_inputs(seed: int = 0) -> dict:
    seeds = jax.random.split(jax.random.key(seed), 8)
    return {
        "layer_input": noise(seeds[0], (C, NX, NY, NZ), 1.0, 6.0, ((1, 16), (2, 16))),
        "pre_activation": noise(seeds[1], (C, NX, NY, NZ), 1.0, 6.0, ((1, 16), (2, 16))),
        "coefficient": jnp.clip(0.5 + 2.0 * jax.random.uniform(seeds[2], (NX, NY, NZ), jnp.float32) ** level_of(seeds[2], (NX, NY, NZ), ((0, 16), (1, 16)), -0.2, 0.2), 0.5, 2.5).astype(jnp.bfloat16),
        "source": noise(seeds[3], (NX, NY, NZ), 1.0, 6.0, ((0, 16), (1, 16))),
        "projection": noise(seeds[4], (C,), C ** -0.5, 1.0, (), jnp.float32),
        "pointwise": noise(seeds[5], (C, C), C ** -0.5, 1.0),
        "spectral_weight": noise(seeds[6], (2, KX, KY, C, MZ * C), 2.0, 12.0, ((1, 16), (2, 16))),
    }


highest = lax.Precision.HIGHEST

def exact_gelu(inputs):
    return jax.nn.gelu(inputs, approximate=False)

def smooth_grid(values):
    for axis_number in range(3):
        values = 0.5 * jnp.roll(values, 1, axis=axis_number) + values + 0.5 * jnp.roll(values, -1, axis=axis_number)
    return values

def operate(values, coef_values):
    return 16.0 / 3.0 * values - 2.0 / 3.0 * smooth_grid(values) - coef_values * values

def reference(layer_input, pre_activation, coefficient, source, projection, pointwise, spectral_weight):
    coef_values = coefficient.astype(jnp.float32)
    source_values = source.astype(jnp.float32)

    def add_channel(running, channel_index):
        term = projection[channel_index] * exact_gelu(pre_activation[channel_index].astype(jnp.float32))
        return (running + term, None)
    field, _ = lax.scan(add_channel, jnp.zeros((NX, NY, NZ), jnp.float32), jnp.arange(C, dtype=jnp.int32))
    residual = operate(field, coef_values) - source_values
    field_grad = operate(residual, coef_values)
    index_x = jnp.concatenate([jnp.arange(MX), NX - MX + jnp.arange(MX)]).astype(jnp.int32)
    index_y = jnp.concatenate([jnp.arange(MY), NY - MY + jnp.arange(MY)]).astype(jnp.int32)

    def channel_modes(values):
        spectrum = jnp.fft.rfftn(values, axes=(0, 1, 2))
        spectrum = jnp.take(spectrum, index_x, axis=0)
        spectrum = jnp.take(spectrum, index_y, axis=1)
        return spectrum[:, :, :MZ]

    def input_channel(channel_index):
        return channel_modes(layer_input[channel_index].astype(jnp.float32))

    def grad_channel(channel_index):
        _, pullback = jax.vjp(exact_gelu, pre_activation[channel_index].astype(jnp.float32))
        return channel_modes(pullback(projection[channel_index] * field_grad)[0])
    channel_list = jnp.arange(C, dtype=jnp.int32)
    input_modes = lax.map(input_channel, channel_list)
    grad_modes = lax.map(grad_channel, channel_list)
    input_t = jnp.transpose(input_modes, (1, 2, 0, 3))
    grad_t = jnp.transpose(grad_modes, (1, 2, 3, 0))
    scale = jnp.where(jnp.arange(MZ) == 0, 1.0, 2.0).astype(jnp.float32) / (NX * NY * NZ)
    product = input_t[..., None] * jnp.conj(grad_t)[:, :, None]
    grad_real = scale[:, None] * jnp.real(product)
    grad_imag = -scale[:, None] * jnp.imag(product)
    weight_grad = jnp.stack([grad_real, grad_imag]).reshape(2, KX, KY, C, MZ * C).astype(jnp.bfloat16)
    weights = spectral_weight.astype(jnp.float32).reshape(2, KX, KY, C, MZ, C)
    conj_weight = weights[0] - 1j * weights[1]
    back_modes = lax.optimization_barrier(jnp.sum(conj_weight * grad_t[:, :, None], axis=-1))

    def channel_spatial(channel_index):
        grid = jnp.zeros((NX, NY, NZ // 2 + 1), back_modes.dtype)
        grid = grid.at[index_x[:, None], index_y[None, :], :MZ].set(back_modes[:, :, channel_index, :])
        return jnp.fft.irfftn(grid, s=(NX, NY, NZ), axes=(0, 1, 2))
    spectral_part = lax.map(channel_spatial, channel_list)
    pointwise_values = pointwise.astype(jnp.float32)

    def block_out(block_index):
        first_x = (block_index * CX).astype(jnp.int32)
        pre_block = lax.dynamic_slice_in_dim(pre_activation, first_x, CX, 1).astype(jnp.float32)
        grad_block = lax.dynamic_slice_in_dim(field_grad, first_x, CX, 0)
        _, pullback = jax.vjp(exact_gelu, pre_block)
        act_block = pullback(projection[:, None, None, None] * grad_block[None])[0]
        local_part = jnp.dot(pointwise_values, act_block.reshape(C, -1), precision=highest).reshape(act_block.shape)
        spec_block = lax.dynamic_slice_in_dim(spectral_part, first_x, CX, 1)
        return (spec_block + local_part).astype(jnp.bfloat16)
    blocks = lax.map(block_out, jnp.arange(N_SLAB, dtype=jnp.int32))
    input_grad = jnp.moveaxis(blocks, 0, 1).reshape(C, NX, NY, NZ)
    return (input_grad, weight_grad)
```

```python
import functools
import math

import jax
import jax.numpy as jnp
import ml_dtypes
import numpy as np
from jax import lax
from jax.experimental import pallas as pl
from jax.experimental.pallas import tpu as pltpu
from jax.sharding import PartitionSpec as P

F32 = jnp.float32
BF16 = jnp.bfloat16
C, CX, CY, NZ = 32, 4, 16, 256
NX, NY = 64, 256
N = 16
KZ = 16
LANES = CX * C
CELLS = float(NX * NY * NZ)
VMEM_LIMIT = 40 * 1024 * 1024


def split_2(table):
    high = table.astype(ml_dtypes.bfloat16)
    low = (table - high.astype(np.float64)).astype(ml_dtypes.bfloat16)
    return high, low


def depth_tables():
    angles = 2.0 * math.pi * ((np.arange(KZ)[:, None] * np.arange(NZ)[None, :]) % NZ) / NZ
    table = np.concatenate([np.cos(angles), -np.sin(angles)], axis=0)
    high, low = split_2(table)
    return np.concatenate([high, low], axis=0), np.concatenate([high, high, low], axis=0)


def wave(index):
    return index if index < 16 else index - 32


def pencil_phases():
    position = 16.0 * np.arange(N)[:, None] + 7.5
    angles = 2.0 * math.pi * np.arange(17)[None, :] * position / NY
    return np.concatenate([np.cos(angles), np.sin(angles)], axis=1).astype(np.float32).reshape(-1)


def slab_tables():
    forward = np.zeros((N, N, 4, 2, LANES))
    backward = np.zeros((N, N, 4, 2, LANES))
    for position in range(N):
        for other in range(N):
            for shift in range(4):
                for group in range(4):
                    k = wave(2 * other + group // 2)
                    lanes = slice(group * C, (group + 1) * C)
                    x = 4 * position + (group - shift) % 4
                    angle = 2.0 * math.pi * ((k * x) % NX) / NX
                    cos, sin = math.cos(angle), math.sin(angle)
                    forward[position, other, shift, 0, lanes] = cos if group % 2 == 0 else -sin
                    forward[position, other, shift, 1, lanes] = sin if group % 2 == 0 else cos
                    x = 4 * position + (group + shift) % 4
                    angle = 2.0 * math.pi * ((k * x) % NX) / NX
                    cos, sin = math.cos(angle), math.sin(angle)
                    backward[position, other, shift, 0, lanes] = cos if group % 2 == 0 else -sin
                    backward[position, other, shift, 1, lanes] = sin if group % 2 == 0 else cos
    shape = (N, N * 8, LANES)
    return forward.astype(np.float32).reshape(shape), backward.astype(np.float32).reshape(shape)


DEPTH_FORWARD, DEPTH_BACKWARD = depth_tables()
PENCIL_PHASES = pencil_phases()
SLAB_FORWARD, SLAB_BACKWARD = slab_tables()


def normal_tail(values):
    size = jnp.abs(values)
    bell = jnp.exp(-0.5 * values * values)
    denominator = 1.0 + (0.3275911 / math.sqrt(2.0)) * size
    t = pl.reciprocal(denominator, approx=True)
    t = t * (2.0 - denominator * t)
    poly = 0.5 * 1.061405429 * t - 0.5 * 1.453152027
    poly = poly * t + 0.5 * 1.421413741
    poly = poly * t - 0.5 * 0.284496736
    poly = poly * t + 0.5 * 0.254829592
    return bell, poly * t * bell


def field_kernel(pre_ref, coef_ref, source_ref, proj_ref, field_ref, up_ref, down_ref):
    def add_channel(c, total):
        values = pre_ref[c].astype(F32)
        _, tail = normal_tail(values)
        return total + proj_ref[c] * (jnp.maximum(values, 0.0) - jnp.abs(values) * tail)

    total = lax.fori_loop(0, C, add_channel, jnp.zeros((CX, CY, NZ), F32), unroll=2)
    field_ref[...] = total
    up_ref[0:2] = total[2:4]
    down_ref[0:2] = total[0:2]
    up_ref[2] = coef_ref[3].astype(F32)
    up_ref[3] = source_ref[3].astype(F32)
    down_ref[2] = coef_ref[0].astype(F32)
    down_ref[3] = source_ref[0].astype(F32)


def slope_kernel(pre_ref, proj_ref, slope_ref):
    def one_channel(c, carry):
        values = pre_ref[c].astype(F32)
        bell, tail = normal_tail(values)
        below = jnp.where(values >= 0.0, 1.0 - tail, tail)
        slope = proj_ref[c] * (below + values * (bell * (1.0 / math.sqrt(2.0 * math.pi))))
        for x in range(CX):
            for side in range(2):
                piece = slope[x, :, side * 128 : (side + 1) * 128]
                slope_ref[side, pl.ds(x * C + c, CY, stride=LANES), :] = piece
        return carry

    lax.fori_loop(0, C, one_channel, 0, unroll=2)


def nt_dot(left, right):
    return lax.dot_general(left, right, (((1,), (1,)), ((), ())), preferred_element_type=F32)


def tn_dot(left, right):
    return lax.dot_general(left, right, (((0,), (0,)), ((), ())), preferred_element_type=F32)


def pencil_forward(modes_ref, phase_ref, position, out_ref, base):
    for half in range(2):
        sums, diffs = [], []
        for part in range(2):
            rows = pl.ds(part * KZ + 8 * half, 8)
            first = [modes_ref[j, rows, :] for j in range(8)]
            second = [modes_ref[15 - j, rows, :] for j in range(8)]
            sums.append([a + b for a, b in zip(first, second)])
            diffs.append([a - b for a, b in zip(first, second)])
        for k in range(17):
            cosines = [math.cos(2.0 * math.pi * k * (7.5 - j) / NY) for j in range(8)]
            sines = [math.sin(2.0 * math.pi * k * (7.5 - j) / NY) for j in range(8)]
            even = [sum(w * v for w, v in zip(cosines, part)) for part in sums]
            w_cos = phase_ref[position * 34 + k]
            w_sin = phase_ref[position * 34 + 17 + k]
            if k == 0:
                results = [(0, even[0], even[1], w_sin)]
            else:
                odd = [sum(w * v for w, v in zip(sines, part)) for part in diffs]
                results = [(32 - k, even[0] + odd[1], even[1] - odd[0], -w_sin)]
                if k < 16:
                    results.append((k, even[0] - odd[1], even[1] + odd[0], w_sin))
            for index, real, imag, sin in results:
                row = base + (index % 2) * 32 + 8 * half
                out_ref[index // 2, pl.ds(row, 8), :] = w_cos * real + sin * imag
                out_ref[index // 2, pl.ds(row + KZ, 8), :] = w_cos * imag - sin * real


def input_kernel(position_ref, phase_ref, input_ref, table_ref, out_ref, rows_ref, modes_ref):
    for side in range(2):
        piece = input_ref[:, :, :, side * 128 : (side + 1) * 128]
        rows_ref[side] = piece.astype(F32).reshape(C * CX * CY, 128)
    for y in range(CY):
        sides = [
            jnp.concatenate(
                [rows_ref[side, pl.ds(x * CY + y, C, stride=CX * CY), :] for x in range(CX)],
                axis=0,
            )
            for side in range(2)
        ]
        values = jnp.concatenate(sides, axis=1).astype(BF16)
        both = nt_dot(table_ref[...], values)
        modes_ref[y] = both[:32] + both[32:]
    pencil_forward(modes_ref, phase_ref, position_ref[0], out_ref, 0)


def pack_kernel(field_ref, coef_ref, source_ref, before_ref, after_ref, up_ref, down_ref):
    for out_ref, cells, cell in ((up_ref, slice(14, 16), slice(15, 16)), (down_ref, slice(0, 2), slice(0, 1))):
        for x in range(8):
            if x < 2:
                rows = before_ref[x, cells, :]
            elif x < 6:
                rows = field_ref[x - 2, cells, :]
            else:
                rows = after_ref[x - 6, cells, :]
            out_ref[2 * x : 2 * x + 2, :] = rows
        for base, part, own_ref in ((16, 2, coef_ref), (22, 3, source_ref)):
            for x in range(6):
                if x == 0:
                    row = before_ref[part, cell, :]
                elif x == 5:
                    row = after_ref[part, cell, :]
                else:
                    row = own_ref[x - 1].astype(F32)[cell, :]
                out_ref[base + x : base + x + 1, :] = row
        out_ref[28:32, :] = jnp.zeros((4, NZ), F32)


def smooth(values):
    values = values + 0.5 * (pltpu.roll(values, 1, 2) + pltpu.roll(values, NZ - 1, 2))
    values = values + 0.5 * (pltpu.roll(values, 1, 1) + pltpu.roll(values, 31, 1))
    return 0.5 * (values[:-2] + values[2:]) + values[1:-1]


def grad_kernel(
    position_ref,
    phase_ref,
    field_ref,
    coef_ref,
    source_ref,
    before_ref,
    after_ref,
    low_ref,
    high_ref,
    slope_ref,
    table_ref,
    input_part_ref,
    out_ref,
    act_ref,
    wide_field,
    wide_coef,
    wide_source,
    grad_ref,
    modes_ref,
):
    own = slice(8, 24)
    wide_field[...] = jnp.zeros_like(wide_field)
    wide_coef[...] = jnp.zeros_like(wide_coef)
    wide_source[...] = jnp.zeros_like(wide_source)
    wide_field[0:2, own, :] = before_ref[0:2]
    wide_field[2:6, own, :] = field_ref[...]
    wide_field[6:8, own, :] = after_ref[0:2]
    for x in range(8):
        wide_field[x, 6:8, :] = low_ref[2 * x : 2 * x + 2, :]
        wide_field[x, 24:26, :] = high_ref[2 * x : 2 * x + 2, :]
    for wide, own_ref, part, base in ((wide_coef, coef_ref, 2, 16), (wide_source, source_ref, 3, 22)):
        wide[0, own, :] = before_ref[part]
        wide[1:5, own, :] = own_ref[...].astype(F32)
        wide[5, own, :] = after_ref[part]
        for x in range(6):
            wide[x, 7:8, :] = low_ref[base + x : base + x + 1, :]
            wide[x, 24:25, :] = high_ref[base + x : base + x + 1, :]
    field = wide_field[...]
    center = field[1:7]
    residual = (16.0 / 3.0 - wide_coef[...]) * center - (2.0 / 3.0) * smooth(field) - wide_source[...]
    grad_ref[...] = (16.0 / 3.0 - wide_coef[1:5]) * residual[1:5] - (2.0 / 3.0) * smooth(residual)
    for y in range(CY):
        grads = []
        for x in range(CX):
            rows = slice(y * LANES + x * C, y * LANES + (x + 1) * C)
            slope = jnp.concatenate([slope_ref[0, rows, :], slope_ref[1, rows, :]], axis=1)
            grads.append(slope * grad_ref[x, 8 + y : 9 + y, :])
        act = jnp.concatenate(grads, axis=0)
        high = act.astype(BF16)
        low = (act - high.astype(F32)).astype(BF16)
        act_ref[y, 0:LANES, :] = high
        act_ref[y, LANES : 2 * LANES, :] = low
        both = nt_dot(table_ref[...], high)
        modes_ref[y] = both[:32] + both[32:] + nt_dot(table_ref[0:32, :], low)
    out_ref[:, 0:64, :] = input_part_ref[...]
    pencil_forward(modes_ref, phase_ref, position_ref[0], out_ref, 64)


def local_kernel(pointwise_ref, act_ref, out_ref):
    for y in range(CY):
        out_ref[y] = jnp.dot(pointwise_ref[...], act_ref[y], preferred_element_type=F32)


def slab_forward_kernel(parts_ref, table_ref, out_ref):
    for block in range(4):
        for half in range(2):
            pieces = []
            for part in range(2):
                rows = pl.ds(block * 32 + part * KZ + 8 * half, 8)
                total = parts_ref[0, rows, :]
                for source in range(1, N):
                    total = total + parts_ref[source, rows, :]
                pieces.append([total] + [pltpu.roll(total, 32 * d, 1) for d in range(1, 4)])
            for owner in range(N):
                result = None
                for d in range(4):
                    for part in range(2):
                        row = owner * 8 + d * 2 + part
                        term = pieces[part][d] * table_ref[row : row + 1, :]
                        result = term if result is None else result + term
                out_ref[owner, pl.ds(block * KZ + 8 * half, 8), :] = result


def flat_modes(block, group):
    lane_group = lax.broadcasted_iota(jnp.int32, (KZ, LANES), 1) // C
    row = lax.broadcasted_iota(jnp.int32, (KZ, LANES), 0)
    picked = jnp.where(lane_group == group, block, 0.0)
    picked = picked + pltpu.roll(picked, 64, 1)
    picked = picked + pltpu.roll(picked, 32, 1)
    tiles = [
        jnp.sum(jnp.where(row == 4 * tile + lane_group, picked, 0.0), axis=0, keepdims=True)
        for tile in range(4)
    ]
    return jnp.concatenate(tiles, axis=1)


def split_3(values):
    high = values.astype(BF16)
    rest = values - high.astype(F32)
    middle = rest.astype(BF16)
    low = (rest - middle.astype(F32)).astype(BF16)
    return high, middle, low


def back_kernel(parts_ref, weight_ref, modes_ref, out_ref):
    total = parts_ref[0]
    for source in range(1, N):
        total = total + parts_ref[source]
    modes_ref[...] = total
    rows = lax.broadcasted_iota(jnp.int32, (KZ, KZ * C), 0)
    lanes = lax.broadcasted_iota(jnp.int32, (KZ, KZ * C), 1)
    mask = jnp.where(lanes // C == rows, 1.0, 0.0).astype(BF16)
    kz = lax.broadcasted_iota(jnp.int32, (KZ, LANES), 0)
    scale = jnp.where(kz == 0, 1.0 / CELLS, 2.0 / CELLS)
    for ky in range(2):
        block = total[32 + ky * KZ : 32 + (ky + 1) * KZ]
        products = []
        for kx in range(2):
            real, imag = flat_modes(block, 2 * kx), flat_modes(block, 2 * kx + 1)
            w_real = weight_ref[0, kx, ky].astype(F32)
            w_imag = weight_ref[1, kx, ky].astype(F32)
            products.append(w_real * real + w_imag * imag)
            products.append(w_real * imag - w_imag * real)
        high, middle, low = split_3(jnp.concatenate(products, axis=0))
        back = scale * (nt_dot(mask, high) + nt_dot(mask, middle) + nt_dot(mask, low))
        for device in range(N):
            out_ref[device, ky * KZ : (ky + 1) * KZ, :] = back


def weight_grad_kernel(modes_ref, out_ref):
    rows = lax.broadcasted_iota(jnp.int32, (KZ, KZ * C), 0)
    lanes = lax.broadcasted_iota(jnp.int32, (KZ, KZ * C), 1)
    mask = jnp.where(lanes // C == rows, 1.0, 0.0).astype(BF16)
    first = lax.broadcasted_iota(jnp.int32, (1, KZ * C), 1) < C
    scale = jnp.where(first, 1.0 / CELLS, 2.0 / CELLS)
    for ky in range(2):
        inputs = modes_ref[ky * KZ : (ky + 1) * KZ, :]
        grads = modes_ref[32 + ky * KZ : 32 + (ky + 1) * KZ, :]
        high, middle, low = split_3(inputs)
        spread = tn_dot(high, mask) + tn_dot(middle, mask) + tn_dot(low, mask)
        for kx in range(2):
            real = scale * flat_modes(grads, 2 * kx)
            imag = scale * flat_modes(grads, 2 * kx + 1)
            in_real = spread[(2 * kx) * C : (2 * kx + 1) * C]
            in_imag = spread[(2 * kx + 1) * C : (2 * kx + 2) * C]
            out_ref[0, kx, ky] = (in_real * real + in_imag * imag).astype(BF16)
            out_ref[1, kx, ky] = (in_real * imag - in_imag * real).astype(BF16)


def slab_backward_kernel(parts_ref, table_ref, out_ref):
    for ky in range(2):
        for half in range(2):
            totals = [[None] * 4, [None] * 4]
            for source in range(N):
                values = parts_ref[source, pl.ds(ky * KZ + 8 * half, 8), :]
                for d in range(4):
                    for part in range(2):
                        row = source * 8 + d * 2 + part
                        term = values * table_ref[row : row + 1, :]
                        last = totals[part][d]
                        totals[part][d] = term if last is None else last + term
            for part in range(2):
                result = totals[part][0]
                for d in range(1, 4):
                    result = result + pltpu.roll(totals[part][d], 32 * d, 1)
                for device in range(N):
                    out_ref[device, pl.ds(ky * 32 + part * KZ + 8 * half, 8), :] = result


def output_kernel(
    position_ref, phase_ref, parts_ref, local_ref, table_ref, out_ref, modes_ref, rows_ref
):
    position = position_ref[0]
    for half in range(2):
        evens, odds = [], []
        for k in range(17):
            w_cos = phase_ref[position * 34 + k]
            w_sin = phase_ref[position * 34 + 17 + k]

            def turned(index, sin):
                row = (index % 2) * 32 + 8 * half
                real = parts_ref[index // 2, pl.ds(row, 8), :]
                imag = parts_ref[index // 2, pl.ds(row + KZ, 8), :]
                return w_cos * real - sin * imag, w_cos * imag + sin * real

            if k == 0:
                evens.append(turned(0, w_sin))
                odds.append(None)
            elif k == 16:
                real, imag = turned(16, -w_sin)
                evens.append((real, imag))
                odds.append((-real, -imag))
            else:
                plus, minus = turned(k, w_sin), turned(32 - k, -w_sin)
                evens.append((plus[0] + minus[0], plus[1] + minus[1]))
                odds.append((plus[0] - minus[0], plus[1] - minus[1]))
            modes_ref[0, k, 0] = evens[-1][0]
            modes_ref[0, k, 1] = evens[-1][1]
            if k:
                modes_ref[1, k, 0] = odds[-1][0]
                modes_ref[1, k, 1] = odds[-1][1]
        for y in range(8):
            even = [modes_ref[0, 0, 0], modes_ref[0, 0, 1]]
            odd = [None, None]
            for k in range(1, 17):
                angle = 2.0 * math.pi * k * (y - 7.5) / NY
                cos, sin = math.cos(angle), math.sin(angle)
                for part in range(2):
                    even[part] = even[part] + cos * modes_ref[0, k, part]
                    term = sin * modes_ref[1, k, part]
                    odd[part] = term if odd[part] is None else odd[part] + term
            rows = pl.ds(8 * half, 8)
            more = pl.ds(KZ + 8 * half, 8)
            rows_ref[y, rows, :] = even[0] - odd[1]
            rows_ref[y, more, :] = even[1] + odd[0]
            rows_ref[15 - y, rows, :] = even[0] + odd[1]
            rows_ref[15 - y, more, :] = even[1] - odd[0]


def finish_kernel(rows_ref, local_ref, table_ref, out_ref, flat_ref):
    for y in range(CY):
        values = rows_ref[y]
        high = values.astype(BF16)
        low = (values - high.astype(F32)).astype(BF16)
        stacked = jnp.concatenate([high, low, high], axis=0)
        result = tn_dot(stacked, table_ref[...]) + local_ref[y]
        for x in range(CX):
            for side in range(2):
                piece = result[x * C : (x + 1) * C, side * 128 : (side + 1) * 128]
                flat_ref[side, pl.ds(x * CY + y, C, stride=CX * CY), :] = piece
    for side in range(2):
        piece = flat_ref[side].astype(BF16).reshape(C, CX, CY, 128)
        out_ref[:, :, :, side * 128 : (side + 1) * 128] = piece


def last_kernel(
    position_ref, phase_ref, parts_ref, local_ref, table_ref, out_ref, modes_ref, rows_ref, flat_ref
):
    output_kernel(
        position_ref, phase_ref, parts_ref, local_ref, table_ref, out_ref, modes_ref, rows_ref
    )
    finish_kernel(rows_ref, local_ref, table_ref, out_ref, flat_ref)


def call(kernel, name, out, scratch=(), scalars=()):
    def run(*args):
        single = not isinstance(out, list)
        specs = [
            pl.BlockSpec(memory_space=pltpu.SMEM if i in scalars else pltpu.VMEM)
            for i in range(len(args))
        ]
        shapes = [jax.ShapeDtypeStruct(*o) for o in ([out] if single else out)]
        result = pl.pallas_call(
            kernel,
            out_shape=shapes,
            in_specs=specs,
            out_specs=[pl.BlockSpec(memory_space=pltpu.VMEM)] * len(shapes),
            scratch_shapes=[pltpu.VMEM(*s) for s in scratch],
            compiler_params=pltpu.CompilerParams(vmem_limit_bytes=VMEM_LIMIT),
            name=name,
        )(*args)
        return result[0] if single else result

    return run


def shards(
    layer_input, pre_activation, coefficient, source, projection, pointwise, spectral_weight
):
    up = [(i, (i + 1) % N) for i in range(N)]
    down = [(j, i) for i, j in up]
    slab = lax.axis_index("slab")
    pencil = lax.axis_index("pencil").reshape(1)
    phases = jnp.asarray(PENCIL_PHASES)
    depth_forward = jnp.asarray(DEPTH_FORWARD)
    depth_backward = jnp.asarray(DEPTH_BACKWARD)
    slab_forward = lax.dynamic_index_in_dim(jnp.asarray(SLAB_FORWARD), slab, 0, False)
    slab_backward = lax.dynamic_index_in_dim(jnp.asarray(SLAB_BACKWARD), slab, 0, False)
    pointwise_4 = jnp.kron(jnp.eye(CX, dtype=BF16), pointwise)
    pointwise_8 = jnp.concatenate([pointwise_4, pointwise_4], axis=1)

    field, edge_up, edge_down = call(
        field_kernel,
        "field",
        [((CX, CY, NZ), F32), ((4, CY, NZ), F32), ((4, CY, NZ), F32)],
        scalars=(3,),
    )(pre_activation, coefficient, source, projection)
    before = lax.ppermute(edge_up, "slab", up)
    after = lax.ppermute(edge_down, "slab", down)
    side_up, side_down = call(pack_kernel, "pack", [((32, NZ), F32), ((32, NZ), F32)])(
        field, coefficient, source, before, after
    )
    low = lax.ppermute(side_up, "pencil", up)
    high = lax.ppermute(side_down, "pencil", down)
    slope = call(slope_kernel, "slope", ((2, CY * LANES, 128), F32), scalars=(1,))(
        pre_activation, projection
    )
    input_part = call(
        input_kernel,
        "input_modes",
        ((N, 64, LANES), F32),
        scratch=[((2, C * CX * CY, 128), F32), ((CY, 32, LANES), F32)],
        scalars=(0, 1),
    )(pencil, phases, layer_input, depth_forward)
    to_pencil, act = call(
        grad_kernel,
        "grad_modes",
        [((N, 128, LANES), F32), ((CY, 2 * LANES, NZ), BF16)],
        scratch=[
            ((8, 32, NZ), F32),
            ((6, 32, NZ), F32),
            ((6, 32, NZ), F32),
            ((4, 32, NZ), F32),
            ((CY, 32, LANES), F32),
        ],
        scalars=(0, 1),
    )(
        pencil,
        phases,
        field,
        coefficient,
        source,
        before,
        after,
        low,
        high,
        slope,
        depth_forward,
        input_part,
    )
    from_pencil = lax.all_to_all(to_pencil, "pencil", 0, 0, tiled=True)
    local = call(local_kernel, "local", ((CY, LANES, NZ), F32))(pointwise_8, act)
    to_slab = call(slab_forward_kernel, "slab_forward", ((N, 64, LANES), F32))(
        from_pencil, slab_forward
    )
    from_slab = lax.all_to_all(to_slab, "slab", 0, 0, tiled=True)
    modes, to_slab = call(back_kernel, "back", [((64, LANES), F32), ((N, 32, LANES), F32)])(
        from_slab, spectral_weight
    )
    from_slab = lax.all_to_all(to_slab, "slab", 0, 0, tiled=True)
    weight_grad = call(weight_grad_kernel, "weight_grad", (spectral_weight.shape, BF16))(modes)
    to_pencil = call(slab_backward_kernel, "slab_backward", ((N, 64, LANES), F32))(
        from_slab, slab_backward
    )
    from_pencil = lax.all_to_all(to_pencil, "pencil", 0, 0, tiled=True)
    input_grad = call(
        last_kernel,
        "output",
        ((C, CX, CY, NZ), BF16),
        scratch=[
            ((2, 17, 2, 8, LANES), F32),
            ((CY, 32, LANES), F32),
            ((2, C * CX * CY, 128), F32),
        ],
        scalars=(0, 1),
    )(pencil, phases, from_pencil, local, depth_backward)
    return (input_grad, weight_grad)


def solution(mesh):
    return jax.shard_map(
        shards,
        mesh=mesh,
        in_specs=(
            P(None, "slab", "pencil", None),
            P(None, "slab", "pencil", None),
            P("slab", "pencil", None),
            P("slab", "pencil", None),
            P(),
            P(),
            P(None, "slab", "pencil", None, None),
        ),
        out_specs=(P(None, "slab", "pencil", None), P(None, "slab", "pencil", None, None)),
        check_vma=False,
    )
```

```python
import functools
import math

import jax
import jax.numpy as jnp
import ml_dtypes
import numpy as np
from jax import lax
from jax.experimental import pallas as pl
from jax.experimental.pallas import tpu as pltpu
from jax.sharding import PartitionSpec as P

F32 = jnp.float32
BF16 = jnp.bfloat16
C, CX, CY, NZ = 32, 4, 16, 256
NX, NY = 64, 256
N = 16
KZ = 16
LANES = CX * C
CELLS = float(NX * NY * NZ)
VMEM_LIMIT = 24 * 1024 * 1024
PITCH = 68
Y_PITCH = LANES + 8
CHUNKS = 4


def split_2(table):
    high = table.astype(ml_dtypes.bfloat16)
    low = (table - high.astype(np.float64)).astype(ml_dtypes.bfloat16)
    return high, low


def depth_tables():
    angles = 2.0 * math.pi * ((np.arange(KZ)[:, None] * np.arange(NZ)[None, :]) % NZ) / NZ
    table = np.concatenate([np.cos(angles), -np.sin(angles)], axis=0)
    high, low = split_2(table)
    return np.concatenate([high, low], axis=0), np.concatenate([high, high, low], axis=0)


def wave(index):
    return index if index < 16 else index - 32


def pencil_phases():
    position = 16.0 * np.arange(N)[:, None] + 7.5
    angles = 2.0 * math.pi * np.arange(17)[None, :] * position / NY
    return np.concatenate([np.cos(angles), np.sin(angles)], axis=1).astype(np.float32).reshape(-1)


def slab_tables():
    forward = np.zeros((N, N, 4, 2, LANES))
    backward = np.zeros((N, N, 4, 2, LANES))
    for position in range(N):
        for other in range(N):
            for shift in range(4):
                for group in range(4):
                    k = wave(2 * other + group // 2)
                    lanes = slice(group * C, (group + 1) * C)
                    x = 4 * position + (group - shift) % 4
                    angle = 2.0 * math.pi * ((k * x) % NX) / NX
                    cos, sin = math.cos(angle), math.sin(angle)
                    forward[position, other, shift, 0, lanes] = cos if group % 2 == 0 else -sin
                    forward[position, other, shift, 1, lanes] = sin if group % 2 == 0 else cos
                    x = 4 * position + (group + shift) % 4
                    angle = 2.0 * math.pi * ((k * x) % NX) / NX
                    cos, sin = math.cos(angle), math.sin(angle)
                    backward[position, other, shift, 0, lanes] = cos if group % 2 == 0 else -sin
                    backward[position, other, shift, 1, lanes] = sin if group % 2 == 0 else cos
    shape = (N, N * 8, LANES)
    return forward.astype(np.float32).reshape(shape), backward.astype(np.float32).reshape(shape)


DEPTH_FORWARD, DEPTH_BACKWARD = depth_tables()
PENCIL_PHASES = pencil_phases()
SLAB_FORWARD, SLAB_BACKWARD = slab_tables()


def normal_tail(values):
    size = jnp.abs(values)
    bell = jnp.exp(-0.5 * values * values)
    denominator = 1.0 + (0.3275911 / math.sqrt(2.0)) * size
    t = pl.reciprocal(denominator, approx=True)
    t = t * (2.0 - denominator * t)
    poly = 0.5 * 1.061405429 * t - 0.5 * 1.453152027
    poly = poly * t + 0.5 * 1.421413741
    poly = poly * t - 0.5 * 0.284496736
    poly = poly * t + 0.5 * 0.254829592
    return bell, poly * t * bell


def field_kernel(
    pre_hbm,
    coef_hbm,
    source_hbm,
    proj_hbm,
    field_ref,
    up_ref,
    down_ref,
    proj_tile_ref,
    pre_ref,
    coef_ref,
    source_ref,
    proj_ref,
    sems,
):
    size = C // CHUNKS
    copies = [pltpu.make_async_copy(proj_hbm, proj_ref, sems.at[CHUNKS])]
    for i in range(CHUNKS):
        part = pl.ds(i * size, size)
        copies.append(pltpu.make_async_copy(pre_hbm.at[part], pre_ref.at[part], sems.at[i]))
    copies.append(pltpu.make_async_copy(coef_hbm, coef_ref, sems.at[CHUNKS + 1]))
    copies.append(pltpu.make_async_copy(source_hbm, source_ref, sems.at[CHUNKS + 2]))
    for copy in copies:
        copy.start()
    copies[0].wait()
    for c in range(C):
        proj_tile_ref[c : c + 1, :] = jnp.full((1, 128), proj_ref[c], F32)

    def add_channel(c, total):
        values = pre_ref[c].astype(F32)
        _, tail = normal_tail(values)
        return total + proj_ref[c] * (jnp.maximum(values, 0.0) - jnp.abs(values) * tail)

    total = jnp.zeros((CX, CY, NZ), F32)
    for i in range(CHUNKS):
        copies[1 + i].wait()
        total = lax.fori_loop(i * size, (i + 1) * size, add_channel, total, unroll=2)
    copies[-2].wait()
    copies[-1].wait()
    field_ref[...] = total
    up_ref[0:2] = total[2:4]
    down_ref[0:2] = total[0:2]
    up_ref[2] = coef_ref[3].astype(F32)
    up_ref[3] = source_ref[3].astype(F32)
    down_ref[2] = coef_ref[0].astype(F32)
    down_ref[3] = source_ref[0].astype(F32)


def slope_kernel(pre_ref, proj_ref, slope_ref):
    def one_channel(c, carry):
        values = pre_ref[c].astype(F32)
        bell, tail = normal_tail(values)
        below = jnp.where(values >= 0.0, 1.0 - tail, tail)
        slope = below + values * (bell * (1.0 / math.sqrt(2.0 * math.pi)))
        weight = proj_ref[pl.ds(c, 1), :]
        for x in range(CX):
            for side in range(2):
                piece = slope[x, :, side * 128 : (side + 1) * 128] * weight
                slope_ref[side, pl.ds(x * C + c, CY, stride=Y_PITCH), :] = piece
        return carry

    lax.fori_loop(0, C, one_channel, 0, unroll=2)


def nt_dot(left, right):
    return lax.dot_general(left, right, (((1,), (1,)), ((), ())), preferred_element_type=F32)


def tn_dot(left, right):
    return lax.dot_general(left, right, (((0,), (0,)), ((), ())), preferred_element_type=F32)


def pencil_forward(modes_ref, phase_ref, position, out_refs):
    for half in range(2):
        sums, diffs = [], []
        for part in range(2):
            rows = pl.ds(part * KZ + 8 * half, 8)
            first = [modes_ref[j, rows, :] for j in range(8)]
            second = [modes_ref[15 - j, rows, :] for j in range(8)]
            sums.append([a + b for a, b in zip(first, second)])
            diffs.append([a - b for a, b in zip(first, second)])
        for k in range(17):
            cosines = [math.cos(2.0 * math.pi * k * (7.5 - j) / NY) for j in range(8)]
            sines = [math.sin(2.0 * math.pi * k * (7.5 - j) / NY) for j in range(8)]
            even = [sum(w * v for w, v in zip(cosines, part)) for part in sums]
            w_cos = phase_ref[position * 34 + k]
            w_sin = phase_ref[position * 34 + 17 + k]
            if k == 0:
                results = [(0, even[0], even[1], w_sin)]
            else:
                odd = [sum(w * v for w, v in zip(sines, part)) for part in diffs]
                results = [(32 - k, even[0] + odd[1], even[1] - odd[0], -w_sin)]
                if k < 16:
                    results.append((k, even[0] - odd[1], even[1] + odd[0], w_sin))
            for index, real, imag, sin in results:
                row = (index % 2) * 32 + 8 * half
                out_ref = out_refs[index // 2 % 2]
                out_ref[index // 4, pl.ds(row, 8), :] = w_cos * real + sin * imag
                out_ref[index // 4, pl.ds(row + KZ, 8), :] = w_cos * imag - sin * real


def by_core(position, function, own_ref, other_ref):
    @pl.when(position % 2 == 0)
    def _():
        function((own_ref, other_ref))

    @pl.when(position % 2 == 1)
    def _():
        function((other_ref, own_ref))


def input_kernel(
    position_ref,
    phase_ref,
    input_ref,
    table_hbm,
    own_ref,
    other_ref,
    rows_ref,
    modes_ref,
    table_ref,
    sem,
):
    copy = pltpu.make_async_copy(table_hbm, table_ref, sem)
    copy.start()
    for side in range(2):
        for c in range(C):
            piece = input_ref[c, :, :, side * 128 : (side + 1) * 128].astype(F32)
            rows_ref[side, c * PITCH : c * PITCH + CX * CY, :] = piece.reshape(CX * CY, 128)
    copy.wait()
    for y in range(CY):
        sides = [
            jnp.concatenate(
                [rows_ref[side, pl.ds(x * CY + y, C, stride=PITCH), :] for x in range(CX)], axis=0
            )
            for side in range(2)
        ]
        values = jnp.concatenate(sides, axis=1).astype(BF16)
        both = nt_dot(table_ref[...], values)
        modes_ref[y] = both[:32] + both[32:]
    position = position_ref[0]
    forward = functools.partial(pencil_forward, modes_ref, phase_ref, position)
    by_core(position, forward, own_ref, other_ref)


def pack_kernel(field_ref, coef_ref, source_ref, before_ref, after_ref, up_ref, down_ref):
    for out_ref, cells, cell in ((up_ref, slice(14, 16), slice(15, 16)), (down_ref, slice(0, 2), slice(0, 1))):
        for x in range(8):
            if x < 2:
                rows = before_ref[x, cells, :]
            elif x < 6:
                rows = field_ref[x - 2, cells, :]
            else:
                rows = after_ref[x - 6, cells, :]
            out_ref[2 * x : 2 * x + 2, :] = rows
        for base, part, own_ref in ((16, 2, coef_ref), (22, 3, source_ref)):
            for x in range(6):
                if x == 0:
                    row = before_ref[part, cell, :]
                elif x == 5:
                    row = after_ref[part, cell, :]
                else:
                    row = own_ref[x - 1].astype(F32)[cell, :]
                out_ref[base + x : base + x + 1, :] = row
        out_ref[28:32, :] = jnp.zeros((4, NZ), F32)


def smooth(values):
    values = values + 0.5 * (pltpu.roll(values, 1, 2) + pltpu.roll(values, NZ - 1, 2))
    values = values + 0.5 * (pltpu.roll(values, 1, 1) + pltpu.roll(values, 31, 1))
    return 0.5 * (values[:-2] + values[2:]) + values[1:-1]


def act_parts(slope_ref, grad_ref, y):
    grads = []
    for x in range(CX):
        rows = slice(y * Y_PITCH + x * C, y * Y_PITCH + (x + 1) * C)
        slope = jnp.concatenate([slope_ref[0, rows, :], slope_ref[1, rows, :]], axis=1)
        grads.append(slope * grad_ref[x, 8 + y : 9 + y, :])
    act = jnp.concatenate(grads, axis=0)
    high = act.astype(BF16)
    return high, (act - high.astype(F32)).astype(BF16)


def grad_kernel(
    position_ref,
    phase_ref,
    field_ref,
    coef_ref,
    source_ref,
    before_ref,
    after_ref,
    low_ref,
    high_ref,
    slope_ref,
    table_hbm,
    own_ref,
    other_ref,
    grad_ref,
    wide_field,
    wide_coef,
    wide_source,
    modes_ref,
    table_ref,
    sem,
):
    copy = pltpu.make_async_copy(table_hbm, table_ref, sem)
    copy.start()
    own = slice(8, 24)
    wide_field[...] = jnp.zeros_like(wide_field)
    wide_coef[...] = jnp.zeros_like(wide_coef)
    wide_source[...] = jnp.zeros_like(wide_source)
    wide_field[0:2, own, :] = before_ref[0:2]
    wide_field[2:6, own, :] = field_ref[...]
    wide_field[6:8, own, :] = after_ref[0:2]
    for x in range(8):
        wide_field[x, 6:8, :] = low_ref[2 * x : 2 * x + 2, :]
        wide_field[x, 24:26, :] = high_ref[2 * x : 2 * x + 2, :]
    for wide, cells, part, base in ((wide_coef, coef_ref, 2, 16), (wide_source, source_ref, 3, 22)):
        wide[0, own, :] = before_ref[part]
        wide[1:5, own, :] = cells[...].astype(F32)
        wide[5, own, :] = after_ref[part]
        for x in range(6):
            wide[x, 7:8, :] = low_ref[base + x : base + x + 1, :]
            wide[x, 24:25, :] = high_ref[base + x : base + x + 1, :]
    field = wide_field[...]
    center = field[1:7]
    residual = (16.0 / 3.0 - wide_coef[...]) * center - (2.0 / 3.0) * smooth(field) - wide_source[...]
    grad_ref[...] = (16.0 / 3.0 - wide_coef[1:5]) * residual[1:5] - (2.0 / 3.0) * smooth(residual)
    copy.wait()
    for y in range(CY):
        high, low = act_parts(slope_ref, grad_ref, y)
        both = nt_dot(table_ref[...], high)
        modes_ref[y] = both[:32] + both[32:] + nt_dot(table_ref[0:32, :], low)
    position = position_ref[0]
    forward = functools.partial(pencil_forward, modes_ref, phase_ref, position)
    by_core(position, forward, own_ref, other_ref)


def combine_kernel(own_in_ref, got_in_ref, own_ref, got_ref, out_ref):
    out_ref[:, 0:64, :] = own_in_ref[...] + got_in_ref[...]
    out_ref[:, 64:128, :] = own_ref[...] + got_ref[...]


def local_kernel(pointwise_ref, slope_ref, grad_ref, out_ref):
    for y in range(CY):
        act = jnp.concatenate(act_parts(slope_ref, grad_ref, y), axis=0)
        out_ref[y] = jnp.dot(pointwise_ref[...], act, preferred_element_type=F32)


def slab_forward_kernel(parts_ref, table_ref, out_ref):
    for block in range(4):
        for half in range(2):
            pieces = []
            for part in range(2):
                rows = pl.ds(block * 32 + part * KZ + 8 * half, 8)
                total = parts_ref[0, rows, :]
                for source in range(1, N // 2):
                    total = total + parts_ref[source, rows, :]
                pieces.append([total] + [pltpu.roll(total, 32 * d, 1) for d in range(1, 4)])
            for owner in range(N):
                result = None
                for d in range(4):
                    for part in range(2):
                        row = owner * 8 + d * 2 + part
                        term = pieces[part][d] * table_ref[row : row + 1, :]
                        result = term if result is None else result + term
                out_ref[owner, pl.ds(block * KZ + 8 * half, 8), :] = result


def flat_modes(block, group):
    lane_group = lax.broadcasted_iota(jnp.int32, (KZ, LANES), 1) // C
    row = lax.broadcasted_iota(jnp.int32, (KZ, LANES), 0)
    picked = jnp.where(lane_group == group, block, 0.0)
    picked = picked + pltpu.roll(picked, 64, 1)
    picked = picked + pltpu.roll(picked, 32, 1)
    tiles = [
        jnp.sum(jnp.where(row == 4 * tile + lane_group, picked, 0.0), axis=0, keepdims=True)
        for tile in range(4)
    ]
    return jnp.concatenate(tiles, axis=1)


def split_3(values):
    high = values.astype(BF16)
    rest = values - high.astype(F32)
    middle = rest.astype(BF16)
    low = (rest - middle.astype(F32)).astype(BF16)
    return high, middle, low


def back_kernel(parts_ref, weight_ref, modes_ref, out_ref):
    total = parts_ref[0]
    for source in range(1, N):
        total = total + parts_ref[source]
    modes_ref[...] = total
    rows = lax.broadcasted_iota(jnp.int32, (KZ, KZ * C), 0)
    lanes = lax.broadcasted_iota(jnp.int32, (KZ, KZ * C), 1)
    mask = jnp.where(lanes // C == rows, 1.0, 0.0).astype(BF16)
    kz = lax.broadcasted_iota(jnp.int32, (KZ, LANES), 0)
    scale = jnp.where(kz == 0, 1.0 / CELLS, 2.0 / CELLS)
    for ky in range(2):
        block = total[32 + ky * KZ : 32 + (ky + 1) * KZ]
        products = []
        for kx in range(2):
            real, imag = flat_modes(block, 2 * kx), flat_modes(block, 2 * kx + 1)
            w_real = weight_ref[0, kx, ky].astype(F32)
            w_imag = weight_ref[1, kx, ky].astype(F32)
            products.append(w_real * real + w_imag * imag)
            products.append(w_real * imag - w_imag * real)
        high, middle, low = split_3(jnp.concatenate(products, axis=0))
        back = scale * (nt_dot(mask, high) + nt_dot(mask, middle) + nt_dot(mask, low))
        for device in range(N):
            out_ref[device, ky * KZ : (ky + 1) * KZ, :] = back


def weight_grad_kernel(modes_ref, out_ref):
    rows = lax.broadcasted_iota(jnp.int32, (KZ, KZ * C), 0)
    lanes = lax.broadcasted_iota(jnp.int32, (KZ, KZ * C), 1)
    mask = jnp.where(lanes // C == rows, 1.0, 0.0).astype(BF16)
    first = lax.broadcasted_iota(jnp.int32, (1, KZ * C), 1) < C
    scale = jnp.where(first, 1.0 / CELLS, 2.0 / CELLS)
    for ky in range(2):
        inputs = modes_ref[ky * KZ : (ky + 1) * KZ, :]
        grads = modes_ref[32 + ky * KZ : 32 + (ky + 1) * KZ, :]
        high, middle, low = split_3(inputs)
        spread = tn_dot(high, mask) + tn_dot(middle, mask) + tn_dot(low, mask)
        for kx in range(2):
            real = scale * flat_modes(grads, 2 * kx)
            imag = scale * flat_modes(grads, 2 * kx + 1)
            in_real = spread[(2 * kx) * C : (2 * kx + 1) * C]
            in_imag = spread[(2 * kx + 1) * C : (2 * kx + 2) * C]
            out_ref[0, kx, ky] = (in_real * real + in_imag * imag).astype(BF16)
            out_ref[1, kx, ky] = (in_real * imag - in_imag * real).astype(BF16)


def slab_backward_kernel(parts_ref, table_ref, out_ref):
    for ky in range(2):
        for half in range(2):
            totals = [[None] * 4, [None] * 4]
            for source in range(N):
                values = parts_ref[source, pl.ds(ky * KZ + 8 * half, 8), :]
                for d in range(4):
                    for part in range(2):
                        row = source * 8 + d * 2 + part
                        term = values * table_ref[row : row + 1, :]
                        last = totals[part][d]
                        totals[part][d] = term if last is None else last + term
            for part in range(2):
                result = totals[part][0]
                for d in range(1, 4):
                    result = result + pltpu.roll(totals[part][d], 32 * d, 1)
                for device in range(N // 2):
                    out_ref[device, pl.ds(ky * 32 + part * KZ + 8 * half, 8), :] = result


def turn_modes(phase_ref, position, modes_ref, parts_refs):
    def turned(index, w_cos, w_sin, rows):
        ref = parts_refs[index // 2 % 2]
        row = (index % 2) * 32 + rows
        real = ref[index // 4, pl.ds(row, 8), :]
        imag = ref[index // 4, pl.ds(row + KZ, 8), :]
        return w_cos * real - w_sin * imag, w_cos * imag + w_sin * real

    for half in range(2):
        for k in range(17):
            w_cos = phase_ref[position * 34 + k]
            w_sin = phase_ref[position * 34 + 17 + k]
            if k == 0:
                even = turned(0, w_cos, w_sin, 8 * half)
                odd = None
            elif k == 16:
                even = turned(16, w_cos, -w_sin, 8 * half)
                odd = [-part for part in even]
            else:
                plus = turned(k, w_cos, w_sin, 8 * half)
                minus = turned(32 - k, w_cos, -w_sin, 8 * half)
                even = [p + m for p, m in zip(plus, minus)]
                odd = [p - m for p, m in zip(plus, minus)]
            for part in range(2):
                modes_ref[half, 0, k, part] = even[part]
                if odd is not None:
                    modes_ref[half, 1, k, part] = odd[part]


def output_kernel(
    position_ref,
    phase_ref,
    own_ref,
    other_ref,
    local_ref,
    table_ref,
    out_ref,
    modes_ref,
    rows_ref,
    flat_ref,
):
    position = position_ref[0]
    turn = functools.partial(turn_modes, phase_ref, position, modes_ref)
    by_core(position, turn, own_ref, other_ref)
    for half in range(2):
        for y in range(8):
            even = [modes_ref[half, 0, 0, 0], modes_ref[half, 0, 0, 1]]
            odd = [None, None]
            for k in range(1, 17):
                angle = 2.0 * math.pi * k * (y - 7.5) / NY
                cos, sin = math.cos(angle), math.sin(angle)
                for part in range(2):
                    even[part] = even[part] + cos * modes_ref[half, 0, k, part]
                    term = sin * modes_ref[half, 1, k, part]
                    odd[part] = term if odd[part] is None else odd[part] + term
            rows = pl.ds(8 * half, 8)
            more = pl.ds(KZ + 8 * half, 8)
            rows_ref[y, rows, :] = even[0] - odd[1]
            rows_ref[y, more, :] = even[1] + odd[0]
            rows_ref[15 - y, rows, :] = even[0] + odd[1]
            rows_ref[15 - y, more, :] = even[1] - odd[0]
    for y in range(CY):
        values = rows_ref[y]
        high = values.astype(BF16)
        low = (values - high.astype(F32)).astype(BF16)
        stacked = jnp.concatenate([high, low, high], axis=0)
        result = tn_dot(stacked, table_ref[...]) + local_ref[y]
        for x in range(CX):
            for side in range(2):
                piece = result[x * C : (x + 1) * C, side * 128 : (side + 1) * 128]
                flat_ref[side, pl.ds(x * CY + y, C, stride=PITCH), :] = piece
    for side in range(2):
        for c in range(C):
            piece = flat_ref[side, c * PITCH : c * PITCH + CX * CY].astype(BF16)
            out_ref[c, :, :, side * 128 : (side + 1) * 128] = piece.reshape(CX, CY, 128)


def call(kernel, name, out, scratch=(), scalars=(), hbm=()):
    def run(*args):
        args = [
            pltpu.with_memory_space_constraint(arg, pltpu.HBM) if i in hbm else arg
            for i, arg in enumerate(args)
        ]
        single = not isinstance(out, list)
        specs = [
            pl.BlockSpec(
                memory_space=pltpu.SMEM if i in scalars else pltpu.HBM if i in hbm else pltpu.VMEM
            )
            for i in range(len(args))
        ]
        shapes = [jax.ShapeDtypeStruct(*o) for o in ([out] if single else out)]
        result = pl.pallas_call(
            kernel,
            out_shape=shapes,
            in_specs=specs,
            out_specs=[pl.BlockSpec(memory_space=pltpu.VMEM)] * len(shapes),
            scratch_shapes=[pltpu.VMEM(*s) if isinstance(s, tuple) else s for s in scratch],
            compiler_params=pltpu.CompilerParams(vmem_limit_bytes=VMEM_LIMIT),
            name=name,
        )(*args)
        return result[0] if single else result

    return run


def shards(
    layer_input, pre_activation, coefficient, source, projection, pointwise, spectral_weight
):
    up = [(i, (i + 1) % N) for i in range(N)]
    down = [(j, i) for i, j in up]
    swap = [(i, i ^ 1) for i in range(N)]
    same_core = [[i for i in range(N) if i % 2 == core] for core in range(2)]
    slab = lax.axis_index("slab")
    pencil = lax.axis_index("pencil").reshape(1)
    phases = jnp.asarray(PENCIL_PHASES)
    depth_forward = jnp.asarray(DEPTH_FORWARD)
    depth_backward = jnp.asarray(DEPTH_BACKWARD)
    slab_forward = lax.dynamic_index_in_dim(jnp.asarray(SLAB_FORWARD), slab, 0, False)
    slab_backward = lax.dynamic_index_in_dim(jnp.asarray(SLAB_BACKWARD), slab, 0, False)
    pointwise_4 = jnp.kron(jnp.eye(CX, dtype=BF16), pointwise)
    pointwise_8 = jnp.concatenate([pointwise_4, pointwise_4], axis=1)

    edge = ((4, CY, NZ), F32)
    field, edge_up, edge_down, proj_tile = call(
        field_kernel,
        "field",
        [((CX, CY, NZ), F32), edge, edge, ((C, 128), F32)],
        scratch=[
            ((C, CX, CY, NZ), BF16),
            ((CX, CY, NZ), BF16),
            ((CX, CY, NZ), BF16),
            pltpu.SMEM((C,), F32),
            pltpu.SemaphoreType.DMA((CHUNKS + 3,)),
        ],
        hbm=(0, 1, 2, 3),
    )(pre_activation, coefficient, source, projection)
    before = lax.ppermute(edge_up, "slab", up)
    after = lax.ppermute(edge_down, "slab", down)
    slope = call(slope_kernel, "slope", ((2, CY * Y_PITCH, 128), F32))(pre_activation, proj_tile)
    half_modes = ((N // 2, 64, LANES), F32)
    own_in, other_in = call(
        input_kernel,
        "input_modes",
        [half_modes, half_modes],
        scratch=[
            ((2, C * PITCH, 128), F32),
            ((CY, 32, LANES), F32),
            (DEPTH_FORWARD.shape, BF16),
            pltpu.SemaphoreType.DMA(()),
        ],
        scalars=(0, 1),
        hbm=(3,),
    )(pencil, phases, layer_input, depth_forward)
    before, after, slope, own_in, other_in = lax.optimization_barrier(
        (before, after, slope, own_in, other_in)
    )
    got_in = lax.ppermute(other_in, "pencil", swap)
    side_up, side_down = call(pack_kernel, "pack", [((32, NZ), F32), ((32, NZ), F32)])(
        field, coefficient, source, before, after
    )
    low = lax.ppermute(side_up, "pencil", up)
    high = lax.ppermute(side_down, "pencil", down)
    own, other, grad = call(
        grad_kernel,
        "grad_modes",
        [half_modes, half_modes, ((CX, 32, NZ), F32)],
        scratch=[
            ((8, 32, NZ), F32),
            ((6, 32, NZ), F32),
            ((6, 32, NZ), F32),
            ((CY, 32, LANES), F32),
            (DEPTH_FORWARD.shape, BF16),
            pltpu.SemaphoreType.DMA(()),
        ],
        scalars=(0, 1),
        hbm=(10,),
    )(
        pencil,
        phases,
        field,
        coefficient,
        source,
        before,
        after,
        low,
        high,
        slope,
        depth_forward,
    )
    got = lax.ppermute(other, "pencil", swap)
    to_pencil = call(combine_kernel, "combine", ((N // 2, 128, LANES), F32))(
        own_in, got_in, own, got
    )
    from_pencil = lax.all_to_all(
        to_pencil, "pencil", 0, 0, axis_index_groups=same_core, tiled=True
    )
    local = call(local_kernel, "local", ((CY, LANES, NZ), F32))(pointwise_8, slope, grad)
    from_pencil, local = lax.optimization_barrier((from_pencil, local))
    to_slab = call(slab_forward_kernel, "slab_forward", ((N, 64, LANES), F32))(
        from_pencil, slab_forward
    )
    from_slab = lax.all_to_all(to_slab, "slab", 0, 0, tiled=True)
    modes, to_slab = call(back_kernel, "back", [((64, LANES), F32), ((N, 32, LANES), F32)])(
        from_slab, spectral_weight
    )
    from_slab = lax.all_to_all(to_slab, "slab", 0, 0, tiled=True)
    weight_grad = call(weight_grad_kernel, "weight_grad", (spectral_weight.shape, BF16))(modes)
    to_pencil = call(slab_backward_kernel, "slab_backward", half_modes)(from_slab, slab_backward)
    own = lax.all_to_all(to_pencil, "pencil", 0, 0, axis_index_groups=same_core, tiled=True)
    other = lax.ppermute(own, "pencil", swap)
    input_grad = call(
        output_kernel,
        "output",
        ((C, CX, CY, NZ), BF16),
        scratch=[
            ((2, 2, 17, 2, 8, LANES), F32),
            ((CY, 32, LANES), F32),
            ((2, C * PITCH, 128), F32),
        ],
        scalars=(0, 1),
    )(pencil, phases, own, other, local, depth_backward)
    return (input_grad, weight_grad)


def solution(mesh):
    return jax.shard_map(
        shards,
        mesh=mesh,
        in_specs=(
            P(None, "slab", "pencil", None),
            P(None, "slab", "pencil", None),
            P("slab", "pencil", None),
            P("slab", "pencil", None),
            P(),
            P(),
            P(None, "slab", "pencil", None, None),
        ),
        out_specs=(P(None, "slab", "pencil", None), P(None, "slab", "pencil", None, None)),
        check_vma=False,
    )
```

```python
import functools
import math

import jax
import jax.numpy as jnp
import ml_dtypes
import numpy as np
from jax import lax
from jax.experimental import pallas as pl
from jax.experimental.pallas import tpu as pltpu
from jax.sharding import PartitionSpec as P

F32 = jnp.float32
BF16 = jnp.bfloat16
C, CX, CY, NZ = 32, 4, 16, 256
NX, NY = 64, 256
N = 16
KZ = 16
LANES = CX * C
CELLS = float(NX * NY * NZ)
VMEM_LIMIT = 24 * 1024 * 1024
PITCH = 68
Y_PITCH = LANES + 8
CHUNKS = 4
BYTES_PER_US = 3_690_000


def split_2(table):
    high = table.astype(ml_dtypes.bfloat16)
    low = (table - high.astype(np.float64)).astype(ml_dtypes.bfloat16)
    return high, low


def depth_tables():
    angles = 2.0 * math.pi * ((np.arange(KZ)[:, None] * np.arange(NZ)[None, :]) % NZ) / NZ
    table = np.concatenate([np.cos(angles), -np.sin(angles)], axis=0)
    high, low = split_2(table)
    return np.concatenate([high, low], axis=0), np.concatenate([high, high, low], axis=0)


def wave(index):
    return index if index < 16 else index - 32


def pencil_phases():
    position = 16.0 * np.arange(N)[:, None] + 7.5
    angles = 2.0 * math.pi * np.arange(17)[None, :] * position / NY
    return np.concatenate([np.cos(angles), np.sin(angles)], axis=1).astype(np.float32).reshape(-1)


def slab_tables():
    forward = np.zeros((N, N, 4, 2, LANES))
    backward = np.zeros((N, N, 4, 2, LANES))
    for position in range(N):
        for other in range(N):
            for shift in range(4):
                for group in range(4):
                    k = wave(2 * other + group // 2)
                    lanes = slice(group * C, (group + 1) * C)
                    x = 4 * position + (group - shift) % 4
                    angle = 2.0 * math.pi * ((k * x) % NX) / NX
                    cos, sin = math.cos(angle), math.sin(angle)
                    forward[position, other, shift, 0, lanes] = cos if group % 2 == 0 else -sin
                    forward[position, other, shift, 1, lanes] = sin if group % 2 == 0 else cos
                    x = 4 * position + (group + shift) % 4
                    angle = 2.0 * math.pi * ((k * x) % NX) / NX
                    cos, sin = math.cos(angle), math.sin(angle)
                    backward[position, other, shift, 0, lanes] = cos if group % 2 == 0 else -sin
                    backward[position, other, shift, 1, lanes] = sin if group % 2 == 0 else cos
    shape = (N, N * 8, LANES)
    return forward.astype(np.float32).reshape(shape), backward.astype(np.float32).reshape(shape)


DEPTH_FORWARD, DEPTH_BACKWARD = depth_tables()
PENCIL_PHASES = pencil_phases()
SLAB_FORWARD, SLAB_BACKWARD = slab_tables()


def normal_tail(values):
    size = jnp.abs(values)
    bell = jnp.exp(-0.5 * values * values)
    denominator = 1.0 + (0.3275911 / math.sqrt(2.0)) * size
    t = pl.reciprocal(denominator, approx=True)
    t = t * (2.0 - denominator * t)
    poly = 0.5 * 1.061405429 * t - 0.5 * 1.453152027
    poly = poly * t + 0.5 * 1.421413741
    poly = poly * t - 0.5 * 0.284496736
    poly = poly * t + 0.5 * 0.254829592
    return bell, poly * t * bell


def field_kernel(
    pre_hbm,
    coef_hbm,
    source_hbm,
    proj_hbm,
    input_hbm,
    field_ref,
    up_ref,
    down_ref,
    pre_ref,
    coef_ref,
    source_ref,
    input_ref,
    proj_tile_ref,
    proj_ref,
    sems,
):
    size = C // CHUNKS
    copies = [pltpu.make_async_copy(proj_hbm, proj_ref, sems.at[CHUNKS])]
    for i in range(CHUNKS):
        part = pl.ds(i * size, size)
        copies.append(pltpu.make_async_copy(pre_hbm.at[part], pre_ref.at[part], sems.at[i]))
    copies.append(pltpu.make_async_copy(coef_hbm, coef_ref, sems.at[CHUNKS + 1]))
    copies.append(pltpu.make_async_copy(source_hbm, source_ref, sems.at[CHUNKS + 2]))
    copies.append(pltpu.make_async_copy(input_hbm, input_ref, sems.at[CHUNKS + 3]))
    for copy in copies:
        copy.start()
    copies[0].wait()
    for c in range(C):
        proj_tile_ref[c : c + 1, :] = jnp.full((1, 128), proj_ref[c], F32)

    def add_channel(c, total):
        values = pre_ref[c].astype(F32)
        _, tail = normal_tail(values)
        return total + proj_ref[c] * (jnp.maximum(values, 0.0) - jnp.abs(values) * tail)

    total = jnp.zeros((CX, CY, NZ), F32)
    for i in range(CHUNKS):
        copies[1 + i].wait()
        total = lax.fori_loop(i * size, (i + 1) * size, add_channel, total, unroll=2)
    for copy in copies[1 + CHUNKS :]:
        copy.wait()
    field_ref[...] = total
    up_ref[0:2] = total[2:4]
    down_ref[0:2] = total[0:2]
    up_ref[2] = coef_ref[3].astype(F32)
    up_ref[3] = source_ref[3].astype(F32)
    down_ref[2] = coef_ref[0].astype(F32)
    down_ref[3] = source_ref[0].astype(F32)


def slope_kernel(pre_ref, proj_ref, slope_ref):
    def one_channel(c, carry):
        values = pre_ref[c].astype(F32)
        bell, tail = normal_tail(values)
        below = jnp.where(values >= 0.0, 1.0 - tail, tail)
        slope = below + values * (bell * (1.0 / math.sqrt(2.0 * math.pi)))
        weight = proj_ref[pl.ds(c, 1), :]
        for x in range(CX):
            for side in range(2):
                piece = slope[x, :, side * 128 : (side + 1) * 128] * weight
                slope_ref[side, pl.ds(x * C + c, CY, stride=Y_PITCH), :] = piece
        return carry

    lax.fori_loop(0, C, one_channel, 0, unroll=2)


def nt_dot(left, right):
    return lax.dot_general(left, right, (((1,), (1,)), ((), ())), preferred_element_type=F32)


def tn_dot(left, right):
    return lax.dot_general(left, right, (((0,), (0,)), ((), ())), preferred_element_type=F32)


def pencil_forward(modes_ref, phase_ref, position, out_refs):
    for half in range(2):
        sums, diffs = [], []
        for part in range(2):
            rows = pl.ds(part * KZ + 8 * half, 8)
            first = [modes_ref[j, rows, :] for j in range(8)]
            second = [modes_ref[15 - j, rows, :] for j in range(8)]
            sums.append([a + b for a, b in zip(first, second)])
            diffs.append([a - b for a, b in zip(first, second)])
        for k in range(17):
            cosines = [math.cos(2.0 * math.pi * k * (7.5 - j) / NY) for j in range(8)]
            sines = [math.sin(2.0 * math.pi * k * (7.5 - j) / NY) for j in range(8)]
            even = [sum(w * v for w, v in zip(cosines, part)) for part in sums]
            w_cos = phase_ref[position * 34 + k]
            w_sin = phase_ref[position * 34 + 17 + k]
            if k == 0:
                results = [(0, even[0], even[1], w_sin)]
            else:
                odd = [sum(w * v for w, v in zip(sines, part)) for part in diffs]
                results = [(32 - k, even[0] + odd[1], even[1] - odd[0], -w_sin)]
                if k < 16:
                    results.append((k, even[0] - odd[1], even[1] + odd[0], w_sin))
            for index, real, imag, sin in results:
                row = (index % 2) * 32 + 8 * half
                out_ref = out_refs[index // 2 % 2]
                out_ref[index // 4, pl.ds(row, 8), :] = w_cos * real + sin * imag
                out_ref[index // 4, pl.ds(row + KZ, 8), :] = w_cos * imag - sin * real


def by_core(position, function, own_ref, other_ref):
    @pl.when(position % 2 == 0)
    def _():
        function((own_ref, other_ref))

    @pl.when(position % 2 == 1)
    def _():
        function((other_ref, own_ref))


def input_kernel(
    phase_ref,
    input_ref,
    table_hbm,
    own_ref,
    other_ref,
    rows_ref,
    modes_ref,
    table_ref,
    sem,
):
    copy = pltpu.make_async_copy(table_hbm, table_ref, sem)
    copy.start()
    for side in range(2):
        for c in range(C):
            piece = input_ref[c, :, :, side * 128 : (side + 1) * 128].astype(F32)
            rows_ref[side, c * PITCH : c * PITCH + CX * CY, :] = piece.reshape(CX * CY, 128)
    copy.wait()
    for y in range(CY):
        sides = [
            jnp.concatenate(
                [rows_ref[side, pl.ds(x * CY + y, C, stride=PITCH), :] for x in range(CX)], axis=0
            )
            for side in range(2)
        ]
        values = jnp.concatenate(sides, axis=1).astype(BF16)
        both = nt_dot(table_ref[...], values)
        modes_ref[y] = both[:32] + both[32:]
    position = lax.axis_index("pencil")
    forward = functools.partial(pencil_forward, modes_ref, phase_ref, position)
    by_core(position, forward, own_ref, other_ref)


def pack_kernel(field_ref, coef_ref, source_ref, before_ref, after_ref, up_ref, down_ref):
    for out_ref, cells, cell in ((up_ref, slice(14, 16), slice(15, 16)), (down_ref, slice(0, 2), slice(0, 1))):
        for x in range(8):
            if x < 2:
                rows = before_ref[x, cells, :]
            elif x < 6:
                rows = field_ref[x - 2, cells, :]
            else:
                rows = after_ref[x - 6, cells, :]
            out_ref[2 * x : 2 * x + 2, :] = rows
        for base, part, own_ref in ((16, 2, coef_ref), (22, 3, source_ref)):
            for x in range(6):
                if x == 0:
                    row = before_ref[part, cell, :]
                elif x == 5:
                    row = after_ref[part, cell, :]
                else:
                    row = own_ref[x - 1].astype(F32)[cell, :]
                out_ref[base + x : base + x + 1, :] = row
        out_ref[28:32, :] = jnp.zeros((4, NZ), F32)


def smooth(values):
    values = values + 0.5 * (pltpu.roll(values, 1, 2) + pltpu.roll(values, NZ - 1, 2))
    values = values + 0.5 * (pltpu.roll(values, 1, 1) + pltpu.roll(values, 31, 1))
    return 0.5 * (values[:-2] + values[2:]) + values[1:-1]


def act_parts(slope_ref, grad_ref, y):
    grads = []
    for x in range(CX):
        rows = slice(y * Y_PITCH + x * C, y * Y_PITCH + (x + 1) * C)
        slope = jnp.concatenate([slope_ref[0, rows, :], slope_ref[1, rows, :]], axis=1)
        grads.append(slope * grad_ref[x, 8 + y : 9 + y, :])
    act = jnp.concatenate(grads, axis=0)
    high = act.astype(BF16)
    return high, (act - high.astype(F32)).astype(BF16)


def grad_kernel(
    phase_ref,
    field_ref,
    coef_ref,
    source_ref,
    before_ref,
    after_ref,
    low_ref,
    high_ref,
    slope_ref,
    table_hbm,
    own_ref,
    other_ref,
    grad_ref,
    wide_field,
    wide_coef,
    wide_source,
    modes_ref,
    table_ref,
    sem,
):
    copy = pltpu.make_async_copy(table_hbm, table_ref, sem)
    copy.start()
    own = slice(8, 24)
    wide_field[...] = jnp.zeros_like(wide_field)
    wide_coef[...] = jnp.zeros_like(wide_coef)
    wide_source[...] = jnp.zeros_like(wide_source)
    wide_field[0:2, own, :] = before_ref[0:2]
    wide_field[2:6, own, :] = field_ref[...]
    wide_field[6:8, own, :] = after_ref[0:2]
    for x in range(8):
        wide_field[x, 6:8, :] = low_ref[2 * x : 2 * x + 2, :]
        wide_field[x, 24:26, :] = high_ref[2 * x : 2 * x + 2, :]
    for wide, cells, part, base in ((wide_coef, coef_ref, 2, 16), (wide_source, source_ref, 3, 22)):
        wide[0, own, :] = before_ref[part]
        wide[1:5, own, :] = cells[...].astype(F32)
        wide[5, own, :] = after_ref[part]
        for x in range(6):
            wide[x, 7:8, :] = low_ref[base + x : base + x + 1, :]
            wide[x, 24:25, :] = high_ref[base + x : base + x + 1, :]
    field = wide_field[...]
    center = field[1:7]
    residual = (16.0 / 3.0 - wide_coef[...]) * center - (2.0 / 3.0) * smooth(field) - wide_source[...]
    grad_ref[...] = (16.0 / 3.0 - wide_coef[1:5]) * residual[1:5] - (2.0 / 3.0) * smooth(residual)
    copy.wait()
    for y in range(CY):
        high, low = act_parts(slope_ref, grad_ref, y)
        both = nt_dot(table_ref[...], high)
        modes_ref[y] = both[:32] + both[32:] + nt_dot(table_ref[0:32, :], low)
    position = lax.axis_index("pencil")
    forward = functools.partial(pencil_forward, modes_ref, phase_ref, position)
    by_core(position, forward, own_ref, other_ref)


def combine_kernel(own_in_ref, got_in_ref, own_ref, got_ref, out_ref):
    out_ref[:, 0:64, :] = own_in_ref[...] + got_in_ref[...]
    out_ref[:, 64:128, :] = own_ref[...] + got_ref[...]


def local_kernel(
    pointwise_ref,
    slope_ref,
    grad_ref,
    forward_hbm,
    backward_hbm,
    out_ref,
    forward_ref,
    backward_ref,
    sems,
):
    slab = lax.axis_index("slab")
    copies = [
        pltpu.make_async_copy(forward_hbm.at[slab], forward_ref, sems.at[0]),
        pltpu.make_async_copy(backward_hbm.at[slab], backward_ref, sems.at[1]),
    ]
    for copy in copies:
        copy.start()
    rows = lax.broadcasted_iota(jnp.int32, (C, LANES), 0)
    lanes = lax.broadcasted_iota(jnp.int32, (C, LANES), 1)
    repeat = jnp.where(lanes % C == rows, 1.0, 0.0).astype(BF16)
    wide = jnp.dot(pointwise_ref[...], repeat, preferred_element_type=F32)
    wide = jnp.concatenate([wide] * CX, axis=0)
    rows = lax.broadcasted_iota(jnp.int32, (LANES, LANES), 0)
    lanes = lax.broadcasted_iota(jnp.int32, (LANES, LANES), 1)
    wide = jnp.where(rows // C == lanes // C, wide, 0.0).astype(BF16)
    wide = jnp.concatenate([wide, wide], axis=1)
    for y in range(CY):
        act = jnp.concatenate(act_parts(slope_ref, grad_ref, y), axis=0)
        out_ref[y] = jnp.dot(wide, act, preferred_element_type=F32)
    for copy in copies:
        copy.wait()


def slab_forward_kernel(parts_ref, table_ref, out_ref):
    for block in range(4):
        for half in range(2):
            pieces = []
            for part in range(2):
                rows = pl.ds(block * 32 + part * KZ + 8 * half, 8)
                total = parts_ref[0, rows, :]
                for source in range(1, N // 2):
                    total = total + parts_ref[source, rows, :]
                pieces.append([total] + [pltpu.roll(total, 32 * d, 1) for d in range(1, 4)])
            for owner in range(N):
                result = None
                for d in range(4):
                    for part in range(2):
                        row = owner * 8 + d * 2 + part
                        term = pieces[part][d] * table_ref[row : row + 1, :]
                        result = term if result is None else result + term
                out_ref[owner, pl.ds(block * KZ + 8 * half, 8), :] = result


def flat_modes(block, group):
    lane_group = lax.broadcasted_iota(jnp.int32, (KZ, LANES), 1) // C
    row = lax.broadcasted_iota(jnp.int32, (KZ, LANES), 0)
    picked = jnp.where(lane_group == group, block, 0.0)
    picked = picked + pltpu.roll(picked, 64, 1)
    picked = picked + pltpu.roll(picked, 32, 1)
    tiles = [
        jnp.sum(jnp.where(row == 4 * tile + lane_group, picked, 0.0), axis=0, keepdims=True)
        for tile in range(4)
    ]
    return jnp.concatenate(tiles, axis=1)


def split_3(values):
    high = values.astype(BF16)
    rest = values - high.astype(F32)
    middle = rest.astype(BF16)
    low = (rest - middle.astype(F32)).astype(BF16)
    return high, middle, low


def back_kernel(parts_ref, weight_ref, modes_ref, out_ref):
    total = parts_ref[0]
    for source in range(1, N):
        total = total + parts_ref[source]
    modes_ref[...] = total
    rows = lax.broadcasted_iota(jnp.int32, (KZ, KZ * C), 0)
    lanes = lax.broadcasted_iota(jnp.int32, (KZ, KZ * C), 1)
    mask = jnp.where(lanes // C == rows, 1.0, 0.0).astype(BF16)
    kz = lax.broadcasted_iota(jnp.int32, (KZ, LANES), 0)
    scale = jnp.where(kz == 0, 1.0 / CELLS, 2.0 / CELLS)
    for ky in range(2):
        block = total[32 + ky * KZ : 32 + (ky + 1) * KZ]
        products = []
        for kx in range(2):
            real, imag = flat_modes(block, 2 * kx), flat_modes(block, 2 * kx + 1)
            w_real = weight_ref[0, kx, ky].astype(F32)
            w_imag = weight_ref[1, kx, ky].astype(F32)
            products.append(w_real * real + w_imag * imag)
            products.append(w_real * imag - w_imag * real)
        high, middle, low = split_3(jnp.concatenate(products, axis=0))
        back = scale * (nt_dot(mask, high) + nt_dot(mask, middle) + nt_dot(mask, low))
        for device in range(N):
            out_ref[device, ky * KZ : (ky + 1) * KZ, :] = back


def weight_grad_kernel(modes_ref, out_ref):
    rows = lax.broadcasted_iota(jnp.int32, (KZ, KZ * C), 0)
    lanes = lax.broadcasted_iota(jnp.int32, (KZ, KZ * C), 1)
    mask = jnp.where(lanes // C == rows, 1.0, 0.0).astype(BF16)
    first = lax.broadcasted_iota(jnp.int32, (1, KZ * C), 1) < C
    scale = jnp.where(first, 1.0 / CELLS, 2.0 / CELLS)
    for ky in range(2):
        inputs = modes_ref[ky * KZ : (ky + 1) * KZ, :]
        grads = modes_ref[32 + ky * KZ : 32 + (ky + 1) * KZ, :]
        high, middle, low = split_3(inputs)
        spread = tn_dot(high, mask) + tn_dot(middle, mask) + tn_dot(low, mask)
        for kx in range(2):
            real = scale * flat_modes(grads, 2 * kx)
            imag = scale * flat_modes(grads, 2 * kx + 1)
            in_real = spread[(2 * kx) * C : (2 * kx + 1) * C]
            in_imag = spread[(2 * kx + 1) * C : (2 * kx + 2) * C]
            out_ref[0, kx, ky] = (in_real * real + in_imag * imag).astype(BF16)
            out_ref[1, kx, ky] = (in_real * imag - in_imag * real).astype(BF16)


def slab_backward_kernel(parts_ref, table_ref, out_ref):
    for ky in range(2):
        for half in range(2):
            totals = [[None] * 4, [None] * 4]
            for source in range(N):
                values = parts_ref[source, pl.ds(ky * KZ + 8 * half, 8), :]
                for d in range(4):
                    for part in range(2):
                        row = source * 8 + d * 2 + part
                        term = values * table_ref[row : row + 1, :]
                        last = totals[part][d]
                        totals[part][d] = term if last is None else last + term
            for part in range(2):
                result = totals[part][0]
                for d in range(1, 4):
                    result = result + pltpu.roll(totals[part][d], 32 * d, 1)
                for device in range(N // 2):
                    out_ref[device, pl.ds(ky * 32 + part * KZ + 8 * half, 8), :] = result


def turn_modes(phase_ref, position, modes_ref, parts_refs):
    def turned(index, w_cos, w_sin, rows):
        ref = parts_refs[index // 2 % 2]
        row = (index % 2) * 32 + rows
        real = ref[index // 4, pl.ds(row, 8), :]
        imag = ref[index // 4, pl.ds(row + KZ, 8), :]
        return w_cos * real - w_sin * imag, w_cos * imag + w_sin * real

    for half in range(2):
        for k in range(17):
            w_cos = phase_ref[position * 34 + k]
            w_sin = phase_ref[position * 34 + 17 + k]
            if k == 0:
                even = turned(0, w_cos, w_sin, 8 * half)
                odd = None
            elif k == 16:
                even = turned(16, w_cos, -w_sin, 8 * half)
                odd = [-part for part in even]
            else:
                plus = turned(k, w_cos, w_sin, 8 * half)
                minus = turned(32 - k, w_cos, -w_sin, 8 * half)
                even = [p + m for p, m in zip(plus, minus)]
                odd = [p - m for p, m in zip(plus, minus)]
            for part in range(2):
                modes_ref[half, 0, k, part] = even[part]
                if odd is not None:
                    modes_ref[half, 1, k, part] = odd[part]


def output_kernel(
    phase_ref,
    own_ref,
    other_ref,
    local_ref,
    table_hbm,
    out_ref,
    modes_ref,
    rows_ref,
    flat_ref,
    table_ref,
    sem,
):
    copy = pltpu.make_async_copy(table_hbm, table_ref, sem)
    copy.start()
    position = lax.axis_index("pencil")
    turn = functools.partial(turn_modes, phase_ref, position, modes_ref)
    by_core(position, turn, own_ref, other_ref)
    for half in range(2):
        for y in range(8):
            even = [modes_ref[half, 0, 0, 0], modes_ref[half, 0, 0, 1]]
            odd = [None, None]
            for k in range(1, 17):
                angle = 2.0 * math.pi * k * (y - 7.5) / NY
                cos, sin = math.cos(angle), math.sin(angle)
                for part in range(2):
                    even[part] = even[part] + cos * modes_ref[half, 0, k, part]
                    term = sin * modes_ref[half, 1, k, part]
                    odd[part] = term if odd[part] is None else odd[part] + term
            rows = pl.ds(8 * half, 8)
            more = pl.ds(KZ + 8 * half, 8)
            rows_ref[y, rows, :] = even[0] - odd[1]
            rows_ref[y, more, :] = even[1] + odd[0]
            rows_ref[15 - y, rows, :] = even[0] + odd[1]
            rows_ref[15 - y, more, :] = even[1] - odd[0]
    copy.wait()
    for y in range(CY):
        values = rows_ref[y]
        high = values.astype(BF16)
        low = (values - high.astype(F32)).astype(BF16)
        stacked = jnp.concatenate([high, low, high], axis=0)
        result = tn_dot(stacked, table_ref[...]) + local_ref[y]
        for x in range(CX):
            for side in range(2):
                piece = result[x * C : (x + 1) * C, side * 128 : (side + 1) * 128]
                flat_ref[side, pl.ds(x * CY + y, C, stride=PITCH), :] = piece
    for side in range(2):
        for c in range(C):
            piece = flat_ref[side, c * PITCH : c * PITCH + CX * CY].astype(BF16)
            out_ref[c, :, :, side * 128 : (side + 1) * 128] = piece.reshape(CX, CY, 128)


def call(kernel, name, out, scratch=(), scalars=(), hbm=(), us=1):
    def run(*args):
        args = [
            pltpu.with_memory_space_constraint(arg, pltpu.HBM) if i in hbm else arg
            for i, arg in enumerate(args)
        ]
        single = not isinstance(out, list)
        specs = [
            pl.BlockSpec(
                memory_space=pltpu.SMEM if i in scalars else pltpu.HBM if i in hbm else pltpu.VMEM
            )
            for i in range(len(args))
        ]
        shapes = [jax.ShapeDtypeStruct(*o) for o in ([out] if single else out)]
        result = pl.pallas_call(
            kernel,
            out_shape=shapes,
            in_specs=specs,
            out_specs=[pl.BlockSpec(memory_space=pltpu.VMEM)] * len(shapes),
            scratch_shapes=[pltpu.VMEM(*s) if isinstance(s, tuple) else s for s in scratch],
            compiler_params=pltpu.CompilerParams(vmem_limit_bytes=VMEM_LIMIT),
            cost_estimate=pl.CostEstimate(
                flops=0, transcendentals=0, bytes_accessed=int(us * BYTES_PER_US)
            ),
            name=name,
        )(*args)
        return result[0] if single else result

    return run


def shards(
    layer_input, pre_activation, coefficient, source, projection, pointwise, spectral_weight
):
    up = [(i, (i + 1) % N) for i in range(N)]
    down = [(j, i) for i, j in up]
    swap = [(i, i ^ 1) for i in range(N)]
    same_core = [[i for i in range(N) if i % 2 == core] for core in range(2)]
    phases = jnp.asarray(PENCIL_PHASES)
    depth_forward = jnp.asarray(DEPTH_FORWARD)
    depth_backward = jnp.asarray(DEPTH_BACKWARD)
    edge = ((4, CY, NZ), F32)
    field, edge_up, edge_down, pre_activation, coefficient, source, layer_input, proj_tile = call(
        field_kernel,
        "field",
        [
            ((CX, CY, NZ), F32),
            edge,
            edge,
            ((C, CX, CY, NZ), BF16),
            ((CX, CY, NZ), BF16),
            ((CX, CY, NZ), BF16),
            ((C, CX, CY, NZ), BF16),
            ((C, 128), F32),
        ],
        scratch=[pltpu.SMEM((C,), F32), pltpu.SemaphoreType.DMA((CHUNKS + 4,))],
        hbm=(0, 1, 2, 3, 4),
        us=4,
    )(pre_activation, coefficient, source, projection, layer_input)
    before = lax.ppermute(edge_up, "slab", up)
    after = lax.ppermute(edge_down, "slab", down)
    slope = call(slope_kernel, "slope", ((2, CY * Y_PITCH, 128), F32), us=2)(pre_activation, proj_tile)
    half_modes = ((N // 2, 64, LANES), F32)
    own_in, other_in = call(
        input_kernel,
        "input_modes",
        [half_modes, half_modes],
        scratch=[
            ((2, C * PITCH, 128), F32),
            ((CY, 32, LANES), F32),
            (DEPTH_FORWARD.shape, BF16),
            pltpu.SemaphoreType.DMA(()),
        ],
        scalars=(0,),
        hbm=(2,),
        us=2,
    )(phases, layer_input, depth_forward)
    before, after, slope, own_in, other_in = lax.optimization_barrier(
        (before, after, slope, own_in, other_in)
    )
    got_in = lax.ppermute(other_in, "pencil", swap)
    side_up, side_down = call(pack_kernel, "pack", [((32, NZ), F32), ((32, NZ), F32)])(
        field, coefficient, source, before, after
    )
    low = lax.ppermute(side_up, "pencil", up)
    high = lax.ppermute(side_down, "pencil", down)
    own, other, grad = call(
        grad_kernel,
        "grad_modes",
        [half_modes, half_modes, ((CX, 32, NZ), F32)],
        scratch=[
            ((8, 32, NZ), F32),
            ((6, 32, NZ), F32),
            ((6, 32, NZ), F32),
            ((CY, 32, LANES), F32),
            (DEPTH_FORWARD.shape, BF16),
            pltpu.SemaphoreType.DMA(()),
        ],
        scalars=(0,),
        hbm=(9,),
        us=3,
    )(
        phases,
        field,
        coefficient,
        source,
        before,
        after,
        low,
        high,
        slope,
        depth_forward,
    )
    got = lax.ppermute(other, "pencil", swap)
    table = (SLAB_FORWARD.shape[1:], F32)
    local, slab_forward, slab_backward = call(
        local_kernel,
        "local",
        [((CY, LANES, NZ), F32), table, table],
        scratch=[pltpu.SemaphoreType.DMA((2,))],
        hbm=(3, 4),
    )(pointwise, slope, grad, jnp.asarray(SLAB_FORWARD), jnp.asarray(SLAB_BACKWARD))
    got, local, slab_forward, slab_backward = lax.optimization_barrier(
        (got, local, slab_forward, slab_backward)
    )
    to_pencil = call(combine_kernel, "combine", ((N // 2, 128, LANES), F32))(
        own_in, got_in, own, got
    )
    from_pencil = lax.all_to_all(
        to_pencil, "pencil", 0, 0, axis_index_groups=same_core, tiled=True
    )
    to_slab = call(slab_forward_kernel, "slab_forward", ((N, 64, LANES), F32))(
        from_pencil, slab_forward
    )
    from_slab = lax.all_to_all(to_slab, "slab", 0, 0, tiled=True)
    modes, to_slab = call(back_kernel, "back", [((64, LANES), F32), ((N, 32, LANES), F32)])(
        from_slab, spectral_weight
    )
    from_slab = lax.all_to_all(to_slab, "slab", 0, 0, tiled=True)
    weight_grad = call(weight_grad_kernel, "weight_grad", (spectral_weight.shape, BF16))(modes)
    to_pencil = call(slab_backward_kernel, "slab_backward", half_modes)(from_slab, slab_backward)
    own = lax.all_to_all(to_pencil, "pencil", 0, 0, axis_index_groups=same_core, tiled=True)
    other = lax.ppermute(own, "pencil", swap)
    input_grad = call(
        output_kernel,
        "output",
        ((C, CX, CY, NZ), BF16),
        scratch=[
            ((2, 2, 17, 2, 8, LANES), F32),
            ((CY, 32, LANES), F32),
            ((2, C * PITCH, 128), F32),
            (DEPTH_BACKWARD.shape, BF16),
            pltpu.SemaphoreType.DMA(()),
        ],
        scalars=(0,),
        hbm=(4,),
    )(phases, own, other, local, depth_backward)
    return (input_grad, weight_grad)


def solution(mesh):
    return jax.shard_map(
        shards,
        mesh=mesh,
        in_specs=(
            P(None, "slab", "pencil", None),
            P(None, "slab", "pencil", None),
            P("slab", "pencil", None),
            P("slab", "pencil", None),
            P(),
            P(),
            P(None, "slab", "pencil", None, None),
        ),
        out_specs=(P(None, "slab", "pencil", None), P(None, "slab", "pencil", None, None)),
        check_vma=False,
    )
```

```python
import functools
import math

import jax
import jax.numpy as jnp
import ml_dtypes
import numpy as np
from jax import lax
from jax.experimental import pallas as pl
from jax.experimental.pallas import tpu as pltpu
from jax.sharding import PartitionSpec as P

F32 = jnp.float32
BF16 = jnp.bfloat16
C, CX, CY, NZ = 32, 4, 16, 256
NX, NY = 64, 256
N = 16
KZ = 16
LANES = CX * C
CELLS = float(NX * NY * NZ)
VMEM_LIMIT = 24 * 1024 * 1024
PITCH = 68
Y_PITCH = LANES + 8
CHUNKS = 4
BYTES_PER_US = 3_690_000


def split_2(table):
    high = table.astype(ml_dtypes.bfloat16)
    low = (table - high.astype(np.float64)).astype(ml_dtypes.bfloat16)
    return high, low


def depth_tables():
    angles = 2.0 * math.pi * ((np.arange(KZ)[:, None] * np.arange(NZ)[None, :]) % NZ) / NZ
    table = np.concatenate([np.cos(angles), -np.sin(angles)], axis=0)
    high, low = split_2(table)
    return np.concatenate([high, low], axis=0), np.concatenate([high, high, low], axis=0)


def wave(index):
    return index if index < 16 else index - 32


def pencil_phases():
    position = 16.0 * np.arange(N)[:, None] + 7.5
    angles = 2.0 * math.pi * np.arange(17)[None, :] * position / NY
    return np.concatenate([np.cos(angles), np.sin(angles)], axis=1).astype(np.float32).reshape(-1)


def slab_tables():
    forward = np.zeros((N, N, 4, 2, LANES))
    backward = np.zeros((N, N, 4, 2, LANES))
    for position in range(N):
        for other in range(N):
            for shift in range(4):
                for group in range(4):
                    k = wave(2 * other + group // 2)
                    lanes = slice(group * C, (group + 1) * C)
                    x = 4 * position + (group - shift) % 4
                    angle = 2.0 * math.pi * ((k * x) % NX) / NX
                    cos, sin = math.cos(angle), math.sin(angle)
                    forward[position, other, shift, 0, lanes] = cos if group % 2 == 0 else -sin
                    forward[position, other, shift, 1, lanes] = sin if group % 2 == 0 else cos
                    x = 4 * position + (group + shift) % 4
                    angle = 2.0 * math.pi * ((k * x) % NX) / NX
                    cos, sin = math.cos(angle), math.sin(angle)
                    backward[position, other, shift, 0, lanes] = cos if group % 2 == 0 else -sin
                    backward[position, other, shift, 1, lanes] = sin if group % 2 == 0 else cos
    shape = (N, N * 8, LANES)
    return forward.astype(np.float32).reshape(shape), backward.astype(np.float32).reshape(shape)


def input_table():
    table = np.zeros((4, N, 4, 2, LANES))
    for q in range(4):
        for device in range(N):
            for shift in range(4):
                for group in range(4):
                    other = (group - shift) % 4
                    angle = 2.0 * math.pi * (((4 * q + group) * (4 * device + other)) % NX) / NX
                    lanes = slice(group * C, (group + 1) * C)
                    table[q, device, shift, 0, lanes] = math.cos(angle)
                    table[q, device, shift, 1, lanes] = math.sin(angle)
    return table.astype(np.float32).reshape(-1, LANES)


DEPTH_FORWARD, DEPTH_BACKWARD = depth_tables()
PENCIL_PHASES = pencil_phases()
SLAB_FORWARD, SLAB_BACKWARD = slab_tables()
INPUT_TABLE = input_table()


def normal_tail(values):
    size = jnp.abs(values)
    bell = jnp.exp(-0.5 * values * values)
    denominator = 1.0 + (0.3275911 / math.sqrt(2.0)) * size
    t = pl.reciprocal(denominator, approx=True)
    t = t * (2.0 - denominator * t)
    poly = 0.5 * 1.061405429 * t - 0.5 * 1.453152027
    poly = poly * t + 0.5 * 1.421413741
    poly = poly * t - 0.5 * 0.284496736
    poly = poly * t + 0.5 * 0.254829592
    return bell, poly * t * bell


def field_kernel(
    pre_hbm,
    coef_hbm,
    source_hbm,
    proj_hbm,
    input_hbm,
    field_ref,
    up_ref,
    down_ref,
    pre_ref,
    coef_ref,
    source_ref,
    input_ref,
    proj_tile_ref,
    proj_ref,
    sems,
):
    size = C // CHUNKS
    copies = [pltpu.make_async_copy(proj_hbm, proj_ref, sems.at[CHUNKS])]
    for i in range(CHUNKS):
        part = pl.ds(i * size, size)
        copies.append(pltpu.make_async_copy(pre_hbm.at[part], pre_ref.at[part], sems.at[i]))
    copies.append(pltpu.make_async_copy(coef_hbm, coef_ref, sems.at[CHUNKS + 1]))
    copies.append(pltpu.make_async_copy(source_hbm, source_ref, sems.at[CHUNKS + 2]))
    copies.append(pltpu.make_async_copy(input_hbm, input_ref, sems.at[CHUNKS + 3]))
    for copy in copies:
        copy.start()
    copies[0].wait()
    for c in range(C):
        proj_tile_ref[c : c + 1, :] = jnp.full((1, 128), proj_ref[c], F32)

    def add_channel(c, total):
        values = pre_ref[c].astype(F32)
        _, tail = normal_tail(values)
        return total + proj_ref[c] * (jnp.maximum(values, 0.0) - jnp.abs(values) * tail)

    total = jnp.zeros((CX, CY, NZ), F32)
    for i in range(CHUNKS):
        copies[1 + i].wait()
        total = lax.fori_loop(i * size, (i + 1) * size, add_channel, total, unroll=2)
    for copy in copies[1 + CHUNKS :]:
        copy.wait()
    field_ref[...] = total
    up_ref[0:2] = total[2:4]
    down_ref[0:2] = total[0:2]
    up_ref[2] = coef_ref[3].astype(F32)
    up_ref[3] = source_ref[3].astype(F32)
    down_ref[2] = coef_ref[0].astype(F32)
    down_ref[3] = source_ref[0].astype(F32)


def slope_kernel(pre_ref, proj_ref, slope_ref):
    def one_channel(c, carry):
        values = pre_ref[c].astype(F32)
        bell, tail = normal_tail(values)
        below = jnp.where(values >= 0.0, 1.0 - tail, tail)
        slope = below + values * (bell * (1.0 / math.sqrt(2.0 * math.pi)))
        weight = proj_ref[pl.ds(c, 1), :]
        for x in range(CX):
            for side in range(2):
                piece = slope[x, :, side * 128 : (side + 1) * 128] * weight
                slope_ref[side, pl.ds(x * C + c, CY, stride=Y_PITCH), :] = piece
        return carry

    lax.fori_loop(0, C, one_channel, 0, unroll=2)


def nt_dot(left, right):
    return lax.dot_general(left, right, (((1,), (1,)), ((), ())), preferred_element_type=F32)


def tn_dot(left, right):
    return lax.dot_general(left, right, (((0,), (0,)), ((), ())), preferred_element_type=F32)


def pencil_forward(modes_ref, phase_ref, position, out_refs):
    for half in range(2):
        sums, diffs = [], []
        for part in range(2):
            rows = pl.ds(part * KZ + 8 * half, 8)
            first = [modes_ref[j, rows, :] for j in range(8)]
            second = [modes_ref[15 - j, rows, :] for j in range(8)]
            sums.append([a + b for a, b in zip(first, second)])
            diffs.append([a - b for a, b in zip(first, second)])
        for k in range(17):
            cosines = [math.cos(2.0 * math.pi * k * (7.5 - j) / NY) for j in range(8)]
            sines = [math.sin(2.0 * math.pi * k * (7.5 - j) / NY) for j in range(8)]
            even = [sum(w * v for w, v in zip(cosines, part)) for part in sums]
            w_cos = phase_ref[position * 34 + k]
            w_sin = phase_ref[position * 34 + 17 + k]
            if k == 0:
                results = [(0, even[0], even[1], w_sin)]
            else:
                odd = [sum(w * v for w, v in zip(sines, part)) for part in diffs]
                results = [(32 - k, even[0] + odd[1], even[1] - odd[0], -w_sin)]
                if k < 16:
                    results.append((k, even[0] - odd[1], even[1] + odd[0], w_sin))
            for index, real, imag, sin in results:
                row = (index % 2) * 32 + 8 * half
                out_ref = out_refs[index // 2 % 2]
                out_ref[index // 4, pl.ds(row, 8), :] = w_cos * real + sin * imag
                out_ref[index // 4, pl.ds(row + KZ, 8), :] = w_cos * imag - sin * real


def by_core(position, function, own_ref, other_ref):
    @pl.when(position % 2 == 0)
    def _():
        function((own_ref, other_ref))

    @pl.when(position % 2 == 1)
    def _():
        function((other_ref, own_ref))


def input_kernel(
    phase_ref,
    input_ref,
    table_hbm,
    own_ref,
    other_ref,
    rows_ref,
    modes_ref,
    table_ref,
    sem,
):
    copy = pltpu.make_async_copy(table_hbm, table_ref, sem)
    copy.start()
    for side in range(2):
        for c in range(C):
            piece = input_ref[c, :, :, side * 128 : (side + 1) * 128].astype(F32)
            rows_ref[side, c * PITCH : c * PITCH + CX * CY, :] = piece.reshape(CX * CY, 128)
    copy.wait()
    for y in range(CY):
        sides = [
            jnp.concatenate(
                [rows_ref[side, pl.ds(x * CY + y, C, stride=PITCH), :] for x in range(CX)], axis=0
            )
            for side in range(2)
        ]
        values = jnp.concatenate(sides, axis=1).astype(BF16)
        both = nt_dot(table_ref[...], values)
        modes_ref[y] = both[:32] + both[32:]
    position = lax.axis_index("pencil")
    forward = functools.partial(pencil_forward, modes_ref, phase_ref, position)
    by_core(position, forward, own_ref, other_ref)


def pack_kernel(field_ref, coef_ref, source_ref, before_ref, after_ref, up_ref, down_ref):
    for out_ref, cells, cell in ((up_ref, slice(14, 16), slice(15, 16)), (down_ref, slice(0, 2), slice(0, 1))):
        for x in range(8):
            if x < 2:
                rows = before_ref[x, cells, :]
            elif x < 6:
                rows = field_ref[x - 2, cells, :]
            else:
                rows = after_ref[x - 6, cells, :]
            out_ref[2 * x : 2 * x + 2, :] = rows
        for base, part, own_ref in ((16, 2, coef_ref), (22, 3, source_ref)):
            for x in range(6):
                if x == 0:
                    row = before_ref[part, cell, :]
                elif x == 5:
                    row = after_ref[part, cell, :]
                else:
                    row = own_ref[x - 1].astype(F32)[cell, :]
                out_ref[base + x : base + x + 1, :] = row
        out_ref[28:32, :] = jnp.zeros((4, NZ), F32)


def smooth(values):
    values = values + 0.5 * (pltpu.roll(values, 1, 2) + pltpu.roll(values, NZ - 1, 2))
    values = values + 0.5 * (pltpu.roll(values, 1, 1) + pltpu.roll(values, 31, 1))
    return 0.5 * (values[:-2] + values[2:]) + values[1:-1]


def act_parts(slope_ref, grad_ref, y):
    grads = []
    for x in range(CX):
        rows = slice(y * Y_PITCH + x * C, y * Y_PITCH + (x + 1) * C)
        slope = jnp.concatenate([slope_ref[0, rows, :], slope_ref[1, rows, :]], axis=1)
        grads.append(slope * grad_ref[x, 8 + y : 9 + y, :])
    act = jnp.concatenate(grads, axis=0)
    high = act.astype(BF16)
    return high, (act - high.astype(F32)).astype(BF16)


def grad_kernel(
    phase_ref,
    field_ref,
    coef_ref,
    source_ref,
    before_ref,
    after_ref,
    low_ref,
    high_ref,
    slope_ref,
    table_hbm,
    own_ref,
    other_ref,
    grad_ref,
    wide_field,
    wide_coef,
    wide_source,
    modes_ref,
    table_ref,
    sem,
):
    copy = pltpu.make_async_copy(table_hbm, table_ref, sem)
    copy.start()
    own = slice(8, 24)
    wide_field[...] = jnp.zeros_like(wide_field)
    wide_coef[...] = jnp.zeros_like(wide_coef)
    wide_source[...] = jnp.zeros_like(wide_source)
    wide_field[0:2, own, :] = before_ref[0:2]
    wide_field[2:6, own, :] = field_ref[...]
    wide_field[6:8, own, :] = after_ref[0:2]
    for x in range(8):
        wide_field[x, 6:8, :] = low_ref[2 * x : 2 * x + 2, :]
        wide_field[x, 24:26, :] = high_ref[2 * x : 2 * x + 2, :]
    for wide, cells, part, base in ((wide_coef, coef_ref, 2, 16), (wide_source, source_ref, 3, 22)):
        wide[0, own, :] = before_ref[part]
        wide[1:5, own, :] = cells[...].astype(F32)
        wide[5, own, :] = after_ref[part]
        for x in range(6):
            wide[x, 7:8, :] = low_ref[base + x : base + x + 1, :]
            wide[x, 24:25, :] = high_ref[base + x : base + x + 1, :]
    field = wide_field[...]
    center = field[1:7]
    residual = (16.0 / 3.0 - wide_coef[...]) * center - (2.0 / 3.0) * smooth(field) - wide_source[...]
    grad_ref[...] = (16.0 / 3.0 - wide_coef[1:5]) * residual[1:5] - (2.0 / 3.0) * smooth(residual)
    copy.wait()
    for y in range(CY):
        high, low = act_parts(slope_ref, grad_ref, y)
        both = nt_dot(table_ref[...], high)
        modes_ref[y] = both[:32] + both[32:] + nt_dot(table_ref[0:32, :], low)
    position = lax.axis_index("pencil")
    forward = functools.partial(pencil_forward, modes_ref, phase_ref, position)
    by_core(position, forward, own_ref, other_ref)


def combine_kernel(own_in_ref, got_in_ref, own_ref, got_ref, out_ref):
    out_ref[:, 0:64, :] = own_in_ref[...] + got_in_ref[...]
    out_ref[:, 64:128, :] = own_ref[...] + got_ref[...]


def local_kernel(
    pointwise_ref,
    slope_ref,
    grad_ref,
    forward_hbm,
    backward_hbm,
    input_hbm,
    out_ref,
    forward_ref,
    backward_ref,
    input_ref,
    sems,
):
    slab = lax.axis_index("slab")
    copies = [
        pltpu.make_async_copy(forward_hbm.at[slab], forward_ref, sems.at[0]),
        pltpu.make_async_copy(backward_hbm.at[slab], backward_ref, sems.at[1]),
        pltpu.make_async_copy(input_hbm, input_ref, sems.at[2]),
    ]
    for copy in copies:
        copy.start()
    rows = lax.broadcasted_iota(jnp.int32, (C, LANES), 0)
    lanes = lax.broadcasted_iota(jnp.int32, (C, LANES), 1)
    repeat = jnp.where(lanes % C == rows, 1.0, 0.0).astype(BF16)
    wide = jnp.dot(pointwise_ref[...], repeat, preferred_element_type=F32)
    wide = jnp.concatenate([wide] * CX, axis=0)
    rows = lax.broadcasted_iota(jnp.int32, (LANES, LANES), 0)
    lanes = lax.broadcasted_iota(jnp.int32, (LANES, LANES), 1)
    wide = jnp.where(rows // C == lanes // C, wide, 0.0).astype(BF16)
    wide = jnp.concatenate([wide, wide], axis=1)
    for y in range(CY):
        act = jnp.concatenate(act_parts(slope_ref, grad_ref, y), axis=0)
        out_ref[y] = jnp.dot(wide, act, preferred_element_type=F32)
    for copy in copies:
        copy.wait()


def slab_forward_kernel(parts_ref, table_ref, out_ref, raw_ref):
    raw = parts_ref[0, 0:64, :]
    for source in range(1, N // 2):
        raw = raw + parts_ref[source, 0:64, :]
    raw_ref[0:64, :] = raw
    raw_ref[64:128, :] = jnp.zeros((64, LANES), F32)
    for kz in range(KZ):
        out_ref[kz, 32:40, :] = raw_ref[pl.ds(kz, 8, stride=KZ), :]
    for ky in range(2):
        for half in range(2):
            pieces = []
            for part in range(2):
                rows = pl.ds(64 + ky * 32 + part * KZ + 8 * half, 8)
                total = parts_ref[0, rows, :]
                for source in range(1, N // 2):
                    total = total + parts_ref[source, rows, :]
                pieces.append([total] + [pltpu.roll(total, 32 * d, 1) for d in range(1, 4)])
            for owner in range(N):
                result = None
                for d in range(4):
                    for part in range(2):
                        row = owner * 8 + d * 2 + part
                        term = pieces[part][d] * table_ref[row : row + 1, :]
                        result = term if result is None else result + term
                out_ref[owner, pl.ds(ky * KZ + 8 * half, 8), :] = result


def flat_modes(block, group):
    lane_group = lax.broadcasted_iota(jnp.int32, (KZ, LANES), 1) // C
    row = lax.broadcasted_iota(jnp.int32, (KZ, LANES), 0)
    picked = jnp.where(lane_group == group, block, 0.0)
    picked = picked + pltpu.roll(picked, 64, 1)
    picked = picked + pltpu.roll(picked, 32, 1)
    tiles = [
        jnp.sum(jnp.where(row == 4 * tile + lane_group, picked, 0.0), axis=0, keepdims=True)
        for tile in range(4)
    ]
    return jnp.concatenate(tiles, axis=1)


def split_3(values):
    high = values.astype(BF16)
    rest = values - high.astype(F32)
    middle = rest.astype(BF16)
    low = (rest - middle.astype(F32)).astype(BF16)
    return high, middle, low


def minus_i(values, even_row):
    return jnp.where(even_row, pltpu.roll(values, 7, 0), -pltpu.roll(values, 1, 0))


def input_modes_at(parts_ref, table_ref):
    row = lax.broadcasted_iota(jnp.int32, (8, LANES), 0)
    group = lax.broadcasted_iota(jnp.int32, (8, LANES), 1) // C
    even_row = row % 2 == 0
    totals = [[None] * 4 for _ in range(4)]
    for source in range(N):
        values = parts_ref[source, 32:40, :]
        turned = minus_i(values, even_row)
        for shift in range(4):
            if shift:
                real, imag = pltpu.roll(values, 32 * shift, 1), pltpu.roll(turned, 32 * shift, 1)
            else:
                real, imag = values, turned
            for q in range(4):
                r = ((q * N + source) * 4 + shift) * 2
                term = real * table_ref[r : r + 1, :] + imag * table_ref[r + 1 : r + 2, :]
                last = totals[q][shift]
                totals[q][shift] = term if last is None else last + term
    lower, upper = [], []
    for q in range(4):
        lower.append(totals[q][0] + totals[q][1] + totals[q][2] + totals[q][3])
        result = None
        for shift in range(4):
            x = (group - shift) % 4
            cos = jnp.where(x == 0, 1.0, jnp.where(x == 2, -1.0, 0.0))
            sin = jnp.where(x == 1, -1.0, jnp.where(x == 3, 1.0, 0.0))
            term = cos * totals[q][shift] + sin * minus_i(totals[q][shift], even_row)
            result = term if result is None else result + term
        upper.append(result)
    return lower + upper


def back_kernel(parts_ref, weight_ref, table_ref, modes_ref, out_ref):
    total = parts_ref[0, 0:32, :]
    for source in range(1, N):
        total = total + parts_ref[source, 0:32, :]
    modes_ref[...] = total
    rows = lax.broadcasted_iota(jnp.int32, (KZ, KZ * C), 0)
    lanes = lax.broadcasted_iota(jnp.int32, (KZ, KZ * C), 1)
    mask = jnp.where(lanes // C == rows, 1.0, 0.0).astype(BF16)
    kz = lax.broadcasted_iota(jnp.int32, (KZ, LANES), 0)
    scale = jnp.where(kz == 0, 1.0 / CELLS, 2.0 / CELLS)
    for ky in range(2):
        block = total[ky * KZ : (ky + 1) * KZ]
        products = []
        for kx in range(2):
            real, imag = flat_modes(block, 2 * kx), flat_modes(block, 2 * kx + 1)
            w_real = weight_ref[0, kx, ky].astype(F32)
            w_imag = weight_ref[1, kx, ky].astype(F32)
            products.append(w_real * real + w_imag * imag)
            products.append(w_real * imag - w_imag * real)
        high, middle, low = split_3(jnp.concatenate(products, axis=0))
        back = scale * (nt_dot(mask, high) + nt_dot(mask, middle) + nt_dot(mask, low))
        for device in range(N):
            out_ref[device, ky * KZ : (ky + 1) * KZ, :] = back
    inputs = input_modes_at(parts_ref, table_ref)
    for device in range(N):
        values = inputs[device // 2]
        out_ref[device, 32:40, :] = values if device % 2 == 0 else pltpu.roll(values, 64, 1)


def weight_grad_kernel(modes_ref, parts_ref, out_ref):
    rows = lax.broadcasted_iota(jnp.int32, (KZ, KZ * C), 0)
    lanes = lax.broadcasted_iota(jnp.int32, (KZ, KZ * C), 1)
    mask = jnp.where(lanes // C == rows, 1.0, 0.0).astype(BF16)
    first = lax.broadcasted_iota(jnp.int32, (1, KZ * C), 1) < C
    scale = jnp.where(first, 1.0 / CELLS, 2.0 / CELLS)
    for ky in range(2):
        grads = modes_ref[ky * KZ : (ky + 1) * KZ, :]
        spread = []
        for part in range(2):
            inputs = parts_ref[pl.ds(32 + 2 * ky + part, KZ, stride=40), :]
            high, middle, low = split_3(inputs)
            spread.append(tn_dot(high, mask) + tn_dot(middle, mask) + tn_dot(low, mask))
        for kx in range(2):
            real = scale * flat_modes(grads, 2 * kx)
            imag = scale * flat_modes(grads, 2 * kx + 1)
            in_real, in_imag = [part[kx * C : (kx + 1) * C] for part in spread]
            out_ref[0, kx, ky] = (in_real * real + in_imag * imag).astype(BF16)
            out_ref[1, kx, ky] = (in_real * imag - in_imag * real).astype(BF16)


def slab_backward_kernel(parts_ref, table_ref, out_ref):
    for ky in range(2):
        for half in range(2):
            totals = [[None] * 4, [None] * 4]
            for source in range(N):
                values = parts_ref[source, pl.ds(ky * KZ + 8 * half, 8), :]
                for d in range(4):
                    for part in range(2):
                        row = source * 8 + d * 2 + part
                        term = values * table_ref[row : row + 1, :]
                        last = totals[part][d]
                        totals[part][d] = term if last is None else last + term
            for part in range(2):
                result = totals[part][0]
                for d in range(1, 4):
                    result = result + pltpu.roll(totals[part][d], 32 * d, 1)
                for device in range(N // 2):
                    out_ref[device, pl.ds(ky * 32 + part * KZ + 8 * half, 8), :] = result


def turn_modes(phase_ref, position, modes_ref, parts_refs):
    def turned(index, w_cos, w_sin, rows):
        ref = parts_refs[index // 2 % 2]
        row = (index % 2) * 32 + rows
        real = ref[index // 4, pl.ds(row, 8), :]
        imag = ref[index // 4, pl.ds(row + KZ, 8), :]
        return w_cos * real - w_sin * imag, w_cos * imag + w_sin * real

    for half in range(2):
        for k in range(17):
            w_cos = phase_ref[position * 34 + k]
            w_sin = phase_ref[position * 34 + 17 + k]
            if k == 0:
                even = turned(0, w_cos, w_sin, 8 * half)
                odd = None
            elif k == 16:
                even = turned(16, w_cos, -w_sin, 8 * half)
                odd = [-part for part in even]
            else:
                plus = turned(k, w_cos, w_sin, 8 * half)
                minus = turned(32 - k, w_cos, -w_sin, 8 * half)
                even = [p + m for p, m in zip(plus, minus)]
                odd = [p - m for p, m in zip(plus, minus)]
            for part in range(2):
                modes_ref[half, 0, k, part] = even[part]
                if odd is not None:
                    modes_ref[half, 1, k, part] = odd[part]


def output_kernel(
    phase_ref,
    own_ref,
    other_ref,
    local_ref,
    table_hbm,
    out_ref,
    modes_ref,
    rows_ref,
    flat_ref,
    table_ref,
    sem,
):
    copy = pltpu.make_async_copy(table_hbm, table_ref, sem)
    copy.start()
    position = lax.axis_index("pencil")
    turn = functools.partial(turn_modes, phase_ref, position, modes_ref)
    by_core(position, turn, own_ref, other_ref)
    for half in range(2):
        for y in range(8):
            even = [modes_ref[half, 0, 0, 0], modes_ref[half, 0, 0, 1]]
            odd = [None, None]
            for k in range(1, 17):
                angle = 2.0 * math.pi * k * (y - 7.5) / NY
                cos, sin = math.cos(angle), math.sin(angle)
                for part in range(2):
                    even[part] = even[part] + cos * modes_ref[half, 0, k, part]
                    term = sin * modes_ref[half, 1, k, part]
                    odd[part] = term if odd[part] is None else odd[part] + term
            rows = pl.ds(8 * half, 8)
            more = pl.ds(KZ + 8 * half, 8)
            rows_ref[y, rows, :] = even[0] - odd[1]
            rows_ref[y, more, :] = even[1] + odd[0]
            rows_ref[15 - y, rows, :] = even[0] + odd[1]
            rows_ref[15 - y, more, :] = even[1] - odd[0]
    copy.wait()
    for y in range(CY):
        values = rows_ref[y]
        high = values.astype(BF16)
        low = (values - high.astype(F32)).astype(BF16)
        stacked = jnp.concatenate([high, low, high], axis=0)
        result = tn_dot(stacked, table_ref[...]) + local_ref[y]
        for x in range(CX):
            for side in range(2):
                piece = result[x * C : (x + 1) * C, side * 128 : (side + 1) * 128]
                flat_ref[side, pl.ds(x * CY + y, C, stride=PITCH), :] = piece
    for side in range(2):
        for c in range(C):
            piece = flat_ref[side, c * PITCH : c * PITCH + CX * CY].astype(BF16)
            out_ref[c, :, :, side * 128 : (side + 1) * 128] = piece.reshape(CX, CY, 128)


def call(kernel, name, out, scratch=(), scalars=(), hbm=(), us=1):
    def run(*args):
        args = [
            pltpu.with_memory_space_constraint(arg, pltpu.HBM) if i in hbm else arg
            for i, arg in enumerate(args)
        ]
        single = not isinstance(out, list)
        specs = [
            pl.BlockSpec(
                memory_space=pltpu.SMEM if i in scalars else pltpu.HBM if i in hbm else pltpu.VMEM
            )
            for i in range(len(args))
        ]
        shapes = [jax.ShapeDtypeStruct(*o) for o in ([out] if single else out)]
        result = pl.pallas_call(
            kernel,
            out_shape=shapes,
            in_specs=specs,
            out_specs=[pl.BlockSpec(memory_space=pltpu.VMEM)] * len(shapes),
            scratch_shapes=[pltpu.VMEM(*s) if isinstance(s, tuple) else s for s in scratch],
            compiler_params=pltpu.CompilerParams(vmem_limit_bytes=VMEM_LIMIT),
            cost_estimate=pl.CostEstimate(
                flops=0, transcendentals=0, bytes_accessed=int(us * BYTES_PER_US)
            ),
            name=name,
        )(*args)
        return result[0] if single else result

    return run


def shards(
    layer_input, pre_activation, coefficient, source, projection, pointwise, spectral_weight
):
    up = [(i, (i + 1) % N) for i in range(N)]
    down = [(j, i) for i, j in up]
    swap = [(i, i ^ 1) for i in range(N)]
    same_core = [[i for i in range(N) if i % 2 == core] for core in range(2)]
    phases = jnp.asarray(PENCIL_PHASES)
    depth_forward = jnp.asarray(DEPTH_FORWARD)
    depth_backward = jnp.asarray(DEPTH_BACKWARD)
    edge = ((4, CY, NZ), F32)
    field, edge_up, edge_down, pre_activation, coefficient, source, layer_input, proj_tile = call(
        field_kernel,
        "field",
        [
            ((CX, CY, NZ), F32),
            edge,
            edge,
            ((C, CX, CY, NZ), BF16),
            ((CX, CY, NZ), BF16),
            ((CX, CY, NZ), BF16),
            ((C, CX, CY, NZ), BF16),
            ((C, 128), F32),
        ],
        scratch=[pltpu.SMEM((C,), F32), pltpu.SemaphoreType.DMA((CHUNKS + 4,))],
        hbm=(0, 1, 2, 3, 4),
        us=4,
    )(pre_activation, coefficient, source, projection, layer_input)
    before = lax.ppermute(edge_up, "slab", up)
    after = lax.ppermute(edge_down, "slab", down)
    slope = call(slope_kernel, "slope", ((2, CY * Y_PITCH, 128), F32), us=2)(pre_activation, proj_tile)
    half_modes = ((N // 2, 64, LANES), F32)
    own_in, other_in = call(
        input_kernel,
        "input_modes",
        [half_modes, half_modes],
        scratch=[
            ((2, C * PITCH, 128), F32),
            ((CY, 32, LANES), F32),
            (DEPTH_FORWARD.shape, BF16),
            pltpu.SemaphoreType.DMA(()),
        ],
        scalars=(0,),
        hbm=(2,),
        us=2,
    )(phases, layer_input, depth_forward)
    before, after, slope, own_in, other_in = lax.optimization_barrier(
        (before, after, slope, own_in, other_in)
    )
    got_in = lax.ppermute(other_in, "pencil", swap)
    side_up, side_down = call(pack_kernel, "pack", [((32, NZ), F32), ((32, NZ), F32)])(
        field, coefficient, source, before, after
    )
    low = lax.ppermute(side_up, "pencil", up)
    high = lax.ppermute(side_down, "pencil", down)
    own, other, grad = call(
        grad_kernel,
        "grad_modes",
        [half_modes, half_modes, ((CX, 32, NZ), F32)],
        scratch=[
            ((8, 32, NZ), F32),
            ((6, 32, NZ), F32),
            ((6, 32, NZ), F32),
            ((CY, 32, LANES), F32),
            (DEPTH_FORWARD.shape, BF16),
            pltpu.SemaphoreType.DMA(()),
        ],
        scalars=(0,),
        hbm=(9,),
        us=3,
    )(
        phases,
        field,
        coefficient,
        source,
        before,
        after,
        low,
        high,
        slope,
        depth_forward,
    )
    got = lax.ppermute(other, "pencil", swap)
    table = (SLAB_FORWARD.shape[1:], F32)
    local, slab_forward, slab_backward, input_phases = call(
        local_kernel,
        "local",
        [((CY, LANES, NZ), F32), table, table, (INPUT_TABLE.shape, F32)],
        scratch=[pltpu.SemaphoreType.DMA((3,))],
        hbm=(3, 4, 5),
    )(
        pointwise,
        slope,
        grad,
        jnp.asarray(SLAB_FORWARD),
        jnp.asarray(SLAB_BACKWARD),
        jnp.asarray(INPUT_TABLE),
    )
    got, local, slab_forward, slab_backward, input_phases = lax.optimization_barrier(
        (got, local, slab_forward, slab_backward, input_phases)
    )
    to_pencil = call(combine_kernel, "combine", ((N // 2, 128, LANES), F32))(
        own_in, got_in, own, got
    )
    from_pencil = lax.all_to_all(
        to_pencil, "pencil", 0, 0, axis_index_groups=same_core, tiled=True
    )
    chunks = ((N, 40, LANES), F32)
    to_slab = call(slab_forward_kernel, "slab_forward", chunks, scratch=[((128, LANES), F32)])(
        from_pencil, slab_forward
    )
    from_slab = lax.all_to_all(to_slab, "slab", 0, 0, tiled=True)
    modes, to_slab = call(back_kernel, "back", [((32, LANES), F32), chunks])(
        from_slab, spectral_weight, input_phases
    )
    from_slab = lax.all_to_all(to_slab, "slab", 0, 0, tiled=True)
    weight_grad = call(weight_grad_kernel, "weight_grad", (spectral_weight.shape, BF16))(
        modes, from_slab.reshape(N * 40, LANES)
    )
    to_pencil = call(slab_backward_kernel, "slab_backward", half_modes)(from_slab, slab_backward)
    own = lax.all_to_all(to_pencil, "pencil", 0, 0, axis_index_groups=same_core, tiled=True)
    other = lax.ppermute(own, "pencil", swap)
    input_grad = call(
        output_kernel,
        "output",
        ((C, CX, CY, NZ), BF16),
        scratch=[
            ((2, 2, 17, 2, 8, LANES), F32),
            ((CY, 32, LANES), F32),
            ((2, C * PITCH, 128), F32),
            (DEPTH_BACKWARD.shape, BF16),
            pltpu.SemaphoreType.DMA(()),
        ],
        scalars=(0,),
        hbm=(4,),
    )(phases, own, other, local, depth_backward)
    return (input_grad, weight_grad)


def solution(mesh):
    return jax.shard_map(
        shards,
        mesh=mesh,
        in_specs=(
            P(None, "slab", "pencil", None),
            P(None, "slab", "pencil", None),
            P("slab", "pencil", None),
            P("slab", "pencil", None),
            P(),
            P(),
            P(None, "slab", "pencil", None, None),
        ),
        out_specs=(P(None, "slab", "pencil", None), P(None, "slab", "pencil", None, None)),
        check_vma=False,
    )
```

```python
import functools
import math

import jax
import jax.numpy as jnp
import ml_dtypes
import numpy as np
from jax import lax
from jax.experimental import pallas as pl
from jax.experimental.pallas import tpu as pltpu
from jax.sharding import PartitionSpec as P

F32 = jnp.float32
BF16 = jnp.bfloat16
C, CX, CY, NZ = 32, 4, 16, 256
NX, NY = 64, 256
N = 16
KZ = 16
LANES = CX * C
CELLS = float(NX * NY * NZ)
VMEM_LIMIT = 24 * 1024 * 1024
PITCH = 68
Y_PITCH = LANES + 8
CHUNKS = 4
BYTES_PER_US = 3_690_000


def split_2(table):
    high = table.astype(ml_dtypes.bfloat16)
    low = (table - high.astype(np.float64)).astype(ml_dtypes.bfloat16)
    return high, low


def depth_tables():
    angles = 2.0 * math.pi * ((np.arange(KZ)[:, None] * np.arange(NZ)[None, :]) % NZ) / NZ
    table = np.concatenate([np.cos(angles), -np.sin(angles)], axis=0)
    high, low = split_2(table)
    return np.concatenate([high, low], axis=0), np.concatenate([high, high, low], axis=0)


def wave(index):
    return index if index < 16 else index - 32


def pencil_phases():
    position = 16.0 * np.arange(N)[:, None] + 7.5
    angles = 2.0 * math.pi * np.arange(17)[None, :] * position / NY
    rows = np.concatenate([np.cos(angles), np.sin(angles), np.zeros((N, 6))], axis=1)
    return np.repeat(rows[:, :, None], LANES, axis=2).astype(np.float32)


def slab_tables():
    forward = np.zeros((N, N, 4, 2, LANES))
    backward = np.zeros((N, N, 4, 2, LANES))
    for position in range(N):
        for other in range(N):
            for shift in range(4):
                for group in range(4):
                    k = wave(2 * other + group // 2)
                    lanes = slice(group * C, (group + 1) * C)
                    x = 4 * position + (group - shift) % 4
                    angle = 2.0 * math.pi * ((k * x) % NX) / NX
                    cos, sin = math.cos(angle), math.sin(angle)
                    forward[position, other, shift, 0, lanes] = cos if group % 2 == 0 else -sin
                    forward[position, other, shift, 1, lanes] = sin if group % 2 == 0 else cos
                    x = 4 * position + (group + shift) % 4
                    angle = 2.0 * math.pi * ((k * x) % NX) / NX
                    cos, sin = math.cos(angle), math.sin(angle)
                    backward[position, other, shift, 0, lanes] = cos if group % 2 == 0 else -sin
                    backward[position, other, shift, 1, lanes] = sin if group % 2 == 0 else cos
    shape = (N, N * 8, LANES)
    return forward.astype(np.float32).reshape(shape), backward.astype(np.float32).reshape(shape)


def input_table():
    table = np.zeros((4, N, 4, 2, LANES))
    for q in range(4):
        for device in range(N):
            for shift in range(4):
                for group in range(4):
                    other = (group - shift) % 4
                    angle = 2.0 * math.pi * (((4 * q + group) * (4 * device + other)) % NX) / NX
                    lanes = slice(group * C, (group + 1) * C)
                    table[q, device, shift, 0, lanes] = math.cos(angle)
                    table[q, device, shift, 1, lanes] = math.sin(angle)
    return table.astype(np.float32).reshape(-1, LANES)


DEPTH_FORWARD, DEPTH_BACKWARD = depth_tables()
PENCIL_PHASES = pencil_phases()
SLAB_FORWARD, SLAB_BACKWARD = slab_tables()
INPUT_TABLE = input_table()


def by_parity(position, function, first_ref, second_ref):
    @pl.when(position % 2 == 0)
    def _():
        function((first_ref, second_ref))

    @pl.when(position % 2 == 1)
    def _():
        function((second_ref, first_ref))


def field_kernel(
    pre_hbm,
    coef_hbm,
    source_hbm,
    proj_hbm,
    input_hbm,
    phase_hbm,
    table_hbm,
    field_ref,
    edge_a_ref,
    edge_b_ref,
    pre_ref,
    coef_ref,
    source_ref,
    input_ref,
    proj_tile_ref,
    phase_ref,
    table_ref,
    proj_ref,
    sems,
):
    size = C // CHUNKS
    copies = [pltpu.make_async_copy(proj_hbm, proj_ref, sems.at[CHUNKS])]
    for i in range(CHUNKS):
        part = pl.ds(i * size, size)
        copies.append(pltpu.make_async_copy(pre_hbm.at[part], pre_ref.at[part], sems.at[i]))
    copies.append(pltpu.make_async_copy(coef_hbm, coef_ref, sems.at[CHUNKS + 1]))
    copies.append(pltpu.make_async_copy(source_hbm, source_ref, sems.at[CHUNKS + 2]))
    copies.append(pltpu.make_async_copy(input_hbm, input_ref, sems.at[CHUNKS + 3]))
    phases = phase_hbm.at[lax.axis_index("pencil")]
    copies.append(pltpu.make_async_copy(phases, phase_ref, sems.at[CHUNKS + 4]))
    copies.append(pltpu.make_async_copy(table_hbm, table_ref, sems.at[CHUNKS + 5]))
    for copy in copies:
        copy.start()
    copies[0].wait()
    for c in range(C):
        proj_tile_ref[c : c + 1, :] = jnp.full((1, 128), proj_ref[c], F32)

    def add_channel(c, total):
        values = pre_ref[c].astype(F32)
        both = values + values * lax.erf(values * math.sqrt(0.5))
        return total + (0.5 * proj_ref[c]) * both

    total = jnp.zeros((CX, CY, NZ), F32)
    for i in range(CHUNKS):
        copies[1 + i].wait()
        total = lax.fori_loop(i * size, (i + 1) * size, add_channel, total, unroll=2)
    for copy in copies[1 + CHUNKS :]:
        copy.wait()
    field_ref[...] = total

    def edges(refs):
        up_ref, down_ref = refs
        up_ref[0:2] = total[2:4]
        down_ref[0:2] = total[0:2]
        up_ref[2] = coef_ref[3].astype(F32)
        up_ref[3] = source_ref[3].astype(F32)
        down_ref[2] = coef_ref[0].astype(F32)
        down_ref[3] = source_ref[0].astype(F32)

    by_parity(lax.axis_index("slab"), edges, edge_a_ref, edge_b_ref)


def slope_kernel(
    pre_ref,
    proj_ref,
    forward_hbm,
    backward_hbm,
    input_hbm,
    depth_hbm,
    slope_ref,
    forward_ref,
    backward_ref,
    input_ref,
    depth_ref,
    sems,
):
    slab = lax.axis_index("slab")
    copies = [
        pltpu.make_async_copy(forward_hbm.at[slab], forward_ref, sems.at[0]),
        pltpu.make_async_copy(backward_hbm.at[slab], backward_ref, sems.at[1]),
        pltpu.make_async_copy(input_hbm, input_ref, sems.at[2]),
        pltpu.make_async_copy(depth_hbm, depth_ref, sems.at[3]),
    ]
    for copy in copies:
        copy.start()

    def one_channel(c, carry):
        values = pre_ref[c].astype(F32)
        below = 0.5 + 0.5 * lax.erf(values * math.sqrt(0.5))
        bell = jnp.exp(-0.5 * values * values)
        slope = below + values * (bell * (1.0 / math.sqrt(2.0 * math.pi)))
        weight = proj_ref[pl.ds(c, 1), :]
        for x in range(CX):
            for side in range(2):
                piece = slope[x, :, side * 128 : (side + 1) * 128] * weight
                slope_ref[side, pl.ds(x * C + c, CY, stride=Y_PITCH), :] = piece
        return carry

    lax.fori_loop(0, C, one_channel, 0, unroll=2)
    for copy in copies:
        copy.wait()


def nt_dot(left, right):
    return lax.dot_general(left, right, (((1,), (1,)), ((), ())), preferred_element_type=F32)


def tn_dot(left, right):
    return lax.dot_general(left, right, (((0,), (0,)), ((), ())), preferred_element_type=F32)


def pencil_forward(modes_ref, phase_ref, out_refs):
    for half in range(2):
        sums, diffs = [], []
        for part in range(2):
            rows = pl.ds(part * KZ + 8 * half, 8)
            first = [modes_ref[j, rows, :] for j in range(8)]
            second = [modes_ref[15 - j, rows, :] for j in range(8)]
            sums.append([a + b for a, b in zip(first, second)])
            diffs.append([a - b for a, b in zip(first, second)])
        for k in range(17):
            cosines = [math.cos(2.0 * math.pi * k * (7.5 - j) / NY) for j in range(8)]
            sines = [math.sin(2.0 * math.pi * k * (7.5 - j) / NY) for j in range(8)]
            even = [sum(w * v for w, v in zip(cosines, part)) for part in sums]
            w_cos = phase_ref[k : k + 1, :]
            w_sin = phase_ref[17 + k : 18 + k, :]
            if k == 0:
                results = [(0, even[0], even[1], w_sin)]
            else:
                odd = [sum(w * v for w, v in zip(sines, part)) for part in diffs]
                results = [(32 - k, even[0] + odd[1], even[1] - odd[0], -w_sin)]
                if k < 16:
                    results.append((k, even[0] - odd[1], even[1] + odd[0], w_sin))
            for index, real, imag, sin in results:
                row = (index % 2) * 32 + 8 * half
                out_ref = out_refs[index // 2 % 2]
                out_ref[index // 4, pl.ds(row, 8), :] = w_cos * real + sin * imag
                out_ref[index // 4, pl.ds(row + KZ, 8), :] = w_cos * imag - sin * real


def input_kernel(
    phase_ref,
    input_ref,
    table_ref,
    own_ref,
    other_ref,
    rows_ref,
    modes_ref,
):
    for side in range(2):
        for c in range(C):
            piece = input_ref[c, :, :, side * 128 : (side + 1) * 128].astype(F32)
            rows_ref[side, c * PITCH : c * PITCH + CX * CY, :] = piece.reshape(CX * CY, 128)
    for y in range(CY):
        sides = [
            jnp.concatenate(
                [rows_ref[side, pl.ds(x * CY + y, C, stride=PITCH), :] for x in range(CX)], axis=0
            )
            for side in range(2)
        ]
        values = jnp.concatenate(sides, axis=1).astype(BF16)
        both = nt_dot(table_ref[...], values)
        modes_ref[y] = both[:32] + both[32:]
    position = lax.axis_index("pencil")
    forward = functools.partial(pencil_forward, modes_ref, phase_ref)
    by_parity(position, forward, own_ref, other_ref)


def pack_kernel(field_ref, coef_ref, source_ref, got_a_ref, got_b_ref, out_a_ref, out_b_ref):
    def pack(x_refs, y_refs):
        after_ref, before_ref = x_refs
        up_ref, down_ref = y_refs
        for out_ref, first in ((up_ref, 14), (down_ref, 0)):
            cells = slice(first, first + 2)
            cell = slice(15, 16) if first else slice(0, 1)
            for x in range(8):
                if x < 2:
                    rows = before_ref[x, cells, :]
                elif x < 6:
                    rows = field_ref[x - 2, cells, :]
                else:
                    rows = after_ref[x - 6, cells, :]
                out_ref[2 * x : 2 * x + 2, :] = rows
            for base, part, own_ref in ((16, 2, coef_ref), (22, 3, source_ref)):
                for x in range(6):
                    if x == 0:
                        row = before_ref[part, cell, :]
                    elif x == 5:
                        row = after_ref[part, cell, :]
                    else:
                        row = own_ref[x - 1].astype(F32)[cell, :]
                    out_ref[base + x : base + x + 1, :] = row
            out_ref[28:32, :] = jnp.zeros((4, NZ), F32)

    def with_x(x_refs):
        y = lax.axis_index("pencil")
        by_parity(y, functools.partial(pack, x_refs), out_a_ref, out_b_ref)

    by_parity(lax.axis_index("slab"), with_x, got_a_ref, got_b_ref)


def smooth(values):
    values = values + 0.5 * (pltpu.roll(values, 1, 2) + pltpu.roll(values, NZ - 1, 2))
    values = values + 0.5 * (pltpu.roll(values, 1, 1) + pltpu.roll(values, 31, 1))
    return 0.5 * (values[:-2] + values[2:]) + values[1:-1]


def act_parts(slope_ref, grad_ref, y):
    grads = []
    for x in range(CX):
        rows = slice(y * Y_PITCH + x * C, y * Y_PITCH + (x + 1) * C)
        slope = jnp.concatenate([slope_ref[0, rows, :], slope_ref[1, rows, :]], axis=1)
        grads.append(slope * grad_ref[x, 8 + y : 9 + y, :])
    act = jnp.concatenate(grads, axis=0)
    high = act.astype(BF16)
    return high, (act - high.astype(F32)).astype(BF16)


def grad_kernel(
    phase_ref,
    field_ref,
    coef_ref,
    source_ref,
    x_a_ref,
    x_b_ref,
    y_a_ref,
    y_b_ref,
    slope_ref,
    table_ref,
    own_ref,
    other_ref,
    grad_ref,
    wide_field,
    wide_coef,
    wide_source,
    modes_ref,
):
    own = slice(8, 24)
    wide_field[2:6, own, :] = field_ref[...]
    wide_coef[1:5, own, :] = coef_ref[...].astype(F32)
    wide_source[1:5, own, :] = source_ref[...].astype(F32)

    def x_sides(refs):
        after_ref, before_ref = refs
        wide_field[0:2, own, :] = before_ref[0:2]
        wide_field[6:8, own, :] = after_ref[0:2]
        for wide, part in ((wide_coef, 2), (wide_source, 3)):
            wide[0, own, :] = before_ref[part]
            wide[5, own, :] = after_ref[part]

    def y_sides(refs):
        high_ref, low_ref = refs
        for x in range(8):
            wide_field[x, 6:8, :] = low_ref[2 * x : 2 * x + 2, :]
            wide_field[x, 24:26, :] = high_ref[2 * x : 2 * x + 2, :]
        for wide, base in ((wide_coef, 16), (wide_source, 22)):
            for x in range(6):
                wide[x, 7:8, :] = low_ref[base + x : base + x + 1, :]
                wide[x, 24:25, :] = high_ref[base + x : base + x + 1, :]

    by_parity(lax.axis_index("slab"), x_sides, x_a_ref, x_b_ref)
    by_parity(lax.axis_index("pencil"), y_sides, y_a_ref, y_b_ref)
    field = wide_field[...]
    center = field[1:7]
    residual = (16.0 / 3.0 - wide_coef[...]) * center - (2.0 / 3.0) * smooth(field) - wide_source[...]
    grad_ref[...] = (16.0 / 3.0 - wide_coef[1:5]) * residual[1:5] - (2.0 / 3.0) * smooth(residual)
    for y in range(CY):
        high, low = act_parts(slope_ref, grad_ref, y)
        both = nt_dot(table_ref[...], high)
        modes_ref[y] = both[:32] + both[32:] + nt_dot(table_ref[0:32, :], low)
    position = lax.axis_index("pencil")
    forward = functools.partial(pencil_forward, modes_ref, phase_ref)
    by_parity(position, forward, own_ref, other_ref)


def combine_kernel(own_in_ref, got_in_ref, own_ref, got_ref, out_ref):
    out_ref[:, 0:64, :] = own_in_ref[...] + got_in_ref[...]
    out_ref[:, 64:128, :] = own_ref[...] + got_ref[...]


def local_kernel(pointwise_ref, slope_ref, grad_ref, out_ref):
    rows = lax.broadcasted_iota(jnp.int32, (C, LANES), 0)
    lanes = lax.broadcasted_iota(jnp.int32, (C, LANES), 1)
    repeat = jnp.where(lanes % C == rows, 1.0, 0.0).astype(BF16)
    wide = jnp.dot(pointwise_ref[...], repeat, preferred_element_type=F32)
    wide = jnp.concatenate([wide] * CX, axis=0)
    rows = lax.broadcasted_iota(jnp.int32, (LANES, LANES), 0)
    lanes = lax.broadcasted_iota(jnp.int32, (LANES, LANES), 1)
    wide = jnp.where(rows // C == lanes // C, wide, 0.0).astype(BF16)
    wide = jnp.concatenate([wide, wide], axis=1)
    for y in range(CY):
        act = jnp.concatenate(act_parts(slope_ref, grad_ref, y), axis=0)
        out_ref[y] = jnp.dot(wide, act, preferred_element_type=F32)


def slab_forward_kernel(parts_ref, table_ref, out_ref, raw_ref):
    raw = parts_ref[0, 0:64, :]
    for source in range(1, N // 2):
        raw = raw + parts_ref[source, 0:64, :]
    raw_ref[0:64, :] = raw
    raw_ref[64:128, :] = jnp.zeros((64, LANES), F32)
    for kz in range(KZ):
        out_ref[kz, 32:40, :] = raw_ref[pl.ds(kz, 8, stride=KZ), :]
    for ky in range(2):
        for half in range(2):
            pieces = []
            for part in range(2):
                rows = pl.ds(64 + ky * 32 + part * KZ + 8 * half, 8)
                total = parts_ref[0, rows, :]
                for source in range(1, N // 2):
                    total = total + parts_ref[source, rows, :]
                pieces.append([total] + [pltpu.roll(total, 32 * d, 1) for d in range(1, 4)])
            for owner in range(N):
                result = None
                for d in range(4):
                    for part in range(2):
                        row = owner * 8 + d * 2 + part
                        term = pieces[part][d] * table_ref[row : row + 1, :]
                        result = term if result is None else result + term
                out_ref[owner, pl.ds(ky * KZ + 8 * half, 8), :] = result


def flat_modes(block, group):
    lane_group = lax.broadcasted_iota(jnp.int32, (KZ, LANES), 1) // C
    row = lax.broadcasted_iota(jnp.int32, (KZ, LANES), 0)
    picked = jnp.where(lane_group == group, block, 0.0)
    picked = picked + pltpu.roll(picked, 64, 1)
    picked = picked + pltpu.roll(picked, 32, 1)
    tiles = [
        jnp.sum(jnp.where(row == 4 * tile + lane_group, picked, 0.0), axis=0, keepdims=True)
        for tile in range(4)
    ]
    return jnp.concatenate(tiles, axis=1)


def split_3(values):
    high = values.astype(BF16)
    rest = values - high.astype(F32)
    middle = rest.astype(BF16)
    low = (rest - middle.astype(F32)).astype(BF16)
    return high, middle, low


def minus_i(values, even_row):
    return jnp.where(even_row, pltpu.roll(values, 7, 0), -pltpu.roll(values, 1, 0))


def input_modes_at(parts_ref, table_ref):
    row = lax.broadcasted_iota(jnp.int32, (8, LANES), 0)
    group = lax.broadcasted_iota(jnp.int32, (8, LANES), 1) // C
    even_row = row % 2 == 0
    totals = [[None] * 4 for _ in range(4)]
    for source in range(N):
        values = parts_ref[source, 32:40, :]
        turned = minus_i(values, even_row)
        for shift in range(4):
            if shift:
                real, imag = pltpu.roll(values, 32 * shift, 1), pltpu.roll(turned, 32 * shift, 1)
            else:
                real, imag = values, turned
            for q in range(4):
                r = ((q * N + source) * 4 + shift) * 2
                term = real * table_ref[r : r + 1, :] + imag * table_ref[r + 1 : r + 2, :]
                last = totals[q][shift]
                totals[q][shift] = term if last is None else last + term
    lower, upper = [], []
    for q in range(4):
        lower.append(totals[q][0] + totals[q][1] + totals[q][2] + totals[q][3])
        result = None
        for shift in range(4):
            x = (group - shift) % 4
            cos = jnp.where(x == 0, 1.0, jnp.where(x == 2, -1.0, 0.0))
            sin = jnp.where(x == 1, -1.0, jnp.where(x == 3, 1.0, 0.0))
            term = cos * totals[q][shift] + sin * minus_i(totals[q][shift], even_row)
            result = term if result is None else result + term
        upper.append(result)
    return lower + upper


def back_kernel(parts_ref, weight_ref, table_ref, modes_ref, out_ref):
    total = parts_ref[0, 0:32, :]
    for source in range(1, N):
        total = total + parts_ref[source, 0:32, :]
    modes_ref[...] = total
    rows = lax.broadcasted_iota(jnp.int32, (KZ, KZ * C), 0)
    lanes = lax.broadcasted_iota(jnp.int32, (KZ, KZ * C), 1)
    mask = jnp.where(lanes // C == rows, 1.0, 0.0).astype(BF16)
    kz = lax.broadcasted_iota(jnp.int32, (KZ, LANES), 0)
    scale = jnp.where(kz == 0, 1.0 / CELLS, 2.0 / CELLS)
    for ky in range(2):
        block = total[ky * KZ : (ky + 1) * KZ]
        products = []
        for kx in range(2):
            real, imag = flat_modes(block, 2 * kx), flat_modes(block, 2 * kx + 1)
            w_real = weight_ref[0, kx, ky].astype(F32)
            w_imag = weight_ref[1, kx, ky].astype(F32)
            products.append(w_real * real + w_imag * imag)
            products.append(w_real * imag - w_imag * real)
        high, middle, low = split_3(jnp.concatenate(products, axis=0))
        back = scale * (nt_dot(mask, high) + nt_dot(mask, middle) + nt_dot(mask, low))
        for device in range(N):
            out_ref[device, ky * KZ : (ky + 1) * KZ, :] = back
    inputs = input_modes_at(parts_ref, table_ref)
    for device in range(N):
        values = inputs[device // 2]
        out_ref[device, 32:40, :] = values if device % 2 == 0 else pltpu.roll(values, 64, 1)


def weight_grad_kernel(modes_ref, parts_ref, out_ref):
    rows = lax.broadcasted_iota(jnp.int32, (KZ, KZ * C), 0)
    lanes = lax.broadcasted_iota(jnp.int32, (KZ, KZ * C), 1)
    mask = jnp.where(lanes // C == rows, 1.0, 0.0).astype(BF16)
    first = lax.broadcasted_iota(jnp.int32, (1, KZ * C), 1) < C
    scale = jnp.where(first, 1.0 / CELLS, 2.0 / CELLS)
    for ky in range(2):
        grads = modes_ref[ky * KZ : (ky + 1) * KZ, :]
        spread = []
        for part in range(2):
            inputs = parts_ref[pl.ds(32 + 2 * ky + part, KZ, stride=40), :]
            high, middle, low = split_3(inputs)
            spread.append(tn_dot(high, mask) + tn_dot(middle, mask) + tn_dot(low, mask))
        for kx in range(2):
            real = scale * flat_modes(grads, 2 * kx)
            imag = scale * flat_modes(grads, 2 * kx + 1)
            in_real, in_imag = [part[kx * C : (kx + 1) * C] for part in spread]
            out_ref[0, kx, ky] = (in_real * real + in_imag * imag).astype(BF16)
            out_ref[1, kx, ky] = (in_real * imag - in_imag * real).astype(BF16)


def slab_backward_kernel(parts_ref, table_ref, out_ref):
    for ky in range(2):
        for half in range(2):
            totals = [[None] * 4, [None] * 4]
            for source in range(N):
                values = parts_ref[source, pl.ds(ky * KZ + 8 * half, 8), :]
                for d in range(4):
                    for part in range(2):
                        row = source * 8 + d * 2 + part
                        term = values * table_ref[row : row + 1, :]
                        last = totals[part][d]
                        totals[part][d] = term if last is None else last + term
            for part in range(2):
                result = totals[part][0]
                for d in range(1, 4):
                    result = result + pltpu.roll(totals[part][d], 32 * d, 1)
                for device in range(N // 2):
                    out_ref[device, pl.ds(ky * 32 + part * KZ + 8 * half, 8), :] = result


def turn_modes(phase_ref, modes_ref, parts_refs):
    def turned(index, w_cos, w_sin, rows):
        ref = parts_refs[index // 2 % 2]
        row = (index % 2) * 32 + rows
        real = ref[index // 4, pl.ds(row, 8), :]
        imag = ref[index // 4, pl.ds(row + KZ, 8), :]
        return w_cos * real - w_sin * imag, w_cos * imag + w_sin * real

    for half in range(2):
        for k in range(17):
            w_cos = phase_ref[k : k + 1, :]
            w_sin = phase_ref[17 + k : 18 + k, :]
            if k == 0:
                even = turned(0, w_cos, w_sin, 8 * half)
                odd = None
            elif k == 16:
                even = turned(16, w_cos, -w_sin, 8 * half)
                odd = [-part for part in even]
            else:
                plus = turned(k, w_cos, w_sin, 8 * half)
                minus = turned(32 - k, w_cos, -w_sin, 8 * half)
                even = [p + m for p, m in zip(plus, minus)]
                odd = [p - m for p, m in zip(plus, minus)]
            for part in range(2):
                modes_ref[half, 0, k, part] = even[part]
                if odd is not None:
                    modes_ref[half, 1, k, part] = odd[part]


def output_kernel(
    phase_ref,
    own_ref,
    other_ref,
    local_ref,
    table_ref,
    out_ref,
    modes_ref,
    rows_ref,
    flat_ref,
):
    position = lax.axis_index("pencil")
    turn = functools.partial(turn_modes, phase_ref, modes_ref)
    by_parity(position, turn, own_ref, other_ref)
    for half in range(2):
        for y in range(8):
            even = [modes_ref[half, 0, 0, 0], modes_ref[half, 0, 0, 1]]
            odd = [None, None]
            for k in range(1, 17):
                angle = 2.0 * math.pi * k * (y - 7.5) / NY
                cos, sin = math.cos(angle), math.sin(angle)
                for part in range(2):
                    even[part] = even[part] + cos * modes_ref[half, 0, k, part]
                    term = sin * modes_ref[half, 1, k, part]
                    odd[part] = term if odd[part] is None else odd[part] + term
            rows = pl.ds(8 * half, 8)
            more = pl.ds(KZ + 8 * half, 8)
            rows_ref[y, rows, :] = even[0] - odd[1]
            rows_ref[y, more, :] = even[1] + odd[0]
            rows_ref[15 - y, rows, :] = even[0] + odd[1]
            rows_ref[15 - y, more, :] = even[1] - odd[0]
    for y in range(CY):
        values = rows_ref[y]
        high = values.astype(BF16)
        low = (values - high.astype(F32)).astype(BF16)
        stacked = jnp.concatenate([high, low, high], axis=0)
        result = tn_dot(stacked, table_ref[...]) + local_ref[y]
        for x in range(CX):
            for side in range(2):
                piece = result[x * C : (x + 1) * C, side * 128 : (side + 1) * 128]
                flat_ref[side, pl.ds(x * CY + y, C, stride=PITCH), :] = piece
    for side in range(2):
        for c in range(C):
            piece = flat_ref[side, c * PITCH : c * PITCH + CX * CY].astype(BF16)
            out_ref[c, :, :, side * 128 : (side + 1) * 128] = piece.reshape(CX, CY, 128)


def call(kernel, name, out, scratch=(), scalars=(), hbm=(), us=1):
    def run(*args):
        args = [
            pltpu.with_memory_space_constraint(arg, pltpu.HBM) if i in hbm else arg
            for i, arg in enumerate(args)
        ]
        single = not isinstance(out, list)
        specs = [
            pl.BlockSpec(
                memory_space=pltpu.SMEM if i in scalars else pltpu.HBM if i in hbm else pltpu.VMEM
            )
            for i in range(len(args))
        ]
        shapes = [jax.ShapeDtypeStruct(*o) for o in ([out] if single else out)]
        result = pl.pallas_call(
            kernel,
            out_shape=shapes,
            in_specs=specs,
            out_specs=[pl.BlockSpec(memory_space=pltpu.VMEM)] * len(shapes),
            scratch_shapes=[pltpu.VMEM(*s) if isinstance(s, tuple) else s for s in scratch],
            compiler_params=pltpu.CompilerParams(vmem_limit_bytes=VMEM_LIMIT),
            cost_estimate=pl.CostEstimate(
                flops=0, transcendentals=0, bytes_accessed=int(us * BYTES_PER_US)
            ),
            name=name,
        )(*args)
        return result[0] if single else result

    return run


def shards(
    layer_input, pre_activation, coefficient, source, projection, pointwise, spectral_weight
):
    swap = [(i, i ^ 1) for i in range(N)]
    swap_odd = [(i, (i + 1 if i % 2 else i - 1) % N) for i in range(N)]
    same_core = [[i for i in range(N) if i % 2 == core] for core in range(2)]
    edge = ((4, CY, NZ), F32)
    (
        field,
        edge_a,
        edge_b,
        pre_activation,
        coefficient,
        source,
        layer_input,
        proj_tile,
        phases,
        depth_forward,
    ) = call(
        field_kernel,
        "field",
        [
            ((CX, CY, NZ), F32),
            edge,
            edge,
            ((C, CX, CY, NZ), BF16),
            ((CX, CY, NZ), BF16),
            ((CX, CY, NZ), BF16),
            ((C, CX, CY, NZ), BF16),
            ((C, 128), F32),
            (PENCIL_PHASES.shape[1:], F32),
            (DEPTH_FORWARD.shape, BF16),
        ],
        scratch=[pltpu.SMEM((C,), F32), pltpu.SemaphoreType.DMA((CHUNKS + 6,))],
        hbm=(0, 1, 2, 3, 4, 5, 6),
        us=4,
    )(
        pre_activation,
        coefficient,
        source,
        projection,
        layer_input,
        jnp.asarray(PENCIL_PHASES),
        jnp.asarray(DEPTH_FORWARD),
    )
    x_a = lax.ppermute(edge_a, "slab", swap)
    x_b = lax.ppermute(edge_b, "slab", swap_odd)
    table = (SLAB_FORWARD.shape[1:], F32)
    slope, slab_forward, slab_backward, input_phases, depth_backward = call(
        slope_kernel,
        "slope",
        [
            ((2, CY * Y_PITCH, 128), F32),
            table,
            table,
            (INPUT_TABLE.shape, F32),
            (DEPTH_BACKWARD.shape, BF16),
        ],
        scratch=[pltpu.SemaphoreType.DMA((4,))],
        hbm=(2, 3, 4, 5),
        us=2,
    )(
        pre_activation,
        proj_tile,
        jnp.asarray(SLAB_FORWARD),
        jnp.asarray(SLAB_BACKWARD),
        jnp.asarray(INPUT_TABLE),
        jnp.asarray(DEPTH_BACKWARD),
    )
    half_modes = ((N // 2, 64, LANES), F32)
    own_in, other_in = call(
        input_kernel,
        "input_modes",
        [half_modes, half_modes],
        scratch=[
            ((2, C * PITCH, 128), F32),
            ((CY, 32, LANES), F32),
        ],
        us=2,
    )(phases, layer_input, depth_forward)
    x_a, x_b, slope, own_in, other_in = lax.optimization_barrier(
        (x_a, x_b, slope, own_in, other_in)
    )
    got_in = lax.ppermute(other_in, "pencil", swap)
    side_a, side_b = call(pack_kernel, "pack", [((32, NZ), F32), ((32, NZ), F32)])(
        field, coefficient, source, x_a, x_b
    )
    y_a = lax.ppermute(side_a, "pencil", swap)
    y_b = lax.ppermute(side_b, "pencil", swap_odd)
    y_a, y_b, got_in = lax.optimization_barrier((y_a, y_b, got_in))
    own, other, grad = call(
        grad_kernel,
        "grad_modes",
        [half_modes, half_modes, ((CX, 32, NZ), F32)],
        scratch=[
            ((8, 32, NZ), F32),
            ((6, 32, NZ), F32),
            ((6, 32, NZ), F32),
            ((CY, 32, LANES), F32),
        ],
        us=3,
    )(
        phases,
        field,
        coefficient,
        source,
        x_a,
        x_b,
        y_a,
        y_b,
        slope,
        depth_forward,
    )
    got = lax.ppermute(other, "pencil", swap)
    local = call(local_kernel, "local", ((CY, LANES, NZ), F32))(pointwise, slope, grad)
    got, local = lax.optimization_barrier((got, local))
    to_pencil = call(combine_kernel, "combine", ((N // 2, 128, LANES), F32))(
        own_in, got_in, own, got
    )
    from_pencil = lax.all_to_all(
        to_pencil, "pencil", 0, 0, axis_index_groups=same_core, tiled=True
    )
    chunks = ((N, 40, LANES), F32)
    to_slab = call(slab_forward_kernel, "slab_forward", chunks, scratch=[((128, LANES), F32)])(
        from_pencil, slab_forward
    )
    from_slab = lax.all_to_all(to_slab, "slab", 0, 0, tiled=True)
    modes, to_slab = call(back_kernel, "back", [((32, LANES), F32), chunks])(
        from_slab, spectral_weight, input_phases
    )
    from_slab = lax.all_to_all(to_slab, "slab", 0, 0, tiled=True)
    weight_grad = call(weight_grad_kernel, "weight_grad", (spectral_weight.shape, BF16))(
        modes, from_slab.reshape(N * 40, LANES)
    )
    to_pencil = call(slab_backward_kernel, "slab_backward", half_modes)(from_slab, slab_backward)
    own = lax.all_to_all(to_pencil, "pencil", 0, 0, axis_index_groups=same_core, tiled=True)
    other = lax.ppermute(own, "pencil", swap)
    input_grad = call(
        output_kernel,
        "output",
        ((C, CX, CY, NZ), BF16),
        scratch=[
            ((2, 2, 17, 2, 8, LANES), F32),
            ((CY, 32, LANES), F32),
            ((2, C * PITCH, 128), F32),
        ],
    )(phases, own, other, local, depth_backward)
    return (input_grad, weight_grad)


def solution(mesh):
    return jax.shard_map(
        shards,
        mesh=mesh,
        in_specs=(
            P(None, "slab", "pencil", None),
            P(None, "slab", "pencil", None),
            P("slab", "pencil", None),
            P("slab", "pencil", None),
            P(),
            P(),
            P(None, "slab", "pencil", None, None),
        ),
        out_specs=(P(None, "slab", "pencil", None), P(None, "slab", "pencil", None, None)),
        check_vma=False,
    )
```

```python
import functools
import math

import jax
import jax.numpy as jnp
import ml_dtypes
import numpy as np
from jax import lax
from jax.experimental import pallas as pl
from jax.experimental.pallas import tpu as pltpu
from jax.sharding import PartitionSpec as P

F32 = jnp.float32
BF16 = jnp.bfloat16
C, CX, CY, NZ = 32, 4, 16, 256
NX, NY = 64, 256
N = 16
KZ = 16
LANES = CX * C
SLAB_ORDER = [2 * z + y for y in range(2) for z in (0, 3, 6, 1, 4, 7, 2, 5)]
SLAB_RANK = [SLAB_ORDER.index(device) for device in range(N)]
CHIP_ORDER = [0, 1, 3, 2, 6, 7, 5, 4]
CHIP_RANK = [CHIP_ORDER.index(chip) for chip in range(N // 2)]
CELLS = float(NX * NY * NZ)
VMEM_LIMIT = 24 * 1024 * 1024
PITCH = 68
Y_PITCH = LANES + 8
CHUNKS = 4
BYTES_PER_US = 3_690_000


def split_2(table):
    high = table.astype(ml_dtypes.bfloat16)
    low = (table - high.astype(np.float64)).astype(ml_dtypes.bfloat16)
    return high, low


def depth_tables():
    angles = 2.0 * math.pi * ((np.arange(KZ)[:, None] * np.arange(NZ)[None, :]) % NZ) / NZ
    table = np.concatenate([np.cos(angles), -np.sin(angles)], axis=0)
    high, low = split_2(table)
    return np.concatenate([high, low], axis=0), np.concatenate([high, high, low], axis=0)


def wave(index):
    return index if index < 16 else index - 32


def pencil_phases():
    position = 16.0 * np.arange(N)[:, None] + 7.5
    angles = 2.0 * math.pi * np.arange(17)[None, :] * position / NY
    rows = np.concatenate([np.cos(angles), np.sin(angles), np.zeros((N, 6))], axis=1)
    return np.repeat(rows[:, :, None], LANES, axis=2).astype(np.float32)


def slab_tables():
    forward = np.zeros((N, N, 4, 2, LANES))
    backward = np.zeros((N, N, 4, 2, LANES))
    for position in range(N):
        for other in range(N):
            for shift in range(4):
                for group in range(4):
                    k = wave(2 * other + group // 2)
                    lanes = slice(group * C, (group + 1) * C)
                    x = 4 * position + (group - shift) % 4
                    angle = 2.0 * math.pi * ((k * x) % NX) / NX
                    cos, sin = math.cos(angle), math.sin(angle)
                    forward[position, other, shift, 0, lanes] = cos if group % 2 == 0 else -sin
                    forward[position, other, shift, 1, lanes] = sin if group % 2 == 0 else cos
                    x = 4 * position + (group + shift) % 4
                    angle = 2.0 * math.pi * ((k * x) % NX) / NX
                    cos, sin = math.cos(angle), math.sin(angle)
                    backward[position, other, shift, 0, lanes] = cos if group % 2 == 0 else -sin
                    backward[position, other, shift, 1, lanes] = sin if group % 2 == 0 else cos
    shape = (N, N * 8, LANES)
    return forward.astype(np.float32).reshape(shape), backward.astype(np.float32).reshape(shape)


def input_table():
    table = np.zeros((4, N, 4, 2, LANES))
    for q in range(4):
        for device in range(N):
            for shift in range(4):
                for group in range(4):
                    other = (group - shift) % 4
                    angle = 2.0 * math.pi * (((4 * q + group) * (4 * device + other)) % NX) / NX
                    lanes = slice(group * C, (group + 1) * C)
                    table[q, device, shift, 0, lanes] = math.cos(angle)
                    table[q, device, shift, 1, lanes] = math.sin(angle)
    return table.astype(np.float32).reshape(-1, LANES)


DEPTH_FORWARD, DEPTH_BACKWARD = depth_tables()
PENCIL_PHASES = pencil_phases()
SLAB_FORWARD, SLAB_BACKWARD = slab_tables()
INPUT_TABLE = input_table()


def by_parity(position, function, first_ref, second_ref):
    @pl.when(position % 2 == 0)
    def _():
        function((first_ref, second_ref))

    @pl.when(position % 2 == 1)
    def _():
        function((second_ref, first_ref))


def field_kernel(
    pre_hbm,
    coef_hbm,
    source_hbm,
    proj_hbm,
    input_hbm,
    phase_hbm,
    table_hbm,
    field_ref,
    edge_a_ref,
    edge_b_ref,
    pre_ref,
    coef_ref,
    source_ref,
    input_ref,
    proj_tile_ref,
    phase_ref,
    table_ref,
    proj_ref,
    sems,
):
    size = C // CHUNKS
    copies = [pltpu.make_async_copy(proj_hbm, proj_ref, sems.at[CHUNKS])]
    for i in range(CHUNKS):
        part = pl.ds(i * size, size)
        copies.append(pltpu.make_async_copy(pre_hbm.at[part], pre_ref.at[part], sems.at[i]))
    copies.append(pltpu.make_async_copy(coef_hbm, coef_ref, sems.at[CHUNKS + 1]))
    copies.append(pltpu.make_async_copy(source_hbm, source_ref, sems.at[CHUNKS + 2]))
    copies.append(pltpu.make_async_copy(input_hbm, input_ref, sems.at[CHUNKS + 3]))
    phases = phase_hbm.at[lax.axis_index("pencil")]
    copies.append(pltpu.make_async_copy(phases, phase_ref, sems.at[CHUNKS + 4]))
    copies.append(pltpu.make_async_copy(table_hbm, table_ref, sems.at[CHUNKS + 5]))
    for copy in copies:
        copy.start()
    copies[0].wait()
    for c in range(C):
        proj_tile_ref[c : c + 1, :] = jnp.full((1, 128), proj_ref[c], F32)

    def add_channel(c, total):
        values = pre_ref[c].astype(F32)
        both = values + values * lax.erf(values * math.sqrt(0.5))
        return total + (0.5 * proj_ref[c]) * both

    total = jnp.zeros((CX, CY, NZ), F32)
    for i in range(CHUNKS):
        copies[1 + i].wait()
        total = lax.fori_loop(i * size, (i + 1) * size, add_channel, total, unroll=2)
    for copy in copies[1 + CHUNKS :]:
        copy.wait()
    field_ref[...] = total

    def edges(refs):
        up_ref, down_ref = refs
        up_ref[0:2] = total[2:4]
        down_ref[0:2] = total[0:2]
        up_ref[2] = coef_ref[3].astype(F32)
        up_ref[3] = source_ref[3].astype(F32)
        down_ref[2] = coef_ref[0].astype(F32)
        down_ref[3] = source_ref[0].astype(F32)

    by_parity(lax.axis_index("slab"), edges, edge_a_ref, edge_b_ref)


def slope_kernel(
    pre_ref,
    proj_ref,
    forward_hbm,
    backward_hbm,
    input_hbm,
    depth_hbm,
    slope_ref,
    forward_ref,
    backward_ref,
    input_ref,
    depth_ref,
    sems,
):
    slab = lax.axis_index("slab")
    copies = [
        pltpu.make_async_copy(forward_hbm.at[slab], forward_ref, sems.at[0]),
        pltpu.make_async_copy(backward_hbm.at[slab], backward_ref, sems.at[1]),
        pltpu.make_async_copy(input_hbm, input_ref, sems.at[2]),
        pltpu.make_async_copy(depth_hbm, depth_ref, sems.at[3]),
    ]
    for copy in copies:
        copy.start()

    def one_channel(c, carry):
        values = pre_ref[c].astype(F32)
        below = 0.5 + 0.5 * lax.erf(values * math.sqrt(0.5))
        bell = jnp.exp(-0.5 * values * values)
        slope = below + values * (bell * (1.0 / math.sqrt(2.0 * math.pi)))
        weight = proj_ref[pl.ds(c, 1), :]
        for x in range(CX):
            for side in range(2):
                piece = slope[x, :, side * 128 : (side + 1) * 128] * weight
                slope_ref[side, pl.ds(x * C + c, CY, stride=Y_PITCH), :] = piece
        return carry

    lax.fori_loop(0, C, one_channel, 0, unroll=2)
    for copy in copies:
        copy.wait()


def nt_dot(left, right):
    return lax.dot_general(left, right, (((1,), (1,)), ((), ())), preferred_element_type=F32)


def tn_dot(left, right):
    return lax.dot_general(left, right, (((0,), (0,)), ((), ())), preferred_element_type=F32)


def pencil_forward(modes_ref, phase_ref, out_refs):
    for half in range(2):
        sums, diffs = [], []
        for part in range(2):
            rows = pl.ds(part * KZ + 8 * half, 8)
            first = [modes_ref[j, rows, :] for j in range(8)]
            second = [modes_ref[15 - j, rows, :] for j in range(8)]
            sums.append([a + b for a, b in zip(first, second)])
            diffs.append([a - b for a, b in zip(first, second)])
        for k in range(17):
            cosines = [math.cos(2.0 * math.pi * k * (7.5 - j) / NY) for j in range(8)]
            sines = [math.sin(2.0 * math.pi * k * (7.5 - j) / NY) for j in range(8)]
            even = [sum(w * v for w, v in zip(cosines, part)) for part in sums]
            w_cos = phase_ref[k : k + 1, :]
            w_sin = phase_ref[17 + k : 18 + k, :]
            if k == 0:
                results = [(0, even[0], even[1], w_sin)]
            else:
                odd = [sum(w * v for w, v in zip(sines, part)) for part in diffs]
                results = [(32 - k, even[0] + odd[1], even[1] - odd[0], -w_sin)]
                if k < 16:
                    results.append((k, even[0] - odd[1], even[1] + odd[0], w_sin))
            for index, real, imag, sin in results:
                row = (index % 2) * 32 + 8 * half
                out_ref = out_refs[index // 2 % 2]
                chip = CHIP_RANK[index // 4]
                out_ref[chip, pl.ds(row, 8), :] = w_cos * real + sin * imag
                out_ref[chip, pl.ds(row + KZ, 8), :] = w_cos * imag - sin * real


def input_kernel(
    phase_ref,
    input_ref,
    table_ref,
    own_ref,
    other_ref,
    rows_ref,
    modes_ref,
):
    for side in range(2):
        for c in range(C):
            piece = input_ref[c, :, :, side * 128 : (side + 1) * 128].astype(F32)
            rows_ref[side, c * PITCH : c * PITCH + CX * CY, :] = piece.reshape(CX * CY, 128)
    for y in range(CY):
        sides = [
            jnp.concatenate(
                [rows_ref[side, pl.ds(x * CY + y, C, stride=PITCH), :] for x in range(CX)], axis=0
            )
            for side in range(2)
        ]
        values = jnp.concatenate(sides, axis=1).astype(BF16)
        both = nt_dot(table_ref[...], values)
        modes_ref[y] = both[:32] + both[32:]
    position = lax.axis_index("pencil")
    forward = functools.partial(pencil_forward, modes_ref, phase_ref)
    by_parity(position, forward, own_ref, other_ref)


def pack_kernel(field_ref, coef_ref, source_ref, got_a_ref, got_b_ref, out_a_ref, out_b_ref):
    def pack(x_refs, y_refs):
        after_ref, before_ref = x_refs
        up_ref, down_ref = y_refs
        for out_ref, first in ((up_ref, 14), (down_ref, 0)):
            cells = slice(first, first + 2)
            cell = slice(15, 16) if first else slice(0, 1)
            for x in range(8):
                if x < 2:
                    rows = before_ref[x, cells, :]
                elif x < 6:
                    rows = field_ref[x - 2, cells, :]
                else:
                    rows = after_ref[x - 6, cells, :]
                out_ref[2 * x : 2 * x + 2, :] = rows
            for base, part, own_ref in ((16, 2, coef_ref), (22, 3, source_ref)):
                for x in range(6):
                    if x == 0:
                        row = before_ref[part, cell, :]
                    elif x == 5:
                        row = after_ref[part, cell, :]
                    else:
                        row = own_ref[x - 1].astype(F32)[cell, :]
                    out_ref[base + x : base + x + 1, :] = row
            out_ref[28:32, :] = jnp.zeros((4, NZ), F32)

    def with_x(x_refs):
        y = lax.axis_index("pencil")
        by_parity(y, functools.partial(pack, x_refs), out_a_ref, out_b_ref)

    by_parity(lax.axis_index("slab"), with_x, got_a_ref, got_b_ref)


def smooth(values):
    values = values + 0.5 * (pltpu.roll(values, 1, 2) + pltpu.roll(values, NZ - 1, 2))
    values = values + 0.5 * (pltpu.roll(values, 1, 1) + pltpu.roll(values, 31, 1))
    return 0.5 * (values[:-2] + values[2:]) + values[1:-1]


def act_parts(slope_ref, grad_ref, y):
    grads = []
    for x in range(CX):
        rows = slice(y * Y_PITCH + x * C, y * Y_PITCH + (x + 1) * C)
        slope = jnp.concatenate([slope_ref[0, rows, :], slope_ref[1, rows, :]], axis=1)
        grads.append(slope * grad_ref[x, 8 + y : 9 + y, :])
    act = jnp.concatenate(grads, axis=0)
    high = act.astype(BF16)
    return high, (act - high.astype(F32)).astype(BF16)


def grad_kernel(
    phase_ref,
    field_ref,
    coef_ref,
    source_ref,
    x_a_ref,
    x_b_ref,
    y_a_ref,
    y_b_ref,
    slope_ref,
    table_ref,
    own_ref,
    other_ref,
    grad_ref,
    wide_field,
    wide_coef,
    wide_source,
    modes_ref,
):
    own = slice(8, 24)
    wide_field[2:6, own, :] = field_ref[...]
    wide_coef[1:5, own, :] = coef_ref[...].astype(F32)
    wide_source[1:5, own, :] = source_ref[...].astype(F32)

    def x_sides(refs):
        after_ref, before_ref = refs
        wide_field[0:2, own, :] = before_ref[0:2]
        wide_field[6:8, own, :] = after_ref[0:2]
        for wide, part in ((wide_coef, 2), (wide_source, 3)):
            wide[0, own, :] = before_ref[part]
            wide[5, own, :] = after_ref[part]

    def y_sides(refs):
        high_ref, low_ref = refs
        for x in range(8):
            wide_field[x, 6:8, :] = low_ref[2 * x : 2 * x + 2, :]
            wide_field[x, 24:26, :] = high_ref[2 * x : 2 * x + 2, :]
        for wide, base in ((wide_coef, 16), (wide_source, 22)):
            for x in range(6):
                wide[x, 7:8, :] = low_ref[base + x : base + x + 1, :]
                wide[x, 24:25, :] = high_ref[base + x : base + x + 1, :]

    by_parity(lax.axis_index("slab"), x_sides, x_a_ref, x_b_ref)
    by_parity(lax.axis_index("pencil"), y_sides, y_a_ref, y_b_ref)
    field = wide_field[...]
    center = field[1:7]
    residual = (16.0 / 3.0 - wide_coef[...]) * center - (2.0 / 3.0) * smooth(field) - wide_source[...]
    grad_ref[...] = (16.0 / 3.0 - wide_coef[1:5]) * residual[1:5] - (2.0 / 3.0) * smooth(residual)
    for y in range(CY):
        high, low = act_parts(slope_ref, grad_ref, y)
        both = nt_dot(table_ref[...], high)
        modes_ref[y] = both[:32] + both[32:] + nt_dot(table_ref[0:32, :], low)
    position = lax.axis_index("pencil")
    forward = functools.partial(pencil_forward, modes_ref, phase_ref)
    by_parity(position, forward, own_ref, other_ref)


def combine_kernel(own_in_ref, got_in_ref, own_ref, got_ref, out_ref):
    out_ref[:, 0:64, :] = own_in_ref[...] + got_in_ref[...]
    out_ref[:, 64:128, :] = own_ref[...] + got_ref[...]


def local_kernel(pointwise_ref, slope_ref, grad_ref, out_ref):
    rows = lax.broadcasted_iota(jnp.int32, (C, LANES), 0)
    lanes = lax.broadcasted_iota(jnp.int32, (C, LANES), 1)
    repeat = jnp.where(lanes % C == rows, 1.0, 0.0).astype(BF16)
    wide = jnp.dot(pointwise_ref[...], repeat, preferred_element_type=F32)
    wide = jnp.concatenate([wide] * CX, axis=0)
    rows = lax.broadcasted_iota(jnp.int32, (LANES, LANES), 0)
    lanes = lax.broadcasted_iota(jnp.int32, (LANES, LANES), 1)
    wide = jnp.where(rows // C == lanes // C, wide, 0.0).astype(BF16)
    wide = jnp.concatenate([wide, wide], axis=1)
    for y in range(CY):
        act = jnp.concatenate(act_parts(slope_ref, grad_ref, y), axis=0)
        out_ref[y] = jnp.dot(wide, act, preferred_element_type=F32)


def slab_forward_kernel(parts_ref, table_ref, out_ref, raw_ref):
    raw = parts_ref[0, 0:64, :]
    for source in range(1, N // 2):
        raw = raw + parts_ref[source, 0:64, :]
    raw_ref[0:64, :] = raw
    raw_ref[64:128, :] = jnp.zeros((64, LANES), F32)
    for kz in range(KZ):
        out_ref[SLAB_RANK[kz], 32:40, :] = raw_ref[pl.ds(kz, 8, stride=KZ), :]
    for ky in range(2):
        for half in range(2):
            pieces = []
            for part in range(2):
                rows = pl.ds(64 + ky * 32 + part * KZ + 8 * half, 8)
                total = parts_ref[0, rows, :]
                for source in range(1, N // 2):
                    total = total + parts_ref[source, rows, :]
                pieces.append([total] + [pltpu.roll(total, 32 * d, 1) for d in range(1, 4)])
            for owner in range(N):
                result = None
                for d in range(4):
                    for part in range(2):
                        row = owner * 8 + d * 2 + part
                        term = pieces[part][d] * table_ref[row : row + 1, :]
                        result = term if result is None else result + term
                out_ref[SLAB_RANK[owner], pl.ds(ky * KZ + 8 * half, 8), :] = result


def flat_modes(block, group):
    lane_group = lax.broadcasted_iota(jnp.int32, (KZ, LANES), 1) // C
    row = lax.broadcasted_iota(jnp.int32, (KZ, LANES), 0)
    picked = jnp.where(lane_group == group, block, 0.0)
    picked = picked + pltpu.roll(picked, 64, 1)
    picked = picked + pltpu.roll(picked, 32, 1)
    tiles = [
        jnp.sum(jnp.where(row == 4 * tile + lane_group, picked, 0.0), axis=0, keepdims=True)
        for tile in range(4)
    ]
    return jnp.concatenate(tiles, axis=1)


def split_3(values):
    high = values.astype(BF16)
    rest = values - high.astype(F32)
    middle = rest.astype(BF16)
    low = (rest - middle.astype(F32)).astype(BF16)
    return high, middle, low


def minus_i(values, even_row):
    return jnp.where(even_row, pltpu.roll(values, 7, 0), -pltpu.roll(values, 1, 0))


def input_modes_at(parts_ref, table_ref):
    row = lax.broadcasted_iota(jnp.int32, (8, LANES), 0)
    group = lax.broadcasted_iota(jnp.int32, (8, LANES), 1) // C
    even_row = row % 2 == 0
    totals = [[None] * 4 for _ in range(4)]
    for source in range(N):
        values = parts_ref[SLAB_RANK[source], 32:40, :]
        turned = minus_i(values, even_row)
        for shift in range(4):
            if shift:
                real, imag = pltpu.roll(values, 32 * shift, 1), pltpu.roll(turned, 32 * shift, 1)
            else:
                real, imag = values, turned
            for q in range(4):
                r = ((q * N + source) * 4 + shift) * 2
                term = real * table_ref[r : r + 1, :] + imag * table_ref[r + 1 : r + 2, :]
                last = totals[q][shift]
                totals[q][shift] = term if last is None else last + term
    lower, upper = [], []
    for q in range(4):
        lower.append(totals[q][0] + totals[q][1] + totals[q][2] + totals[q][3])
        result = None
        for shift in range(4):
            x = (group - shift) % 4
            cos = jnp.where(x == 0, 1.0, jnp.where(x == 2, -1.0, 0.0))
            sin = jnp.where(x == 1, -1.0, jnp.where(x == 3, 1.0, 0.0))
            term = cos * totals[q][shift] + sin * minus_i(totals[q][shift], even_row)
            result = term if result is None else result + term
        upper.append(result)
    return lower + upper


def back_kernel(parts_ref, weight_ref, table_ref, modes_ref, out_ref):
    total = parts_ref[0, 0:32, :]
    for source in range(1, N):
        total = total + parts_ref[source, 0:32, :]
    modes_ref[...] = total
    rows = lax.broadcasted_iota(jnp.int32, (KZ, KZ * C), 0)
    lanes = lax.broadcasted_iota(jnp.int32, (KZ, KZ * C), 1)
    mask = jnp.where(lanes // C == rows, 1.0, 0.0).astype(BF16)
    kz = lax.broadcasted_iota(jnp.int32, (KZ, LANES), 0)
    scale = jnp.where(kz == 0, 1.0 / CELLS, 2.0 / CELLS)
    for ky in range(2):
        block = total[ky * KZ : (ky + 1) * KZ]
        products = []
        for kx in range(2):
            real, imag = flat_modes(block, 2 * kx), flat_modes(block, 2 * kx + 1)
            w_real = weight_ref[0, kx, ky].astype(F32)
            w_imag = weight_ref[1, kx, ky].astype(F32)
            products.append(w_real * real + w_imag * imag)
            products.append(w_real * imag - w_imag * real)
        high, middle, low = split_3(jnp.concatenate(products, axis=0))
        back = scale * (nt_dot(mask, high) + nt_dot(mask, middle) + nt_dot(mask, low))
        for device in range(N):
            out_ref[device, ky * KZ : (ky + 1) * KZ, :] = back
    inputs = input_modes_at(parts_ref, table_ref)
    for device in range(N):
        values = inputs[device // 2]
        if device % 2:
            values = pltpu.roll(values, 64, 1)
        out_ref[SLAB_RANK[device], 32:40, :] = values


def weight_grad_kernel(modes_ref, parts_ref, out_ref):
    rows = lax.broadcasted_iota(jnp.int32, (KZ, KZ * C), 0)
    lanes = lax.broadcasted_iota(jnp.int32, (KZ, KZ * C), 1)
    kz = sum(jnp.where(rows == rank, SLAB_ORDER[rank], 0) for rank in range(N))
    mask = jnp.where(lanes // C == kz, 1.0, 0.0).astype(BF16)
    first = lax.broadcasted_iota(jnp.int32, (1, KZ * C), 1) < C
    scale = jnp.where(first, 1.0 / CELLS, 2.0 / CELLS)
    for ky in range(2):
        grads = modes_ref[ky * KZ : (ky + 1) * KZ, :]
        spread = []
        for part in range(2):
            inputs = parts_ref[pl.ds(32 + 2 * ky + part, KZ, stride=40), :]
            high, middle, low = split_3(inputs)
            spread.append(tn_dot(high, mask) + tn_dot(middle, mask) + tn_dot(low, mask))
        for kx in range(2):
            real = scale * flat_modes(grads, 2 * kx)
            imag = scale * flat_modes(grads, 2 * kx + 1)
            in_real, in_imag = [part[kx * C : (kx + 1) * C] for part in spread]
            out_ref[0, kx, ky] = (in_real * real + in_imag * imag).astype(BF16)
            out_ref[1, kx, ky] = (in_real * imag - in_imag * real).astype(BF16)


def slab_backward_kernel(parts_ref, table_ref, out_ref):
    for ky in range(2):
        for half in range(2):
            totals = [[None] * 4, [None] * 4]
            for source in range(N):
                values = parts_ref[SLAB_RANK[source], pl.ds(ky * KZ + 8 * half, 8), :]
                for d in range(4):
                    for part in range(2):
                        row = source * 8 + d * 2 + part
                        term = values * table_ref[row : row + 1, :]
                        last = totals[part][d]
                        totals[part][d] = term if last is None else last + term
            for part in range(2):
                result = totals[part][0]
                for d in range(1, 4):
                    result = result + pltpu.roll(totals[part][d], 32 * d, 1)
                for device in range(N // 2):
                    out_ref[device, pl.ds(ky * 32 + part * KZ + 8 * half, 8), :] = result


def turn_modes(phase_ref, modes_ref, parts_refs):
    def turned(index, w_cos, w_sin, rows):
        ref = parts_refs[index // 2 % 2]
        row = (index % 2) * 32 + rows
        chip = CHIP_RANK[index // 4]
        real = ref[chip, pl.ds(row, 8), :]
        imag = ref[chip, pl.ds(row + KZ, 8), :]
        return w_cos * real - w_sin * imag, w_cos * imag + w_sin * real

    for half in range(2):
        for k in range(17):
            w_cos = phase_ref[k : k + 1, :]
            w_sin = phase_ref[17 + k : 18 + k, :]
            if k == 0:
                even = turned(0, w_cos, w_sin, 8 * half)
                odd = None
            elif k == 16:
                even = turned(16, w_cos, -w_sin, 8 * half)
                odd = [-part for part in even]
            else:
                plus = turned(k, w_cos, w_sin, 8 * half)
                minus = turned(32 - k, w_cos, -w_sin, 8 * half)
                even = [p + m for p, m in zip(plus, minus)]
                odd = [p - m for p, m in zip(plus, minus)]
            for part in range(2):
                modes_ref[half, 0, k, part] = even[part]
                if odd is not None:
                    modes_ref[half, 1, k, part] = odd[part]


def output_kernel(
    phase_ref,
    own_ref,
    other_ref,
    local_ref,
    table_ref,
    out_ref,
    modes_ref,
    rows_ref,
    flat_ref,
):
    position = lax.axis_index("pencil")
    turn = functools.partial(turn_modes, phase_ref, modes_ref)
    by_parity(position, turn, own_ref, other_ref)
    for half in range(2):
        for y in range(8):
            even = [modes_ref[half, 0, 0, 0], modes_ref[half, 0, 0, 1]]
            odd = [None, None]
            for k in range(1, 17):
                angle = 2.0 * math.pi * k * (y - 7.5) / NY
                cos, sin = math.cos(angle), math.sin(angle)
                for part in range(2):
                    even[part] = even[part] + cos * modes_ref[half, 0, k, part]
                    term = sin * modes_ref[half, 1, k, part]
                    odd[part] = term if odd[part] is None else odd[part] + term
            rows = pl.ds(8 * half, 8)
            more = pl.ds(KZ + 8 * half, 8)
            rows_ref[y, rows, :] = even[0] - odd[1]
            rows_ref[y, more, :] = even[1] + odd[0]
            rows_ref[15 - y, rows, :] = even[0] + odd[1]
            rows_ref[15 - y, more, :] = even[1] - odd[0]
    for y in range(CY):
        values = rows_ref[y]
        high = values.astype(BF16)
        low = (values - high.astype(F32)).astype(BF16)
        stacked = jnp.concatenate([high, low, high], axis=0)
        result = tn_dot(stacked, table_ref[...]) + local_ref[y]
        for x in range(CX):
            for side in range(2):
                piece = result[x * C : (x + 1) * C, side * 128 : (side + 1) * 128]
                flat_ref[side, pl.ds(x * CY + y, C, stride=PITCH), :] = piece
    for side in range(2):
        for c in range(C):
            piece = flat_ref[side, c * PITCH : c * PITCH + CX * CY].astype(BF16)
            out_ref[c, :, :, side * 128 : (side + 1) * 128] = piece.reshape(CX, CY, 128)


def call(kernel, name, out, scratch=(), scalars=(), hbm=(), us=1):
    def run(*args):
        args = [
            pltpu.with_memory_space_constraint(arg, pltpu.HBM) if i in hbm else arg
            for i, arg in enumerate(args)
        ]
        single = not isinstance(out, list)
        specs = [
            pl.BlockSpec(
                memory_space=pltpu.SMEM if i in scalars else pltpu.HBM if i in hbm else pltpu.VMEM
            )
            for i in range(len(args))
        ]
        shapes = [jax.ShapeDtypeStruct(*o) for o in ([out] if single else out)]
        result = pl.pallas_call(
            kernel,
            out_shape=shapes,
            in_specs=specs,
            out_specs=[pl.BlockSpec(memory_space=pltpu.VMEM)] * len(shapes),
            scratch_shapes=[pltpu.VMEM(*s) if isinstance(s, tuple) else s for s in scratch],
            compiler_params=pltpu.CompilerParams(vmem_limit_bytes=VMEM_LIMIT),
            cost_estimate=pl.CostEstimate(
                flops=0, transcendentals=0, bytes_accessed=int(us * BYTES_PER_US)
            ),
            name=name,
        )(*args)
        return result[0] if single else result

    return run


def shards(
    layer_input, pre_activation, coefficient, source, projection, pointwise, spectral_weight
):
    swap = [(i, i ^ 1) for i in range(N)]
    swap_odd = [(i, (i + 1 if i % 2 else i - 1) % N) for i in range(N)]
    same_core = [[2 * chip + core for chip in CHIP_ORDER] for core in range(2)]
    all_slabs = [SLAB_ORDER]
    edge = ((4, CY, NZ), F32)
    (
        field,
        edge_a,
        edge_b,
        pre_activation,
        coefficient,
        source,
        layer_input,
        proj_tile,
        phases,
        depth_forward,
    ) = call(
        field_kernel,
        "field",
        [
            ((CX, CY, NZ), F32),
            edge,
            edge,
            ((C, CX, CY, NZ), BF16),
            ((CX, CY, NZ), BF16),
            ((CX, CY, NZ), BF16),
            ((C, CX, CY, NZ), BF16),
            ((C, 128), F32),
            (PENCIL_PHASES.shape[1:], F32),
            (DEPTH_FORWARD.shape, BF16),
        ],
        scratch=[pltpu.SMEM((C,), F32), pltpu.SemaphoreType.DMA((CHUNKS + 6,))],
        hbm=(0, 1, 2, 3, 4, 5, 6),
        us=4,
    )(
        pre_activation,
        coefficient,
        source,
        projection,
        layer_input,
        jnp.asarray(PENCIL_PHASES),
        jnp.asarray(DEPTH_FORWARD),
    )
    x_a = lax.ppermute(edge_a, "slab", swap)
    x_b = lax.ppermute(edge_b, "slab", swap_odd)
    table = (SLAB_FORWARD.shape[1:], F32)
    slope, slab_forward, slab_backward, input_phases, depth_backward = call(
        slope_kernel,
        "slope",
        [
            ((2, CY * Y_PITCH, 128), F32),
            table,
            table,
            (INPUT_TABLE.shape, F32),
            (DEPTH_BACKWARD.shape, BF16),
        ],
        scratch=[pltpu.SemaphoreType.DMA((4,))],
        hbm=(2, 3, 4, 5),
        us=2,
    )(
        pre_activation,
        proj_tile,
        jnp.asarray(SLAB_FORWARD),
        jnp.asarray(SLAB_BACKWARD),
        jnp.asarray(INPUT_TABLE),
        jnp.asarray(DEPTH_BACKWARD),
    )
    half_modes = ((N // 2, 64, LANES), F32)
    own_in, other_in = call(
        input_kernel,
        "input_modes",
        [half_modes, half_modes],
        scratch=[
            ((2, C * PITCH, 128), F32),
            ((CY, 32, LANES), F32),
        ],
        us=2,
    )(phases, layer_input, depth_forward)
    x_a, x_b, slope, own_in, other_in = lax.optimization_barrier(
        (x_a, x_b, slope, own_in, other_in)
    )
    got_in = lax.ppermute(other_in, "pencil", swap)
    side_a, side_b = call(pack_kernel, "pack", [((32, NZ), F32), ((32, NZ), F32)])(
        field, coefficient, source, x_a, x_b
    )
    y_a = lax.ppermute(side_a, "pencil", swap)
    y_b = lax.ppermute(side_b, "pencil", swap_odd)
    y_a, y_b, got_in = lax.optimization_barrier((y_a, y_b, got_in))
    own, other, grad = call(
        grad_kernel,
        "grad_modes",
        [half_modes, half_modes, ((CX, 32, NZ), F32)],
        scratch=[
            ((8, 32, NZ), F32),
            ((6, 32, NZ), F32),
            ((6, 32, NZ), F32),
            ((CY, 32, LANES), F32),
        ],
        us=3,
    )(
        phases,
        field,
        coefficient,
        source,
        x_a,
        x_b,
        y_a,
        y_b,
        slope,
        depth_forward,
    )
    got = lax.ppermute(other, "pencil", swap)
    local = call(local_kernel, "local", ((CY, LANES, NZ), F32))(pointwise, slope, grad)
    got, local = lax.optimization_barrier((got, local))
    to_pencil = call(combine_kernel, "combine", ((N // 2, 128, LANES), F32))(
        own_in, got_in, own, got
    )
    from_pencil = lax.all_to_all(
        to_pencil, "pencil", 0, 0, axis_index_groups=same_core, tiled=True
    )
    chunks = ((N, 40, LANES), F32)
    to_slab = call(slab_forward_kernel, "slab_forward", chunks, scratch=[((128, LANES), F32)])(
        from_pencil, slab_forward
    )
    from_slab = lax.all_to_all(to_slab, "slab", 0, 0, axis_index_groups=all_slabs, tiled=True)
    modes, to_slab = call(back_kernel, "back", [((32, LANES), F32), chunks])(
        from_slab, spectral_weight, input_phases
    )
    from_slab = lax.all_to_all(to_slab, "slab", 0, 0, axis_index_groups=all_slabs, tiled=True)
    weight_grad = call(weight_grad_kernel, "weight_grad", (spectral_weight.shape, BF16))(
        modes, from_slab.reshape(N * 40, LANES)
    )
    to_pencil = call(slab_backward_kernel, "slab_backward", half_modes)(from_slab, slab_backward)
    own = lax.all_to_all(to_pencil, "pencil", 0, 0, axis_index_groups=same_core, tiled=True)
    other = lax.ppermute(own, "pencil", swap)
    input_grad = call(
        output_kernel,
        "output",
        ((C, CX, CY, NZ), BF16),
        scratch=[
            ((2, 2, 17, 2, 8, LANES), F32),
            ((CY, 32, LANES), F32),
            ((2, C * PITCH, 128), F32),
        ],
    )(phases, own, other, local, depth_backward)
    return (input_grad, weight_grad)


def solution(mesh):
    return jax.shard_map(
        shards,
        mesh=mesh,
        in_specs=(
            P(None, "slab", "pencil", None),
            P(None, "slab", "pencil", None),
            P("slab", "pencil", None),
            P("slab", "pencil", None),
            P(),
            P(),
            P(None, "slab", "pencil", None, None),
        ),
        out_specs=(P(None, "slab", "pencil", None), P(None, "slab", "pencil", None, None)),
        check_vma=False,
    )
```

```python
import functools
import math

import jax
import jax.numpy as jnp
import ml_dtypes
import numpy as np
from jax import lax
from jax.experimental import pallas as pl
from jax.experimental.pallas import tpu as pltpu
from jax.sharding import PartitionSpec as P

F32 = jnp.float32
BF16 = jnp.bfloat16
C, CX, CY, NZ = 32, 4, 16, 256
NX, NY = 64, 256
N = 16
KZ = 16
LANES = CX * C
SLAB_ORDER = [2 * (5 * i % 8) for i in range(8)] + [2 * (3 * i % 8) + 1 for i in range(8)]
SLAB_RANK = [SLAB_ORDER.index(device) for device in range(N)]
CHIP_ORDER = [0, 1, 3, 2, 6, 7, 5, 4]
CHIP_RANK = [CHIP_ORDER.index(chip) for chip in range(N // 2)]
CELLS = float(NX * NY * NZ)
VMEM_LIMIT = 24 * 1024 * 1024
PITCH = 68
Y_PITCH = LANES + 8
CHUNKS = 4
BYTES_PER_US = 3_690_000


def split_2(table):
    high = table.astype(ml_dtypes.bfloat16)
    low = (table - high.astype(np.float64)).astype(ml_dtypes.bfloat16)
    return high, low


def depth_tables():
    angles = 2.0 * math.pi * ((np.arange(KZ)[:, None] * np.arange(NZ)[None, :]) % NZ) / NZ
    table = np.concatenate([np.cos(angles), -np.sin(angles)], axis=0)
    high, low = split_2(table)
    return np.concatenate([high, low], axis=0), np.concatenate([high, high, low], axis=0)


def wave(index):
    return index if index < 16 else index - 32


def pencil_phases():
    position = 16.0 * np.arange(N)[:, None] + 7.5
    angles = 2.0 * math.pi * np.arange(17)[None, :] * position / NY
    rows = np.concatenate([np.cos(angles), np.sin(angles), np.zeros((N, 6))], axis=1)
    return np.repeat(rows[:, :, None], LANES, axis=2).astype(np.float32)


def slab_tables():
    forward = np.zeros((N, N, 4, 2, LANES))
    backward = np.zeros((N, N, 4, 2, LANES))
    for position in range(N):
        for other in range(N):
            for shift in range(4):
                for group in range(4):
                    k = wave(2 * other + group // 2)
                    lanes = slice(group * C, (group + 1) * C)
                    x = 4 * position + (group - shift) % 4
                    angle = 2.0 * math.pi * ((k * x) % NX) / NX
                    cos, sin = math.cos(angle), math.sin(angle)
                    forward[position, other, shift, 0, lanes] = cos if group % 2 == 0 else -sin
                    forward[position, other, shift, 1, lanes] = sin if group % 2 == 0 else cos
                    x = 4 * position + (group + shift) % 4
                    angle = 2.0 * math.pi * ((k * x) % NX) / NX
                    cos, sin = math.cos(angle), math.sin(angle)
                    backward[position, other, shift, 0, lanes] = cos if group % 2 == 0 else -sin
                    backward[position, other, shift, 1, lanes] = sin if group % 2 == 0 else cos
    shape = (N, N * 8, LANES)
    return forward.astype(np.float32).reshape(shape), backward.astype(np.float32).reshape(shape)


def input_table():
    table = np.zeros((4, N, 4, 2, LANES))
    for q in range(4):
        for device in range(N):
            for shift in range(4):
                for group in range(4):
                    other = (group - shift) % 4
                    angle = 2.0 * math.pi * (((4 * q + group) * (4 * device + other)) % NX) / NX
                    lanes = slice(group * C, (group + 1) * C)
                    table[q, device, shift, 0, lanes] = math.cos(angle)
                    table[q, device, shift, 1, lanes] = math.sin(angle)
    return table.astype(np.float32).reshape(-1, LANES)


DEPTH_FORWARD, DEPTH_BACKWARD = depth_tables()
PENCIL_PHASES = pencil_phases()
SLAB_FORWARD, SLAB_BACKWARD = slab_tables()
INPUT_TABLE = input_table()


def by_parity(position, function, first_ref, second_ref):
    @pl.when(position % 2 == 0)
    def _():
        function((first_ref, second_ref))

    @pl.when(position % 2 == 1)
    def _():
        function((second_ref, first_ref))


def field_kernel(
    pre_hbm,
    coef_hbm,
    source_hbm,
    proj_hbm,
    input_hbm,
    phase_hbm,
    table_hbm,
    field_ref,
    edge_a_ref,
    edge_b_ref,
    pre_ref,
    coef_ref,
    source_ref,
    input_ref,
    proj_tile_ref,
    phase_ref,
    table_ref,
    proj_ref,
    sems,
):
    size = C // CHUNKS
    copies = [pltpu.make_async_copy(proj_hbm, proj_ref, sems.at[CHUNKS])]
    for i in range(CHUNKS):
        part = pl.ds(i * size, size)
        copies.append(pltpu.make_async_copy(pre_hbm.at[part], pre_ref.at[part], sems.at[i]))
    copies.append(pltpu.make_async_copy(coef_hbm, coef_ref, sems.at[CHUNKS + 1]))
    copies.append(pltpu.make_async_copy(source_hbm, source_ref, sems.at[CHUNKS + 2]))
    copies.append(pltpu.make_async_copy(input_hbm, input_ref, sems.at[CHUNKS + 3]))
    phases = phase_hbm.at[lax.axis_index("pencil")]
    copies.append(pltpu.make_async_copy(phases, phase_ref, sems.at[CHUNKS + 4]))
    copies.append(pltpu.make_async_copy(table_hbm, table_ref, sems.at[CHUNKS + 5]))
    for copy in copies:
        copy.start()
    copies[0].wait()
    for c in range(C):
        proj_tile_ref[c : c + 1, :] = jnp.full((1, 128), proj_ref[c], F32)

    def add_channel(c, total):
        values = pre_ref[c].astype(F32)
        both = values + values * lax.erf(values * math.sqrt(0.5))
        return total + (0.5 * proj_ref[c]) * both

    total = jnp.zeros((CX, CY, NZ), F32)
    for i in range(CHUNKS):
        copies[1 + i].wait()
        total = lax.fori_loop(i * size, (i + 1) * size, add_channel, total, unroll=2)
    for copy in copies[1 + CHUNKS :]:
        copy.wait()
    field_ref[...] = total

    def edges(refs):
        up_ref, down_ref = refs
        up_ref[0:2] = total[2:4]
        down_ref[0:2] = total[0:2]
        up_ref[2] = coef_ref[3].astype(F32)
        up_ref[3] = source_ref[3].astype(F32)
        down_ref[2] = coef_ref[0].astype(F32)
        down_ref[3] = source_ref[0].astype(F32)

    by_parity(lax.axis_index("slab"), edges, edge_a_ref, edge_b_ref)


def slope_kernel(
    pre_ref,
    proj_ref,
    forward_hbm,
    backward_hbm,
    input_hbm,
    depth_hbm,
    slope_ref,
    forward_ref,
    backward_ref,
    input_ref,
    depth_ref,
    sems,
):
    slab = lax.axis_index("slab")
    copies = [
        pltpu.make_async_copy(forward_hbm.at[slab], forward_ref, sems.at[0]),
        pltpu.make_async_copy(backward_hbm.at[slab], backward_ref, sems.at[1]),
        pltpu.make_async_copy(input_hbm, input_ref, sems.at[2]),
        pltpu.make_async_copy(depth_hbm, depth_ref, sems.at[3]),
    ]
    for copy in copies:
        copy.start()

    def one_channel(c, carry):
        values = pre_ref[c].astype(F32)
        below = 0.5 + 0.5 * lax.erf(values * math.sqrt(0.5))
        bell = jnp.exp(-0.5 * values * values)
        slope = below + values * (bell * (1.0 / math.sqrt(2.0 * math.pi)))
        weight = proj_ref[pl.ds(c, 1), :]
        for x in range(CX):
            for side in range(2):
                piece = slope[x, :, side * 128 : (side + 1) * 128] * weight
                slope_ref[side, pl.ds(x * C + c, CY, stride=Y_PITCH), :] = piece
        return carry

    lax.fori_loop(0, C, one_channel, 0, unroll=2)
    for copy in copies:
        copy.wait()


def nt_dot(left, right):
    return lax.dot_general(left, right, (((1,), (1,)), ((), ())), preferred_element_type=F32)


def tn_dot(left, right):
    return lax.dot_general(left, right, (((0,), (0,)), ((), ())), preferred_element_type=F32)


def pencil_forward(modes_ref, phase_ref, out_refs):
    for half in range(2):
        sums, diffs = [], []
        for part in range(2):
            rows = pl.ds(part * KZ + 8 * half, 8)
            first = [modes_ref[j, rows, :] for j in range(8)]
            second = [modes_ref[15 - j, rows, :] for j in range(8)]
            sums.append([a + b for a, b in zip(first, second)])
            diffs.append([a - b for a, b in zip(first, second)])
        for k in range(17):
            cosines = [math.cos(2.0 * math.pi * k * (7.5 - j) / NY) for j in range(8)]
            sines = [math.sin(2.0 * math.pi * k * (7.5 - j) / NY) for j in range(8)]
            even = [sum(w * v for w, v in zip(cosines, part)) for part in sums]
            w_cos = phase_ref[k : k + 1, :]
            w_sin = phase_ref[17 + k : 18 + k, :]
            if k == 0:
                results = [(0, even[0], even[1], w_sin)]
            else:
                odd = [sum(w * v for w, v in zip(sines, part)) for part in diffs]
                results = [(32 - k, even[0] + odd[1], even[1] - odd[0], -w_sin)]
                if k < 16:
                    results.append((k, even[0] - odd[1], even[1] + odd[0], w_sin))
            for index, real, imag, sin in results:
                row = (index % 2) * 32 + 8 * half
                out_ref = out_refs[index // 2 % 2]
                chip = CHIP_RANK[index // 4]
                out_ref[chip, pl.ds(row, 8), :] = w_cos * real + sin * imag
                out_ref[chip, pl.ds(row + KZ, 8), :] = w_cos * imag - sin * real


def input_kernel(
    phase_ref,
    input_ref,
    table_ref,
    own_ref,
    other_ref,
    rows_ref,
    modes_ref,
):
    for side in range(2):
        for c in range(C):
            piece = input_ref[c, :, :, side * 128 : (side + 1) * 128].astype(F32)
            rows_ref[side, c * PITCH : c * PITCH + CX * CY, :] = piece.reshape(CX * CY, 128)
    for y in range(CY):
        sides = [
            jnp.concatenate(
                [rows_ref[side, pl.ds(x * CY + y, C, stride=PITCH), :] for x in range(CX)], axis=0
            )
            for side in range(2)
        ]
        values = jnp.concatenate(sides, axis=1).astype(BF16)
        both = nt_dot(table_ref[...], values)
        modes_ref[y] = both[:32] + both[32:]
    position = lax.axis_index("pencil")
    forward = functools.partial(pencil_forward, modes_ref, phase_ref)
    by_parity(position, forward, own_ref, other_ref)


def pack_kernel(field_ref, coef_ref, source_ref, got_a_ref, got_b_ref, out_a_ref, out_b_ref):
    def pack(x_refs, y_refs):
        after_ref, before_ref = x_refs
        up_ref, down_ref = y_refs
        for out_ref, first in ((up_ref, 14), (down_ref, 0)):
            cells = slice(first, first + 2)
            cell = slice(15, 16) if first else slice(0, 1)
            for x in range(8):
                if x < 2:
                    rows = before_ref[x, cells, :]
                elif x < 6:
                    rows = field_ref[x - 2, cells, :]
                else:
                    rows = after_ref[x - 6, cells, :]
                out_ref[2 * x : 2 * x + 2, :] = rows
            for base, part, own_ref in ((16, 2, coef_ref), (22, 3, source_ref)):
                for x in range(6):
                    if x == 0:
                        row = before_ref[part, cell, :]
                    elif x == 5:
                        row = after_ref[part, cell, :]
                    else:
                        row = own_ref[x - 1].astype(F32)[cell, :]
                    out_ref[base + x : base + x + 1, :] = row
            out_ref[28:32, :] = jnp.zeros((4, NZ), F32)

    def with_x(x_refs):
        y = lax.axis_index("pencil")
        by_parity(y, functools.partial(pack, x_refs), out_a_ref, out_b_ref)

    by_parity(lax.axis_index("slab"), with_x, got_a_ref, got_b_ref)


def smooth(values):
    values = values + 0.5 * (pltpu.roll(values, 1, 2) + pltpu.roll(values, NZ - 1, 2))
    values = values + 0.5 * (pltpu.roll(values, 1, 1) + pltpu.roll(values, 31, 1))
    return 0.5 * (values[:-2] + values[2:]) + values[1:-1]


def act_parts(slope_ref, grad_ref, y):
    grads = []
    for x in range(CX):
        rows = slice(y * Y_PITCH + x * C, y * Y_PITCH + (x + 1) * C)
        slope = jnp.concatenate([slope_ref[0, rows, :], slope_ref[1, rows, :]], axis=1)
        grads.append(slope * grad_ref[x, 8 + y : 9 + y, :])
    act = jnp.concatenate(grads, axis=0)
    high = act.astype(BF16)
    return high, (act - high.astype(F32)).astype(BF16)


def grad_kernel(
    phase_ref,
    field_ref,
    coef_ref,
    source_ref,
    x_a_ref,
    x_b_ref,
    y_a_ref,
    y_b_ref,
    slope_ref,
    table_ref,
    own_ref,
    other_ref,
    grad_ref,
    wide_field,
    wide_coef,
    wide_source,
    modes_ref,
):
    own = slice(8, 24)
    wide_field[2:6, own, :] = field_ref[...]
    wide_coef[1:5, own, :] = coef_ref[...].astype(F32)
    wide_source[1:5, own, :] = source_ref[...].astype(F32)

    def x_sides(refs):
        after_ref, before_ref = refs
        wide_field[0:2, own, :] = before_ref[0:2]
        wide_field[6:8, own, :] = after_ref[0:2]
        for wide, part in ((wide_coef, 2), (wide_source, 3)):
            wide[0, own, :] = before_ref[part]
            wide[5, own, :] = after_ref[part]

    def y_sides(refs):
        high_ref, low_ref = refs
        for x in range(8):
            wide_field[x, 6:8, :] = low_ref[2 * x : 2 * x + 2, :]
            wide_field[x, 24:26, :] = high_ref[2 * x : 2 * x + 2, :]
        for wide, base in ((wide_coef, 16), (wide_source, 22)):
            for x in range(6):
                wide[x, 7:8, :] = low_ref[base + x : base + x + 1, :]
                wide[x, 24:25, :] = high_ref[base + x : base + x + 1, :]

    by_parity(lax.axis_index("slab"), x_sides, x_a_ref, x_b_ref)
    by_parity(lax.axis_index("pencil"), y_sides, y_a_ref, y_b_ref)
    field = wide_field[...]
    center = field[1:7]
    residual = (16.0 / 3.0 - wide_coef[...]) * center - (2.0 / 3.0) * smooth(field) - wide_source[...]
    grad_ref[...] = (16.0 / 3.0 - wide_coef[1:5]) * residual[1:5] - (2.0 / 3.0) * smooth(residual)
    for y in range(CY):
        high, low = act_parts(slope_ref, grad_ref, y)
        both = nt_dot(table_ref[...], high)
        modes_ref[y] = both[:32] + both[32:] + nt_dot(table_ref[0:32, :], low)
    position = lax.axis_index("pencil")
    forward = functools.partial(pencil_forward, modes_ref, phase_ref)
    by_parity(position, forward, own_ref, other_ref)


def combine_kernel(own_in_ref, got_in_ref, own_ref, got_ref, out_ref):
    out_ref[:, 0:64, :] = own_in_ref[...] + got_in_ref[...]
    out_ref[:, 64:128, :] = own_ref[...] + got_ref[...]


def local_kernel(pointwise_ref, slope_ref, grad_ref, out_ref):
    rows = lax.broadcasted_iota(jnp.int32, (C, LANES), 0)
    lanes = lax.broadcasted_iota(jnp.int32, (C, LANES), 1)
    repeat = jnp.where(lanes % C == rows, 1.0, 0.0).astype(BF16)
    wide = jnp.dot(pointwise_ref[...], repeat, preferred_element_type=F32)
    wide = jnp.concatenate([wide] * CX, axis=0)
    rows = lax.broadcasted_iota(jnp.int32, (LANES, LANES), 0)
    lanes = lax.broadcasted_iota(jnp.int32, (LANES, LANES), 1)
    wide = jnp.where(rows // C == lanes // C, wide, 0.0).astype(BF16)
    wide = jnp.concatenate([wide, wide], axis=1)
    for y in range(CY):
        act = jnp.concatenate(act_parts(slope_ref, grad_ref, y), axis=0)
        out_ref[y] = jnp.dot(wide, act, preferred_element_type=F32)


def slab_forward_kernel(parts_ref, table_ref, out_ref, raw_ref):
    raw = parts_ref[0, 0:64, :]
    for source in range(1, N // 2):
        raw = raw + parts_ref[source, 0:64, :]
    raw_ref[0:64, :] = raw
    raw_ref[64:128, :] = jnp.zeros((64, LANES), F32)
    for kz in range(KZ):
        out_ref[SLAB_RANK[kz], 32:40, :] = raw_ref[pl.ds(kz, 8, stride=KZ), :]
    for ky in range(2):
        for half in range(2):
            pieces = []
            for part in range(2):
                rows = pl.ds(64 + ky * 32 + part * KZ + 8 * half, 8)
                total = parts_ref[0, rows, :]
                for source in range(1, N // 2):
                    total = total + parts_ref[source, rows, :]
                pieces.append([total] + [pltpu.roll(total, 32 * d, 1) for d in range(1, 4)])
            for owner in range(N):
                result = None
                for d in range(4):
                    for part in range(2):
                        row = owner * 8 + d * 2 + part
                        term = pieces[part][d] * table_ref[row : row + 1, :]
                        result = term if result is None else result + term
                out_ref[SLAB_RANK[owner], pl.ds(ky * KZ + 8 * half, 8), :] = result


def flat_modes(block, group):
    lane_group = lax.broadcasted_iota(jnp.int32, (KZ, LANES), 1) // C
    row = lax.broadcasted_iota(jnp.int32, (KZ, LANES), 0)
    picked = jnp.where(lane_group == group, block, 0.0)
    picked = picked + pltpu.roll(picked, 64, 1)
    picked = picked + pltpu.roll(picked, 32, 1)
    tiles = [
        jnp.sum(jnp.where(row == 4 * tile + lane_group, picked, 0.0), axis=0, keepdims=True)
        for tile in range(4)
    ]
    return jnp.concatenate(tiles, axis=1)


def split_3(values):
    high = values.astype(BF16)
    rest = values - high.astype(F32)
    middle = rest.astype(BF16)
    low = (rest - middle.astype(F32)).astype(BF16)
    return high, middle, low


def minus_i(values, even_row):
    return jnp.where(even_row, pltpu.roll(values, 7, 0), -pltpu.roll(values, 1, 0))


def input_modes_at(parts_ref, table_ref):
    row = lax.broadcasted_iota(jnp.int32, (8, LANES), 0)
    group = lax.broadcasted_iota(jnp.int32, (8, LANES), 1) // C
    even_row = row % 2 == 0
    totals = [[None] * 4 for _ in range(4)]
    for source in range(N):
        values = parts_ref[SLAB_RANK[source], 32:40, :]
        turned = minus_i(values, even_row)
        for shift in range(4):
            if shift:
                real, imag = pltpu.roll(values, 32 * shift, 1), pltpu.roll(turned, 32 * shift, 1)
            else:
                real, imag = values, turned
            for q in range(4):
                r = ((q * N + source) * 4 + shift) * 2
                term = real * table_ref[r : r + 1, :] + imag * table_ref[r + 1 : r + 2, :]
                last = totals[q][shift]
                totals[q][shift] = term if last is None else last + term
    lower, upper = [], []
    for q in range(4):
        lower.append(totals[q][0] + totals[q][1] + totals[q][2] + totals[q][3])
        result = None
        for shift in range(4):
            x = (group - shift) % 4
            cos = jnp.where(x == 0, 1.0, jnp.where(x == 2, -1.0, 0.0))
            sin = jnp.where(x == 1, -1.0, jnp.where(x == 3, 1.0, 0.0))
            term = cos * totals[q][shift] + sin * minus_i(totals[q][shift], even_row)
            result = term if result is None else result + term
        upper.append(result)
    return lower + upper


def back_kernel(parts_ref, weight_ref, table_ref, modes_ref, out_ref):
    total = parts_ref[0, 0:32, :]
    for source in range(1, N):
        total = total + parts_ref[source, 0:32, :]
    modes_ref[...] = total
    rows = lax.broadcasted_iota(jnp.int32, (KZ, KZ * C), 0)
    lanes = lax.broadcasted_iota(jnp.int32, (KZ, KZ * C), 1)
    mask = jnp.where(lanes // C == rows, 1.0, 0.0).astype(BF16)
    kz = lax.broadcasted_iota(jnp.int32, (KZ, LANES), 0)
    scale = jnp.where(kz == 0, 1.0 / CELLS, 2.0 / CELLS)
    for ky in range(2):
        block = total[ky * KZ : (ky + 1) * KZ]
        products = []
        for kx in range(2):
            real, imag = flat_modes(block, 2 * kx), flat_modes(block, 2 * kx + 1)
            w_real = weight_ref[0, kx, ky].astype(F32)
            w_imag = weight_ref[1, kx, ky].astype(F32)
            products.append(w_real * real + w_imag * imag)
            products.append(w_real * imag - w_imag * real)
        high, middle, low = split_3(jnp.concatenate(products, axis=0))
        back = scale * (nt_dot(mask, high) + nt_dot(mask, middle) + nt_dot(mask, low))
        for device in range(N):
            out_ref[device, ky * KZ : (ky + 1) * KZ, :] = back
    inputs = input_modes_at(parts_ref, table_ref)
    for device in range(N):
        values = inputs[device // 2]
        if device % 2:
            values = pltpu.roll(values, 64, 1)
        out_ref[SLAB_RANK[device], 32:40, :] = values


def weight_grad_kernel(modes_ref, parts_ref, out_ref):
    rows = lax.broadcasted_iota(jnp.int32, (KZ, KZ * C), 0)
    lanes = lax.broadcasted_iota(jnp.int32, (KZ, KZ * C), 1)
    kz = sum(jnp.where(rows == rank, SLAB_ORDER[rank], 0) for rank in range(N))
    mask = jnp.where(lanes // C == kz, 1.0, 0.0).astype(BF16)
    first = lax.broadcasted_iota(jnp.int32, (1, KZ * C), 1) < C
    scale = jnp.where(first, 1.0 / CELLS, 2.0 / CELLS)
    for ky in range(2):
        grads = modes_ref[ky * KZ : (ky + 1) * KZ, :]
        spread = []
        for part in range(2):
            inputs = parts_ref[pl.ds(32 + 2 * ky + part, KZ, stride=40), :]
            high, middle, low = split_3(inputs)
            spread.append(tn_dot(high, mask) + tn_dot(middle, mask) + tn_dot(low, mask))
        for kx in range(2):
            real = scale * flat_modes(grads, 2 * kx)
            imag = scale * flat_modes(grads, 2 * kx + 1)
            in_real, in_imag = [part[kx * C : (kx + 1) * C] for part in spread]
            out_ref[0, kx, ky] = (in_real * real + in_imag * imag).astype(BF16)
            out_ref[1, kx, ky] = (in_real * imag - in_imag * real).astype(BF16)


def slab_backward_kernel(parts_ref, table_ref, out_ref):
    for ky in range(2):
        for half in range(2):
            totals = [[None] * 4, [None] * 4]
            for source in range(N):
                values = parts_ref[SLAB_RANK[source], pl.ds(ky * KZ + 8 * half, 8), :]
                for d in range(4):
                    for part in range(2):
                        row = source * 8 + d * 2 + part
                        term = values * table_ref[row : row + 1, :]
                        last = totals[part][d]
                        totals[part][d] = term if last is None else last + term
            for part in range(2):
                result = totals[part][0]
                for d in range(1, 4):
                    result = result + pltpu.roll(totals[part][d], 32 * d, 1)
                for device in range(N // 2):
                    out_ref[device, pl.ds(ky * 32 + part * KZ + 8 * half, 8), :] = result


def turn_modes(phase_ref, modes_ref, parts_refs):
    def turned(index, w_cos, w_sin, rows):
        ref = parts_refs[index // 2 % 2]
        row = (index % 2) * 32 + rows
        chip = CHIP_RANK[index // 4]
        real = ref[chip, pl.ds(row, 8), :]
        imag = ref[chip, pl.ds(row + KZ, 8), :]
        return w_cos * real - w_sin * imag, w_cos * imag + w_sin * real

    for half in range(2):
        for k in range(17):
            w_cos = phase_ref[k : k + 1, :]
            w_sin = phase_ref[17 + k : 18 + k, :]
            if k == 0:
                even = turned(0, w_cos, w_sin, 8 * half)
                odd = None
            elif k == 16:
                even = turned(16, w_cos, -w_sin, 8 * half)
                odd = [-part for part in even]
            else:
                plus = turned(k, w_cos, w_sin, 8 * half)
                minus = turned(32 - k, w_cos, -w_sin, 8 * half)
                even = [p + m for p, m in zip(plus, minus)]
                odd = [p - m for p, m in zip(plus, minus)]
            for part in range(2):
                modes_ref[half, 0, k, part] = even[part]
                if odd is not None:
                    modes_ref[half, 1, k, part] = odd[part]


def output_kernel(
    phase_ref,
    own_ref,
    other_ref,
    local_ref,
    table_ref,
    out_ref,
    modes_ref,
    rows_ref,
    flat_ref,
):
    position = lax.axis_index("pencil")
    turn = functools.partial(turn_modes, phase_ref, modes_ref)
    by_parity(position, turn, own_ref, other_ref)
    for half in range(2):
        for y in range(8):
            even = [modes_ref[half, 0, 0, 0], modes_ref[half, 0, 0, 1]]
            odd = [None, None]
            for k in range(1, 17):
                angle = 2.0 * math.pi * k * (y - 7.5) / NY
                cos, sin = math.cos(angle), math.sin(angle)
                for part in range(2):
                    even[part] = even[part] + cos * modes_ref[half, 0, k, part]
                    term = sin * modes_ref[half, 1, k, part]
                    odd[part] = term if odd[part] is None else odd[part] + term
            rows = pl.ds(8 * half, 8)
            more = pl.ds(KZ + 8 * half, 8)
            rows_ref[y, rows, :] = even[0] - odd[1]
            rows_ref[y, more, :] = even[1] + odd[0]
            rows_ref[15 - y, rows, :] = even[0] + odd[1]
            rows_ref[15 - y, more, :] = even[1] - odd[0]
    for y in range(CY):
        values = rows_ref[y]
        high = values.astype(BF16)
        low = (values - high.astype(F32)).astype(BF16)
        stacked = jnp.concatenate([high, low, high], axis=0)
        result = tn_dot(stacked, table_ref[...]) + local_ref[y]
        for x in range(CX):
            for side in range(2):
                piece = result[x * C : (x + 1) * C, side * 128 : (side + 1) * 128]
                flat_ref[side, pl.ds(x * CY + y, C, stride=PITCH), :] = piece
    for side in range(2):
        for c in range(C):
            piece = flat_ref[side, c * PITCH : c * PITCH + CX * CY].astype(BF16)
            out_ref[c, :, :, side * 128 : (side + 1) * 128] = piece.reshape(CX, CY, 128)


def call(kernel, name, out, scratch=(), scalars=(), hbm=(), us=1):
    def run(*args):
        args = [
            pltpu.with_memory_space_constraint(arg, pltpu.HBM) if i in hbm else arg
            for i, arg in enumerate(args)
        ]
        single = not isinstance(out, list)
        specs = [
            pl.BlockSpec(
                memory_space=pltpu.SMEM if i in scalars else pltpu.HBM if i in hbm else pltpu.VMEM
            )
            for i in range(len(args))
        ]
        shapes = [jax.ShapeDtypeStruct(*o) for o in ([out] if single else out)]
        result = pl.pallas_call(
            kernel,
            out_shape=shapes,
            in_specs=specs,
            out_specs=[pl.BlockSpec(memory_space=pltpu.VMEM)] * len(shapes),
            scratch_shapes=[pltpu.VMEM(*s) if isinstance(s, tuple) else s for s in scratch],
            compiler_params=pltpu.CompilerParams(vmem_limit_bytes=VMEM_LIMIT),
            cost_estimate=pl.CostEstimate(
                flops=0, transcendentals=0, bytes_accessed=int(us * BYTES_PER_US)
            ),
            name=name,
        )(*args)
        return result[0] if single else result

    return run


def shards(
    layer_input, pre_activation, coefficient, source, projection, pointwise, spectral_weight
):
    swap = [(i, i ^ 1) for i in range(N)]
    swap_odd = [(i, (i + 1 if i % 2 else i - 1) % N) for i in range(N)]
    same_core = [[2 * chip + core for chip in CHIP_ORDER] for core in range(2)]
    all_slabs = [SLAB_ORDER]
    edge = ((4, CY, NZ), F32)
    (
        field,
        edge_a,
        edge_b,
        pre_activation,
        coefficient,
        source,
        layer_input,
        proj_tile,
        phases,
        depth_forward,
    ) = call(
        field_kernel,
        "field",
        [
            ((CX, CY, NZ), F32),
            edge,
            edge,
            ((C, CX, CY, NZ), BF16),
            ((CX, CY, NZ), BF16),
            ((CX, CY, NZ), BF16),
            ((C, CX, CY, NZ), BF16),
            ((C, 128), F32),
            (PENCIL_PHASES.shape[1:], F32),
            (DEPTH_FORWARD.shape, BF16),
        ],
        scratch=[pltpu.SMEM((C,), F32), pltpu.SemaphoreType.DMA((CHUNKS + 6,))],
        hbm=(0, 1, 2, 3, 4, 5, 6),
        us=4,
    )(
        pre_activation,
        coefficient,
        source,
        projection,
        layer_input,
        jnp.asarray(PENCIL_PHASES),
        jnp.asarray(DEPTH_FORWARD),
    )
    x_a = lax.ppermute(edge_a, "slab", swap)
    x_b = lax.ppermute(edge_b, "slab", swap_odd)
    table = (SLAB_FORWARD.shape[1:], F32)
    slope, slab_forward, slab_backward, input_phases, depth_backward = call(
        slope_kernel,
        "slope",
        [
            ((2, CY * Y_PITCH, 128), F32),
            table,
            table,
            (INPUT_TABLE.shape, F32),
            (DEPTH_BACKWARD.shape, BF16),
        ],
        scratch=[pltpu.SemaphoreType.DMA((4,))],
        hbm=(2, 3, 4, 5),
        us=2,
    )(
        pre_activation,
        proj_tile,
        jnp.asarray(SLAB_FORWARD),
        jnp.asarray(SLAB_BACKWARD),
        jnp.asarray(INPUT_TABLE),
        jnp.asarray(DEPTH_BACKWARD),
    )
    half_modes = ((N // 2, 64, LANES), F32)
    own_in, other_in = call(
        input_kernel,
        "input_modes",
        [half_modes, half_modes],
        scratch=[
            ((2, C * PITCH, 128), F32),
            ((CY, 32, LANES), F32),
        ],
        us=2,
    )(phases, layer_input, depth_forward)
    x_a, x_b, slope, own_in, other_in = lax.optimization_barrier(
        (x_a, x_b, slope, own_in, other_in)
    )
    got_in = lax.ppermute(other_in, "pencil", swap)
    side_a, side_b = call(pack_kernel, "pack", [((32, NZ), F32), ((32, NZ), F32)])(
        field, coefficient, source, x_a, x_b
    )
    y_a = lax.ppermute(side_a, "pencil", swap)
    y_b = lax.ppermute(side_b, "pencil", swap_odd)
    y_a, y_b, got_in = lax.optimization_barrier((y_a, y_b, got_in))
    own, other, grad = call(
        grad_kernel,
        "grad_modes",
        [half_modes, half_modes, ((CX, 32, NZ), F32)],
        scratch=[
            ((8, 32, NZ), F32),
            ((6, 32, NZ), F32),
            ((6, 32, NZ), F32),
            ((CY, 32, LANES), F32),
        ],
        us=3,
    )(
        phases,
        field,
        coefficient,
        source,
        x_a,
        x_b,
        y_a,
        y_b,
        slope,
        depth_forward,
    )
    got = lax.ppermute(other, "pencil", swap)
    local = call(local_kernel, "local", ((CY, LANES, NZ), F32))(pointwise, slope, grad)
    got, local = lax.optimization_barrier((got, local))
    to_pencil = call(combine_kernel, "combine", ((N // 2, 128, LANES), F32))(
        own_in, got_in, own, got
    )
    from_pencil = lax.all_to_all(
        to_pencil, "pencil", 0, 0, axis_index_groups=same_core, tiled=True
    )
    chunks = ((N, 40, LANES), F32)
    to_slab = call(slab_forward_kernel, "slab_forward", chunks, scratch=[((128, LANES), F32)])(
        from_pencil, slab_forward
    )
    from_slab = lax.all_to_all(to_slab, "slab", 0, 0, axis_index_groups=all_slabs, tiled=True)
    modes, to_slab = call(back_kernel, "back", [((32, LANES), F32), chunks])(
        from_slab, spectral_weight, input_phases
    )
    from_slab = lax.all_to_all(to_slab, "slab", 0, 0, axis_index_groups=all_slabs, tiled=True)
    weight_grad = call(weight_grad_kernel, "weight_grad", (spectral_weight.shape, BF16))(
        modes, from_slab.reshape(N * 40, LANES)
    )
    to_pencil = call(slab_backward_kernel, "slab_backward", half_modes)(from_slab, slab_backward)
    own = lax.all_to_all(to_pencil, "pencil", 0, 0, axis_index_groups=same_core, tiled=True)
    other = lax.ppermute(own, "pencil", swap)
    input_grad = call(
        output_kernel,
        "output",
        ((C, CX, CY, NZ), BF16),
        scratch=[
            ((2, 2, 17, 2, 8, LANES), F32),
            ((CY, 32, LANES), F32),
            ((2, C * PITCH, 128), F32),
        ],
    )(phases, own, other, local, depth_backward)
    return (input_grad, weight_grad)


def solution(mesh):
    return jax.shard_map(
        shards,
        mesh=mesh,
        in_specs=(
            P(None, "slab", "pencil", None),
            P(None, "slab", "pencil", None),
            P("slab", "pencil", None),
            P("slab", "pencil", None),
            P(),
            P(),
            P(None, "slab", "pencil", None, None),
        ),
        out_specs=(P(None, "slab", "pencil", None), P(None, "slab", "pencil", None, None)),
        check_vma=False,
    )
```

```python
import functools
import math

import jax
import jax.numpy as jnp
import ml_dtypes
import numpy as np
from jax import lax
from jax.experimental import pallas as pl
from jax.experimental.pallas import tpu as pltpu
from jax.sharding import PartitionSpec as P

F32 = jnp.float32
BF16 = jnp.bfloat16
C, CX, CY, NZ = 32, 4, 16, 256
NX, NY = 64, 256
N = 16
KZ = 16
LANES = CX * C
SLAB_ORDER = [2 * (5 * i % 8) for i in range(8)] + [2 * (3 * i % 8) + 1 for i in range(8)]
SLAB_RANK = [SLAB_ORDER.index(device) for device in range(N)]
CHIP_ORDER = [0, 1, 3, 2, 6, 7, 5, 4]
CHIP_RANK = [CHIP_ORDER.index(chip) for chip in range(N // 2)]
CELLS = float(NX * NY * NZ)
VMEM_LIMIT = 24 * 1024 * 1024
PITCH = 68
Y_PITCH = LANES + 8
CHUNKS = 8
BYTES_PER_US = 3_690_000


def split_2(table):
    high = table.astype(ml_dtypes.bfloat16)
    low = (table - high.astype(np.float64)).astype(ml_dtypes.bfloat16)
    return high, low


def depth_tables():
    angles = 2.0 * math.pi * ((np.arange(KZ)[:, None] * np.arange(NZ)[None, :]) % NZ) / NZ
    table = np.concatenate([np.cos(angles), -np.sin(angles)], axis=0)
    high, low = split_2(table)
    return np.concatenate([high, low], axis=0), np.concatenate([high, high, low], axis=0)


def wave(index):
    return index if index < 16 else index - 32


def pencil_phases():
    position = 16.0 * np.arange(N)[:, None] + 7.5
    angles = 2.0 * math.pi * np.arange(17)[None, :] * position / NY
    rows = np.concatenate([np.cos(angles), np.sin(angles), np.zeros((N, 6))], axis=1)
    return np.repeat(rows[:, :, None], LANES, axis=2).astype(np.float32)


def slab_tables():
    forward = np.zeros((N, N, 4, 2, LANES))
    backward = np.zeros((N, N, 4, 2, LANES))
    for position in range(N):
        for other in range(N):
            for shift in range(4):
                for group in range(4):
                    k = wave(2 * other + group // 2)
                    lanes = slice(group * C, (group + 1) * C)
                    x = 4 * position + (group - shift) % 4
                    angle = 2.0 * math.pi * ((k * x) % NX) / NX
                    cos, sin = math.cos(angle), math.sin(angle)
                    forward[position, other, shift, 0, lanes] = cos if group % 2 == 0 else -sin
                    forward[position, other, shift, 1, lanes] = sin if group % 2 == 0 else cos
                    x = 4 * position + (group + shift) % 4
                    angle = 2.0 * math.pi * ((k * x) % NX) / NX
                    cos, sin = math.cos(angle), math.sin(angle)
                    backward[position, other, shift, 0, lanes] = cos if group % 2 == 0 else -sin
                    backward[position, other, shift, 1, lanes] = sin if group % 2 == 0 else cos
    shape = (N, N * 8, LANES)
    return forward.astype(np.float32).reshape(shape), backward.astype(np.float32).reshape(shape)


def input_table():
    table = np.zeros((4, N, 4, 2, LANES))
    for q in range(4):
        for device in range(N):
            for shift in range(4):
                for group in range(4):
                    other = (group - shift) % 4
                    angle = 2.0 * math.pi * (((4 * q + group) * (4 * device + other)) % NX) / NX
                    lanes = slice(group * C, (group + 1) * C)
                    table[q, device, shift, 0, lanes] = math.cos(angle)
                    table[q, device, shift, 1, lanes] = math.sin(angle)
    return table.astype(np.float32).reshape(-1, LANES)


DEPTH_FORWARD, DEPTH_BACKWARD = depth_tables()
PENCIL_PHASES = pencil_phases()
SLAB_FORWARD, SLAB_BACKWARD = slab_tables()
INPUT_TABLE = input_table()


def by_parity(position, function, first_ref, second_ref):
    @pl.when(position % 2 == 0)
    def _():
        function((first_ref, second_ref))

    @pl.when(position % 2 == 1)
    def _():
        function((second_ref, first_ref))


def field_kernel(
    pre_hbm,
    coef_hbm,
    source_hbm,
    proj_hbm,
    phase_hbm,
    table_hbm,
    field_ref,
    edge_a_ref,
    edge_b_ref,
    pre_ref,
    coef_ref,
    source_ref,
    proj_tile_ref,
    phase_ref,
    table_ref,
    proj_ref,
    sems,
):
    size = C // CHUNKS
    copies = [pltpu.make_async_copy(proj_hbm, proj_ref, sems.at[CHUNKS])]
    for i in range(CHUNKS):
        part = pl.ds(i * size, size)
        copies.append(pltpu.make_async_copy(pre_hbm.at[part], pre_ref.at[part], sems.at[i]))
    copies.append(pltpu.make_async_copy(coef_hbm, coef_ref, sems.at[CHUNKS + 1]))
    copies.append(pltpu.make_async_copy(source_hbm, source_ref, sems.at[CHUNKS + 2]))
    phases = phase_hbm.at[lax.axis_index("pencil")]
    copies.append(pltpu.make_async_copy(phases, phase_ref, sems.at[CHUNKS + 3]))
    copies.append(pltpu.make_async_copy(table_hbm, table_ref, sems.at[CHUNKS + 4]))
    for copy in copies:
        copy.start()
    copies[0].wait()
    for c in range(C):
        proj_tile_ref[c : c + 1, :] = jnp.full((1, 128), proj_ref[c], F32)

    def add_channel(c, total):
        values = pre_ref[c].astype(F32)
        both = values + values * lax.erf(values * math.sqrt(0.5))
        return total + (0.5 * proj_ref[c]) * both

    total = jnp.zeros((CX, CY, NZ), F32)
    for i in range(CHUNKS):
        copies[1 + i].wait()
        total = lax.fori_loop(i * size, (i + 1) * size, add_channel, total, unroll=2)
    for copy in copies[1 + CHUNKS :]:
        copy.wait()
    field_ref[...] = total

    def edges(refs):
        up_ref, down_ref = refs
        up_ref[0:2] = total[2:4]
        down_ref[0:2] = total[0:2]
        up_ref[2] = coef_ref[3].astype(F32)
        up_ref[3] = source_ref[3].astype(F32)
        down_ref[2] = coef_ref[0].astype(F32)
        down_ref[3] = source_ref[0].astype(F32)

    by_parity(lax.axis_index("slab"), edges, edge_a_ref, edge_b_ref)


def slope_kernel(
    pre_ref,
    proj_ref,
    forward_hbm,
    backward_hbm,
    input_hbm,
    depth_hbm,
    slope_ref,
    forward_ref,
    backward_ref,
    input_ref,
    depth_ref,
    sems,
):
    slab = lax.axis_index("slab")
    copies = [
        pltpu.make_async_copy(forward_hbm.at[slab], forward_ref, sems.at[0]),
        pltpu.make_async_copy(backward_hbm.at[slab], backward_ref, sems.at[1]),
        pltpu.make_async_copy(input_hbm, input_ref, sems.at[2]),
        pltpu.make_async_copy(depth_hbm, depth_ref, sems.at[3]),
    ]
    for copy in copies:
        copy.start()

    def one_channel(c, carry):
        values = pre_ref[c].astype(F32)
        below = 0.5 + 0.5 * lax.erf(values * math.sqrt(0.5))
        bell = jnp.exp(-0.5 * values * values)
        slope = below + values * (bell * (1.0 / math.sqrt(2.0 * math.pi)))
        weight = proj_ref[pl.ds(c, 1), :]
        for x in range(CX):
            for side in range(2):
                piece = slope[x, :, side * 128 : (side + 1) * 128] * weight
                slope_ref[side, pl.ds(x * C + c, CY, stride=Y_PITCH), :] = piece
        return carry

    lax.fori_loop(0, C, one_channel, 0, unroll=2)
    for copy in copies:
        copy.wait()


def nt_dot(left, right):
    return lax.dot_general(left, right, (((1,), (1,)), ((), ())), preferred_element_type=F32)


def tn_dot(left, right):
    return lax.dot_general(left, right, (((0,), (0,)), ((), ())), preferred_element_type=F32)


def pencil_forward(modes_ref, phase_ref, out_refs):
    for half in range(2):
        sums, diffs = [], []
        for part in range(2):
            rows = pl.ds(part * KZ + 8 * half, 8)
            first = [modes_ref[j, rows, :] for j in range(8)]
            second = [modes_ref[15 - j, rows, :] for j in range(8)]
            sums.append([a + b for a, b in zip(first, second)])
            diffs.append([a - b for a, b in zip(first, second)])
        for k in range(17):
            cosines = [math.cos(2.0 * math.pi * k * (7.5 - j) / NY) for j in range(8)]
            sines = [math.sin(2.0 * math.pi * k * (7.5 - j) / NY) for j in range(8)]
            even = [sum(w * v for w, v in zip(cosines, part)) for part in sums]
            w_cos = phase_ref[k : k + 1, :]
            w_sin = phase_ref[17 + k : 18 + k, :]
            if k == 0:
                results = [(0, even[0], even[1], w_sin)]
            else:
                odd = [sum(w * v for w, v in zip(sines, part)) for part in diffs]
                results = [(32 - k, even[0] + odd[1], even[1] - odd[0], -w_sin)]
                if k < 16:
                    results.append((k, even[0] - odd[1], even[1] + odd[0], w_sin))
            for index, real, imag, sin in results:
                row = (index % 2) * 32 + 8 * half
                out_ref = out_refs[index // 2 % 2]
                chip = CHIP_RANK[index // 4]
                out_ref[chip, pl.ds(row, 8), :] = w_cos * real + sin * imag
                out_ref[chip, pl.ds(row + KZ, 8), :] = w_cos * imag - sin * real


def input_kernel(
    phase_ref,
    input_ref,
    table_ref,
    own_ref,
    other_ref,
    rows_ref,
    modes_ref,
):
    for side in range(2):
        for c in range(C):
            piece = input_ref[c, :, :, side * 128 : (side + 1) * 128].astype(F32)
            rows_ref[side, c * PITCH : c * PITCH + CX * CY, :] = piece.reshape(CX * CY, 128)
    for y in range(CY):
        sides = [
            jnp.concatenate(
                [rows_ref[side, pl.ds(x * CY + y, C, stride=PITCH), :] for x in range(CX)], axis=0
            )
            for side in range(2)
        ]
        values = jnp.concatenate(sides, axis=1).astype(BF16)
        both = nt_dot(table_ref[...], values)
        modes_ref[y] = both[:32] + both[32:]
    position = lax.axis_index("pencil")
    forward = functools.partial(pencil_forward, modes_ref, phase_ref)
    by_parity(position, forward, own_ref, other_ref)


def pack_kernel(field_ref, coef_ref, source_ref, got_a_ref, got_b_ref, out_a_ref, out_b_ref):
    def pack(x_refs, y_refs):
        after_ref, before_ref = x_refs
        up_ref, down_ref = y_refs
        for out_ref, first in ((up_ref, 14), (down_ref, 0)):
            cells = slice(first, first + 2)
            cell = slice(15, 16) if first else slice(0, 1)
            for x in range(8):
                if x < 2:
                    rows = before_ref[x, cells, :]
                elif x < 6:
                    rows = field_ref[x - 2, cells, :]
                else:
                    rows = after_ref[x - 6, cells, :]
                out_ref[2 * x : 2 * x + 2, :] = rows
            for base, part, own_ref in ((16, 2, coef_ref), (22, 3, source_ref)):
                for x in range(6):
                    if x == 0:
                        row = before_ref[part, cell, :]
                    elif x == 5:
                        row = after_ref[part, cell, :]
                    else:
                        row = own_ref[x - 1].astype(F32)[cell, :]
                    out_ref[base + x : base + x + 1, :] = row
            out_ref[28:32, :] = jnp.zeros((4, NZ), F32)

    def with_x(x_refs):
        y = lax.axis_index("pencil")
        by_parity(y, functools.partial(pack, x_refs), out_a_ref, out_b_ref)

    by_parity(lax.axis_index("slab"), with_x, got_a_ref, got_b_ref)


def smooth(values):
    values = values + 0.5 * (pltpu.roll(values, 1, 2) + pltpu.roll(values, NZ - 1, 2))
    values = values + 0.5 * (pltpu.roll(values, 1, 1) + pltpu.roll(values, 31, 1))
    return 0.5 * (values[:-2] + values[2:]) + values[1:-1]


def act_parts(slope_ref, grad_ref, y):
    grads = []
    for x in range(CX):
        rows = slice(y * Y_PITCH + x * C, y * Y_PITCH + (x + 1) * C)
        slope = jnp.concatenate([slope_ref[0, rows, :], slope_ref[1, rows, :]], axis=1)
        grads.append(slope * grad_ref[x, 8 + y : 9 + y, :])
    act = jnp.concatenate(grads, axis=0)
    high = act.astype(BF16)
    return high, (act - high.astype(F32)).astype(BF16)


def grad_kernel(
    phase_ref,
    field_ref,
    coef_ref,
    source_ref,
    x_a_ref,
    x_b_ref,
    y_a_ref,
    y_b_ref,
    slope_ref,
    table_ref,
    own_ref,
    other_ref,
    grad_ref,
    wide_field,
    wide_coef,
    wide_source,
    modes_ref,
):
    own = slice(8, 24)
    wide_field[2:6, own, :] = field_ref[...]
    wide_coef[1:5, own, :] = coef_ref[...].astype(F32)
    wide_source[1:5, own, :] = source_ref[...].astype(F32)

    def x_sides(refs):
        after_ref, before_ref = refs
        wide_field[0:2, own, :] = before_ref[0:2]
        wide_field[6:8, own, :] = after_ref[0:2]
        for wide, part in ((wide_coef, 2), (wide_source, 3)):
            wide[0, own, :] = before_ref[part]
            wide[5, own, :] = after_ref[part]

    def y_sides(refs):
        high_ref, low_ref = refs
        for x in range(8):
            wide_field[x, 6:8, :] = low_ref[2 * x : 2 * x + 2, :]
            wide_field[x, 24:26, :] = high_ref[2 * x : 2 * x + 2, :]
        for wide, base in ((wide_coef, 16), (wide_source, 22)):
            for x in range(6):
                wide[x, 7:8, :] = low_ref[base + x : base + x + 1, :]
                wide[x, 24:25, :] = high_ref[base + x : base + x + 1, :]

    by_parity(lax.axis_index("slab"), x_sides, x_a_ref, x_b_ref)
    by_parity(lax.axis_index("pencil"), y_sides, y_a_ref, y_b_ref)
    field = wide_field[...]
    center = field[1:7]
    residual = (16.0 / 3.0 - wide_coef[...]) * center - (2.0 / 3.0) * smooth(field) - wide_source[...]
    grad_ref[...] = (16.0 / 3.0 - wide_coef[1:5]) * residual[1:5] - (2.0 / 3.0) * smooth(residual)
    for y in range(CY):
        high, low = act_parts(slope_ref, grad_ref, y)
        both = nt_dot(table_ref[...], high)
        modes_ref[y] = both[:32] + both[32:] + nt_dot(table_ref[0:32, :], low)
    position = lax.axis_index("pencil")
    forward = functools.partial(pencil_forward, modes_ref, phase_ref)
    by_parity(position, forward, own_ref, other_ref)


def combine_kernel(own_in_ref, got_in_ref, own_ref, got_ref, out_ref):
    out_ref[:, 0:64, :] = own_in_ref[...] + got_in_ref[...]
    out_ref[:, 64:128, :] = own_ref[...] + got_ref[...]


def local_kernel(pointwise_ref, slope_ref, grad_ref, out_ref):
    rows = lax.broadcasted_iota(jnp.int32, (C, LANES), 0)
    lanes = lax.broadcasted_iota(jnp.int32, (C, LANES), 1)
    repeat = jnp.where(lanes % C == rows, 1.0, 0.0).astype(BF16)
    wide = jnp.dot(pointwise_ref[...], repeat, preferred_element_type=F32)
    wide = jnp.concatenate([wide] * CX, axis=0)
    rows = lax.broadcasted_iota(jnp.int32, (LANES, LANES), 0)
    lanes = lax.broadcasted_iota(jnp.int32, (LANES, LANES), 1)
    wide = jnp.where(rows // C == lanes // C, wide, 0.0).astype(BF16)
    wide = jnp.concatenate([wide, wide], axis=1)
    for y in range(CY):
        act = jnp.concatenate(act_parts(slope_ref, grad_ref, y), axis=0)
        out_ref[y] = jnp.dot(wide, act, preferred_element_type=F32)


def slab_forward_kernel(parts_ref, table_ref, out_ref, raw_ref):
    raw = parts_ref[0, 0:64, :]
    for source in range(1, N // 2):
        raw = raw + parts_ref[source, 0:64, :]
    raw_ref[0:64, :] = raw
    raw_ref[64:128, :] = jnp.zeros((64, LANES), F32)
    for kz in range(KZ):
        out_ref[SLAB_RANK[kz], 32:40, :] = raw_ref[pl.ds(kz, 8, stride=KZ), :]
    for ky in range(2):
        for half in range(2):
            pieces = []
            for part in range(2):
                rows = pl.ds(64 + ky * 32 + part * KZ + 8 * half, 8)
                total = parts_ref[0, rows, :]
                for source in range(1, N // 2):
                    total = total + parts_ref[source, rows, :]
                pieces.append([total] + [pltpu.roll(total, 32 * d, 1) for d in range(1, 4)])
            for owner in range(N):
                result = None
                for d in range(4):
                    for part in range(2):
                        row = owner * 8 + d * 2 + part
                        term = pieces[part][d] * table_ref[row : row + 1, :]
                        result = term if result is None else result + term
                out_ref[SLAB_RANK[owner], pl.ds(ky * KZ + 8 * half, 8), :] = result


def flat_modes(block, group):
    lane_group = lax.broadcasted_iota(jnp.int32, (KZ, LANES), 1) // C
    row = lax.broadcasted_iota(jnp.int32, (KZ, LANES), 0)
    picked = jnp.where(lane_group == group, block, 0.0)
    picked = picked + pltpu.roll(picked, 64, 1)
    picked = picked + pltpu.roll(picked, 32, 1)
    tiles = [
        jnp.sum(jnp.where(row == 4 * tile + lane_group, picked, 0.0), axis=0, keepdims=True)
        for tile in range(4)
    ]
    return jnp.concatenate(tiles, axis=1)


def split_3(values):
    high = values.astype(BF16)
    rest = values - high.astype(F32)
    middle = rest.astype(BF16)
    low = (rest - middle.astype(F32)).astype(BF16)
    return high, middle, low


def minus_i(values, even_row):
    return jnp.where(even_row, pltpu.roll(values, 7, 0), -pltpu.roll(values, 1, 0))


def input_modes_at(parts_ref, table_ref):
    row = lax.broadcasted_iota(jnp.int32, (8, LANES), 0)
    group = lax.broadcasted_iota(jnp.int32, (8, LANES), 1) // C
    even_row = row % 2 == 0
    totals = [[None] * 4 for _ in range(4)]
    for source in range(N):
        values = parts_ref[SLAB_RANK[source], 32:40, :]
        turned = minus_i(values, even_row)
        for shift in range(4):
            if shift:
                real, imag = pltpu.roll(values, 32 * shift, 1), pltpu.roll(turned, 32 * shift, 1)
            else:
                real, imag = values, turned
            for q in range(4):
                r = ((q * N + source) * 4 + shift) * 2
                term = real * table_ref[r : r + 1, :] + imag * table_ref[r + 1 : r + 2, :]
                last = totals[q][shift]
                totals[q][shift] = term if last is None else last + term
    lower, upper = [], []
    for q in range(4):
        lower.append(totals[q][0] + totals[q][1] + totals[q][2] + totals[q][3])
        result = None
        for shift in range(4):
            x = (group - shift) % 4
            cos = jnp.where(x == 0, 1.0, jnp.where(x == 2, -1.0, 0.0))
            sin = jnp.where(x == 1, -1.0, jnp.where(x == 3, 1.0, 0.0))
            term = cos * totals[q][shift] + sin * minus_i(totals[q][shift], even_row)
            result = term if result is None else result + term
        upper.append(result)
    return lower + upper


def back_kernel(parts_ref, weight_ref, table_ref, modes_ref, out_ref):
    total = parts_ref[0, 0:32, :]
    for source in range(1, N):
        total = total + parts_ref[source, 0:32, :]
    modes_ref[...] = total
    rows = lax.broadcasted_iota(jnp.int32, (KZ, KZ * C), 0)
    lanes = lax.broadcasted_iota(jnp.int32, (KZ, KZ * C), 1)
    mask = jnp.where(lanes // C == rows, 1.0, 0.0).astype(BF16)
    kz = lax.broadcasted_iota(jnp.int32, (KZ, LANES), 0)
    scale = jnp.where(kz == 0, 1.0 / CELLS, 2.0 / CELLS)
    for ky in range(2):
        block = total[ky * KZ : (ky + 1) * KZ]
        products = []
        for kx in range(2):
            real, imag = flat_modes(block, 2 * kx), flat_modes(block, 2 * kx + 1)
            w_real = weight_ref[0, kx, ky].astype(F32)
            w_imag = weight_ref[1, kx, ky].astype(F32)
            products.append(w_real * real + w_imag * imag)
            products.append(w_real * imag - w_imag * real)
        high, middle, low = split_3(jnp.concatenate(products, axis=0))
        back = scale * (nt_dot(mask, high) + nt_dot(mask, middle) + nt_dot(mask, low))
        for device in range(N):
            out_ref[device, ky * KZ : (ky + 1) * KZ, :] = back
    inputs = input_modes_at(parts_ref, table_ref)
    for device in range(N):
        values = inputs[device // 2]
        if device % 2:
            values = pltpu.roll(values, 64, 1)
        out_ref[SLAB_RANK[device], 32:40, :] = values


def weight_grad_kernel(modes_ref, parts_ref, out_ref):
    rows = lax.broadcasted_iota(jnp.int32, (KZ, KZ * C), 0)
    lanes = lax.broadcasted_iota(jnp.int32, (KZ, KZ * C), 1)
    kz = sum(jnp.where(rows == rank, SLAB_ORDER[rank], 0) for rank in range(N))
    mask = jnp.where(lanes // C == kz, 1.0, 0.0).astype(BF16)
    first = lax.broadcasted_iota(jnp.int32, (1, KZ * C), 1) < C
    scale = jnp.where(first, 1.0 / CELLS, 2.0 / CELLS)
    for ky in range(2):
        grads = modes_ref[ky * KZ : (ky + 1) * KZ, :]
        spread = []
        for part in range(2):
            inputs = parts_ref[pl.ds(32 + 2 * ky + part, KZ, stride=40), :]
            high, middle, low = split_3(inputs)
            spread.append(tn_dot(high, mask) + tn_dot(middle, mask) + tn_dot(low, mask))
        for kx in range(2):
            real = scale * flat_modes(grads, 2 * kx)
            imag = scale * flat_modes(grads, 2 * kx + 1)
            in_real, in_imag = [part[kx * C : (kx + 1) * C] for part in spread]
            out_ref[0, kx, ky] = (in_real * real + in_imag * imag).astype(BF16)
            out_ref[1, kx, ky] = (in_real * imag - in_imag * real).astype(BF16)


def slab_backward_kernel(parts_ref, table_ref, out_ref):
    for ky in range(2):
        for half in range(2):
            totals = [[None] * 4, [None] * 4]
            for source in range(N):
                values = parts_ref[SLAB_RANK[source], pl.ds(ky * KZ + 8 * half, 8), :]
                for d in range(4):
                    for part in range(2):
                        row = source * 8 + d * 2 + part
                        term = values * table_ref[row : row + 1, :]
                        last = totals[part][d]
                        totals[part][d] = term if last is None else last + term
            for part in range(2):
                result = totals[part][0]
                for d in range(1, 4):
                    result = result + pltpu.roll(totals[part][d], 32 * d, 1)
                for device in range(N // 2):
                    out_ref[device, pl.ds(ky * 32 + part * KZ + 8 * half, 8), :] = result


def turn_modes(phase_ref, modes_ref, parts_refs):
    def turned(index, w_cos, w_sin, rows):
        ref = parts_refs[index // 2 % 2]
        row = (index % 2) * 32 + rows
        chip = CHIP_RANK[index // 4]
        real = ref[chip, pl.ds(row, 8), :]
        imag = ref[chip, pl.ds(row + KZ, 8), :]
        return w_cos * real - w_sin * imag, w_cos * imag + w_sin * real

    for half in range(2):
        for k in range(17):
            w_cos = phase_ref[k : k + 1, :]
            w_sin = phase_ref[17 + k : 18 + k, :]
            if k == 0:
                even = turned(0, w_cos, w_sin, 8 * half)
                odd = None
            elif k == 16:
                even = turned(16, w_cos, -w_sin, 8 * half)
                odd = [-part for part in even]
            else:
                plus = turned(k, w_cos, w_sin, 8 * half)
                minus = turned(32 - k, w_cos, -w_sin, 8 * half)
                even = [p + m for p, m in zip(plus, minus)]
                odd = [p - m for p, m in zip(plus, minus)]
            for part in range(2):
                modes_ref[half, 0, k, part] = even[part]
                if odd is not None:
                    modes_ref[half, 1, k, part] = odd[part]


def output_kernel(
    phase_ref,
    own_ref,
    other_ref,
    local_ref,
    table_ref,
    out_ref,
    modes_ref,
    rows_ref,
    flat_ref,
):
    position = lax.axis_index("pencil")
    turn = functools.partial(turn_modes, phase_ref, modes_ref)
    by_parity(position, turn, own_ref, other_ref)
    for half in range(2):
        for y in range(8):
            even = [modes_ref[half, 0, 0, 0], modes_ref[half, 0, 0, 1]]
            odd = [None, None]
            for k in range(1, 17):
                angle = 2.0 * math.pi * k * (y - 7.5) / NY
                cos, sin = math.cos(angle), math.sin(angle)
                for part in range(2):
                    even[part] = even[part] + cos * modes_ref[half, 0, k, part]
                    term = sin * modes_ref[half, 1, k, part]
                    odd[part] = term if odd[part] is None else odd[part] + term
            rows = pl.ds(8 * half, 8)
            more = pl.ds(KZ + 8 * half, 8)
            rows_ref[y, rows, :] = even[0] - odd[1]
            rows_ref[y, more, :] = even[1] + odd[0]
            rows_ref[15 - y, rows, :] = even[0] + odd[1]
            rows_ref[15 - y, more, :] = even[1] - odd[0]
    for y in range(CY):
        values = rows_ref[y]
        high = values.astype(BF16)
        low = (values - high.astype(F32)).astype(BF16)
        stacked = jnp.concatenate([high, low, high], axis=0)
        result = tn_dot(stacked, table_ref[...]) + local_ref[y]
        for x in range(CX):
            for side in range(2):
                piece = result[x * C : (x + 1) * C, side * 128 : (side + 1) * 128]
                flat_ref[side, pl.ds(x * CY + y, C, stride=PITCH), :] = piece
    for side in range(2):
        for c in range(C):
            piece = flat_ref[side, c * PITCH : c * PITCH + CX * CY].astype(BF16)
            out_ref[c, :, :, side * 128 : (side + 1) * 128] = piece.reshape(CX, CY, 128)


def call(kernel, name, out, scratch=(), scalars=(), hbm=(), us=1):
    def run(*args):
        args = [
            pltpu.with_memory_space_constraint(arg, pltpu.HBM) if i in hbm else arg
            for i, arg in enumerate(args)
        ]
        single = not isinstance(out, list)
        specs = [
            pl.BlockSpec(
                memory_space=pltpu.SMEM if i in scalars else pltpu.HBM if i in hbm else pltpu.VMEM
            )
            for i in range(len(args))
        ]
        shapes = [jax.ShapeDtypeStruct(*o) for o in ([out] if single else out)]
        result = pl.pallas_call(
            kernel,
            out_shape=shapes,
            in_specs=specs,
            out_specs=[pl.BlockSpec(memory_space=pltpu.VMEM)] * len(shapes),
            scratch_shapes=[pltpu.VMEM(*s) if isinstance(s, tuple) else s for s in scratch],
            compiler_params=pltpu.CompilerParams(vmem_limit_bytes=VMEM_LIMIT),
            cost_estimate=pl.CostEstimate(
                flops=0, transcendentals=0, bytes_accessed=int(us * BYTES_PER_US)
            ),
            name=name,
        )(*args)
        return result[0] if single else result

    return run


def shards(
    layer_input, pre_activation, coefficient, source, projection, pointwise, spectral_weight
):
    swap = [(i, i ^ 1) for i in range(N)]
    swap_odd = [(i, (i + 1 if i % 2 else i - 1) % N) for i in range(N)]
    same_core = [[2 * chip + core for chip in CHIP_ORDER] for core in range(2)]
    all_slabs = [SLAB_ORDER]
    edge = ((4, CY, NZ), F32)
    (
        field,
        edge_a,
        edge_b,
        pre_activation,
        coefficient,
        source,
        proj_tile,
        phases,
        depth_forward,
    ) = call(
        field_kernel,
        "field",
        [
            ((CX, CY, NZ), F32),
            edge,
            edge,
            ((C, CX, CY, NZ), BF16),
            ((CX, CY, NZ), BF16),
            ((CX, CY, NZ), BF16),
            ((C, 128), F32),
            (PENCIL_PHASES.shape[1:], F32),
            (DEPTH_FORWARD.shape, BF16),
        ],
        scratch=[pltpu.SMEM((C,), F32), pltpu.SemaphoreType.DMA((CHUNKS + 5,))],
        hbm=(0, 1, 2, 3, 4, 5),
        us=4,
    )(
        pre_activation,
        coefficient,
        source,
        projection,
        jnp.asarray(PENCIL_PHASES),
        jnp.asarray(DEPTH_FORWARD),
    )
    x_a = lax.ppermute(edge_a, "slab", swap)
    x_b = lax.ppermute(edge_b, "slab", swap_odd)
    table = (SLAB_FORWARD.shape[1:], F32)
    slope, slab_forward, slab_backward, input_phases, depth_backward = call(
        slope_kernel,
        "slope",
        [
            ((2, CY * Y_PITCH, 128), F32),
            table,
            table,
            (INPUT_TABLE.shape, F32),
            (DEPTH_BACKWARD.shape, BF16),
        ],
        scratch=[pltpu.SemaphoreType.DMA((4,))],
        hbm=(2, 3, 4, 5),
        us=2,
    )(
        pre_activation,
        proj_tile,
        jnp.asarray(SLAB_FORWARD),
        jnp.asarray(SLAB_BACKWARD),
        jnp.asarray(INPUT_TABLE),
        jnp.asarray(DEPTH_BACKWARD),
    )
    half_modes = ((N // 2, 64, LANES), F32)
    own_in, other_in = call(
        input_kernel,
        "input_modes",
        [half_modes, half_modes],
        scratch=[
            ((2, C * PITCH, 128), F32),
            ((CY, 32, LANES), F32),
        ],
        us=2,
    )(phases, layer_input, depth_forward)
    x_a, x_b, slope, own_in, other_in = lax.optimization_barrier(
        (x_a, x_b, slope, own_in, other_in)
    )
    got_in = lax.ppermute(other_in, "pencil", swap)
    side_a, side_b = call(pack_kernel, "pack", [((32, NZ), F32), ((32, NZ), F32)])(
        field, coefficient, source, x_a, x_b
    )
    y_a = lax.ppermute(side_a, "pencil", swap)
    y_b = lax.ppermute(side_b, "pencil", swap_odd)
    y_a, y_b, got_in = lax.optimization_barrier((y_a, y_b, got_in))
    own, other, grad = call(
        grad_kernel,
        "grad_modes",
        [half_modes, half_modes, ((CX, 32, NZ), F32)],
        scratch=[
            ((8, 32, NZ), F32),
            ((6, 32, NZ), F32),
            ((6, 32, NZ), F32),
            ((CY, 32, LANES), F32),
        ],
        us=3,
    )(
        phases,
        field,
        coefficient,
        source,
        x_a,
        x_b,
        y_a,
        y_b,
        slope,
        depth_forward,
    )
    got = lax.ppermute(other, "pencil", swap)
    local = call(local_kernel, "local", ((CY, LANES, NZ), F32))(pointwise, slope, grad)
    got, local = lax.optimization_barrier((got, local))
    to_pencil = call(combine_kernel, "combine", ((N // 2, 128, LANES), F32))(
        own_in, got_in, own, got
    )
    from_pencil = lax.all_to_all(
        to_pencil, "pencil", 0, 0, axis_index_groups=same_core, tiled=True
    )
    chunks = ((N, 40, LANES), F32)
    to_slab = call(slab_forward_kernel, "slab_forward", chunks, scratch=[((128, LANES), F32)])(
        from_pencil, slab_forward
    )
    from_slab = lax.all_to_all(to_slab, "slab", 0, 0, axis_index_groups=all_slabs, tiled=True)
    modes, to_slab = call(back_kernel, "back", [((32, LANES), F32), chunks])(
        from_slab, spectral_weight, input_phases
    )
    from_slab = lax.all_to_all(to_slab, "slab", 0, 0, axis_index_groups=all_slabs, tiled=True)
    weight_grad = call(weight_grad_kernel, "weight_grad", (spectral_weight.shape, BF16))(
        modes, from_slab.reshape(N * 40, LANES)
    )
    to_pencil = call(slab_backward_kernel, "slab_backward", half_modes)(from_slab, slab_backward)
    own = lax.all_to_all(to_pencil, "pencil", 0, 0, axis_index_groups=same_core, tiled=True)
    other = lax.ppermute(own, "pencil", swap)
    input_grad = call(
        output_kernel,
        "output",
        ((C, CX, CY, NZ), BF16),
        scratch=[
            ((2, 2, 17, 2, 8, LANES), F32),
            ((CY, 32, LANES), F32),
            ((2, C * PITCH, 128), F32),
        ],
    )(phases, own, other, local, depth_backward)
    return (input_grad, weight_grad)


def solution(mesh):
    return jax.shard_map(
        shards,
        mesh=mesh,
        in_specs=(
            P(None, "slab", "pencil", None),
            P(None, "slab", "pencil", None),
            P("slab", "pencil", None),
            P("slab", "pencil", None),
            P(),
            P(),
            P(None, "slab", "pencil", None, None),
        ),
        out_specs=(P(None, "slab", "pencil", None), P(None, "slab", "pencil", None, None)),
        check_vma=False,
    )
```

```python
import functools
import math

import jax
import jax.numpy as jnp
import ml_dtypes
import numpy as np
from jax import lax
from jax.experimental import pallas as pl
from jax.experimental.pallas import tpu as pltpu
from jax.sharding import PartitionSpec as P

F32 = jnp.float32
BF16 = jnp.bfloat16
C, CX, CY, NZ = 32, 4, 16, 256
NX, NY = 64, 256
N = 16
KZ = 16
LANES = CX * C
SLAB_ORDER = [2 * (5 * i % 8) for i in range(8)] + [2 * (3 * i % 8) + 1 for i in range(8)]
SLAB_RANK = [SLAB_ORDER.index(device) for device in range(N)]
CHIP_ORDER = [0, 1, 3, 2, 6, 7, 5, 4]
CHIP_RANK = [CHIP_ORDER.index(chip) for chip in range(N // 2)]
CELLS = float(NX * NY * NZ)
VMEM_LIMIT = 24 * 1024 * 1024
PITCH = 68
Y_PITCH = LANES + 8
CHUNKS = 4
BYTES_PER_US = 3_690_000


def split_2(table):
    high = table.astype(ml_dtypes.bfloat16)
    low = (table - high.astype(np.float64)).astype(ml_dtypes.bfloat16)
    return high, low


def depth_tables():
    angles = 2.0 * math.pi * ((np.arange(KZ)[:, None] * np.arange(NZ)[None, :]) % NZ) / NZ
    table = np.concatenate([np.cos(angles), -np.sin(angles)], axis=0)
    high, low = split_2(table)
    return np.concatenate([high, low], axis=0), np.concatenate([high, high, low], axis=0)


def wave(index):
    return index if index < 16 else index - 32


def pencil_phases():
    position = 16.0 * np.arange(N)[:, None] + 7.5
    angles = 2.0 * math.pi * np.arange(17)[None, :] * position / NY
    rows = np.concatenate([np.cos(angles), np.sin(angles), np.zeros((N, 6))], axis=1)
    return np.repeat(rows[:, :, None], LANES, axis=2).astype(np.float32)


def slab_tables():
    forward = np.zeros((N, N, 4, 2, LANES))
    backward = np.zeros((N, N, 4, 2, LANES))
    for position in range(N):
        for other in range(N):
            for shift in range(4):
                for group in range(4):
                    k = wave(2 * other + group // 2)
                    lanes = slice(group * C, (group + 1) * C)
                    x = 4 * position + (group - shift) % 4
                    angle = 2.0 * math.pi * ((k * x) % NX) / NX
                    cos, sin = math.cos(angle), math.sin(angle)
                    forward[position, other, shift, 0, lanes] = cos if group % 2 == 0 else -sin
                    forward[position, other, shift, 1, lanes] = sin if group % 2 == 0 else cos
                    x = 4 * position + (group + shift) % 4
                    angle = 2.0 * math.pi * ((k * x) % NX) / NX
                    cos, sin = math.cos(angle), math.sin(angle)
                    backward[position, other, shift, 0, lanes] = cos if group % 2 == 0 else -sin
                    backward[position, other, shift, 1, lanes] = sin if group % 2 == 0 else cos
    shape = (N, N * 8, LANES)
    return forward.astype(np.float32).reshape(shape), backward.astype(np.float32).reshape(shape)


def input_table():
    table = np.zeros((4, N, 4, 2, LANES))
    for q in range(4):
        for device in range(N):
            for shift in range(4):
                for group in range(4):
                    other = (group - shift) % 4
                    angle = 2.0 * math.pi * (((4 * q + group) * (4 * device + other)) % NX) / NX
                    lanes = slice(group * C, (group + 1) * C)
                    table[q, device, shift, 0, lanes] = math.cos(angle)
                    table[q, device, shift, 1, lanes] = math.sin(angle)
    return table.astype(np.float32).reshape(-1, LANES)


DEPTH_FORWARD, DEPTH_BACKWARD = depth_tables()
PENCIL_PHASES = pencil_phases()
SLAB_FORWARD, SLAB_BACKWARD = slab_tables()
INPUT_TABLE = input_table()


def by_parity(position, function, first_ref, second_ref):
    @pl.when(position % 2 == 0)
    def _():
        function((first_ref, second_ref))

    @pl.when(position % 2 == 1)
    def _():
        function((second_ref, first_ref))


def field_kernel(
    pre_hbm,
    coef_hbm,
    source_hbm,
    proj_hbm,
    input_hbm,
    phase_hbm,
    table_hbm,
    field_ref,
    edge_a_ref,
    edge_b_ref,
    pre_ref,
    coef_ref,
    source_ref,
    input_ref,
    proj_tile_ref,
    phase_ref,
    table_ref,
    proj_ref,
    sems,
):
    size = C // CHUNKS
    copies = [pltpu.make_async_copy(proj_hbm, proj_ref, sems.at[CHUNKS])]
    for i in range(CHUNKS):
        part = pl.ds(i * size, size)
        copies.append(pltpu.make_async_copy(pre_hbm.at[part], pre_ref.at[part], sems.at[i]))
    copies.append(pltpu.make_async_copy(coef_hbm, coef_ref, sems.at[CHUNKS + 1]))
    copies.append(pltpu.make_async_copy(source_hbm, source_ref, sems.at[CHUNKS + 2]))
    copies.append(pltpu.make_async_copy(input_hbm, input_ref, sems.at[CHUNKS + 3]))
    phases = phase_hbm.at[lax.axis_index("pencil")]
    copies.append(pltpu.make_async_copy(phases, phase_ref, sems.at[CHUNKS + 4]))
    copies.append(pltpu.make_async_copy(table_hbm, table_ref, sems.at[CHUNKS + 5]))
    for copy in copies:
        copy.start()
    copies[0].wait()
    for c in range(C):
        proj_tile_ref[c : c + 1, :] = jnp.full((1, 128), proj_ref[c], F32)

    def add_channel(c, total):
        values = pre_ref[c].astype(F32)
        both = values + values * lax.erf(values * math.sqrt(0.5))
        return total + (0.5 * proj_ref[c]) * both

    total = jnp.zeros((CX, CY, NZ), F32)
    for i in range(CHUNKS):
        copies[1 + i].wait()
        total = lax.fori_loop(i * size, (i + 1) * size, add_channel, total, unroll=2)
    for copy in copies[1 + CHUNKS :]:
        copy.wait()
    field_ref[...] = total

    def edges(refs):
        up_ref, down_ref = refs
        up_ref[0:2] = total[2:4]
        down_ref[0:2] = total[0:2]
        up_ref[2] = coef_ref[3].astype(F32)
        up_ref[3] = source_ref[3].astype(F32)
        down_ref[2] = coef_ref[0].astype(F32)
        down_ref[3] = source_ref[0].astype(F32)

    by_parity(lax.axis_index("slab"), edges, edge_a_ref, edge_b_ref)


def slope_kernel(
    pre_ref,
    proj_ref,
    forward_hbm,
    backward_hbm,
    input_hbm,
    depth_hbm,
    slope_ref,
    forward_ref,
    backward_ref,
    input_ref,
    depth_ref,
    sems,
):
    slab = lax.axis_index("slab")
    copies = [
        pltpu.make_async_copy(forward_hbm.at[slab], forward_ref, sems.at[0]),
        pltpu.make_async_copy(backward_hbm.at[slab], backward_ref, sems.at[1]),
        pltpu.make_async_copy(input_hbm, input_ref, sems.at[2]),
        pltpu.make_async_copy(depth_hbm, depth_ref, sems.at[3]),
    ]
    for copy in copies:
        copy.start()

    def one_channel(c, carry):
        values = pre_ref[c].astype(F32)
        below = 0.5 + 0.5 * lax.erf(values * math.sqrt(0.5))
        bell = jnp.exp(-0.5 * values * values)
        slope = below + values * (bell * (1.0 / math.sqrt(2.0 * math.pi)))
        weight = proj_ref[pl.ds(c, 1), :]
        for x in range(CX):
            for side in range(2):
                piece = slope[x, :, side * 128 : (side + 1) * 128] * weight
                slope_ref[side, pl.ds(x * C + c, CY, stride=Y_PITCH), :] = piece
        return carry

    lax.fori_loop(0, C, one_channel, 0, unroll=2)
    for copy in copies:
        copy.wait()


def nt_dot(left, right):
    return lax.dot_general(left, right, (((1,), (1,)), ((), ())), preferred_element_type=F32)


def tn_dot(left, right):
    return lax.dot_general(left, right, (((0,), (0,)), ((), ())), preferred_element_type=F32)


def pencil_forward(modes_ref, phase_ref, out_refs):
    for half in range(2):
        sums, diffs = [], []
        for part in range(2):
            rows = pl.ds(part * KZ + 8 * half, 8)
            first = [modes_ref[j, rows, :] for j in range(8)]
            second = [modes_ref[15 - j, rows, :] for j in range(8)]
            sums.append([a + b for a, b in zip(first, second)])
            diffs.append([a - b for a, b in zip(first, second)])
        for k in range(17):
            cosines = [math.cos(2.0 * math.pi * k * (7.5 - j) / NY) for j in range(8)]
            sines = [math.sin(2.0 * math.pi * k * (7.5 - j) / NY) for j in range(8)]
            even = [sum(w * v for w, v in zip(cosines, part)) for part in sums]
            w_cos = phase_ref[k : k + 1, :]
            w_sin = phase_ref[17 + k : 18 + k, :]
            if k == 0:
                results = [(0, even[0], even[1], w_sin)]
            else:
                odd = [sum(w * v for w, v in zip(sines, part)) for part in diffs]
                results = [(32 - k, even[0] + odd[1], even[1] - odd[0], -w_sin)]
                if k < 16:
                    results.append((k, even[0] - odd[1], even[1] + odd[0], w_sin))
            for index, real, imag, sin in results:
                row = (index % 2) * 32 + 8 * half
                out_ref = out_refs[index // 2 % 2]
                chip = CHIP_RANK[index // 4]
                out_ref[chip, pl.ds(row, 8), :] = w_cos * real + sin * imag
                out_ref[chip, pl.ds(row + KZ, 8), :] = w_cos * imag - sin * real


def input_kernel(
    phase_ref,
    input_ref,
    table_ref,
    own_ref,
    other_ref,
    rows_ref,
    modes_ref,
):
    for side in range(2):
        for c in range(C):
            piece = input_ref[c, :, :, side * 128 : (side + 1) * 128].astype(F32)
            rows_ref[side, c * PITCH : c * PITCH + CX * CY, :] = piece.reshape(CX * CY, 128)
    for y in range(CY):
        sides = [
            jnp.concatenate(
                [rows_ref[side, pl.ds(x * CY + y, C, stride=PITCH), :] for x in range(CX)], axis=0
            )
            for side in range(2)
        ]
        values = jnp.concatenate(sides, axis=1).astype(BF16)
        both = nt_dot(table_ref[...], values)
        modes_ref[y] = both[:32] + both[32:]
    position = lax.axis_index("pencil")
    forward = functools.partial(pencil_forward, modes_ref, phase_ref)
    by_parity(position, forward, own_ref, other_ref)


def pack_kernel(field_ref, coef_ref, source_ref, got_a_ref, got_b_ref, out_a_ref, out_b_ref):
    def pack(x_refs, y_refs):
        after_ref, before_ref = x_refs
        up_ref, down_ref = y_refs
        for out_ref, first in ((up_ref, 14), (down_ref, 0)):
            cells = slice(first, first + 2)
            cell = slice(15, 16) if first else slice(0, 1)
            for x in range(8):
                if x < 2:
                    rows = before_ref[x, cells, :]
                elif x < 6:
                    rows = field_ref[x - 2, cells, :]
                else:
                    rows = after_ref[x - 6, cells, :]
                out_ref[2 * x : 2 * x + 2, :] = rows
            for base, part, own_ref in ((16, 2, coef_ref), (22, 3, source_ref)):
                for x in range(6):
                    if x == 0:
                        row = before_ref[part, cell, :]
                    elif x == 5:
                        row = after_ref[part, cell, :]
                    else:
                        row = own_ref[x - 1].astype(F32)[cell, :]
                    out_ref[base + x : base + x + 1, :] = row
            out_ref[28:32, :] = jnp.zeros((4, NZ), F32)

    def with_x(x_refs):
        y = lax.axis_index("pencil")
        by_parity(y, functools.partial(pack, x_refs), out_a_ref, out_b_ref)

    by_parity(lax.axis_index("slab"), with_x, got_a_ref, got_b_ref)


def smooth(values):
    values = values + 0.5 * (pltpu.roll(values, 1, 2) + pltpu.roll(values, NZ - 1, 2))
    values = values + 0.5 * (pltpu.roll(values, 1, 1) + pltpu.roll(values, 31, 1))
    return 0.5 * (values[:-2] + values[2:]) + values[1:-1]


def act_parts(slope_ref, grad_ref, y):
    grads = []
    for x in range(CX):
        rows = slice(y * Y_PITCH + x * C, y * Y_PITCH + (x + 1) * C)
        slope = jnp.concatenate([slope_ref[0, rows, :], slope_ref[1, rows, :]], axis=1)
        grads.append(slope * grad_ref[x, 8 + y : 9 + y, :])
    act = jnp.concatenate(grads, axis=0)
    high = act.astype(BF16)
    return high, (act - high.astype(F32)).astype(BF16)


def grad_kernel(
    phase_ref,
    field_ref,
    coef_ref,
    source_ref,
    x_a_ref,
    x_b_ref,
    y_a_ref,
    y_b_ref,
    slope_ref,
    table_ref,
    own_ref,
    other_ref,
    grad_ref,
    wide_field,
    wide_coef,
    wide_source,
    modes_ref,
):
    own = slice(8, 24)
    wide_field[2:6, own, :] = field_ref[...]
    wide_coef[1:5, own, :] = coef_ref[...].astype(F32)
    wide_source[1:5, own, :] = source_ref[...].astype(F32)

    def x_sides(refs):
        after_ref, before_ref = refs
        wide_field[0:2, own, :] = before_ref[0:2]
        wide_field[6:8, own, :] = after_ref[0:2]
        for wide, part in ((wide_coef, 2), (wide_source, 3)):
            wide[0, own, :] = before_ref[part]
            wide[5, own, :] = after_ref[part]

    def y_sides(refs):
        high_ref, low_ref = refs
        for x in range(8):
            wide_field[x, 6:8, :] = low_ref[2 * x : 2 * x + 2, :]
            wide_field[x, 24:26, :] = high_ref[2 * x : 2 * x + 2, :]
        for wide, base in ((wide_coef, 16), (wide_source, 22)):
            for x in range(6):
                wide[x, 7:8, :] = low_ref[base + x : base + x + 1, :]
                wide[x, 24:25, :] = high_ref[base + x : base + x + 1, :]

    by_parity(lax.axis_index("slab"), x_sides, x_a_ref, x_b_ref)
    by_parity(lax.axis_index("pencil"), y_sides, y_a_ref, y_b_ref)
    field = wide_field[...]
    center = field[1:7]
    residual = (16.0 / 3.0 - wide_coef[...]) * center - (2.0 / 3.0) * smooth(field) - wide_source[...]
    grad_ref[...] = (16.0 / 3.0 - wide_coef[1:5]) * residual[1:5] - (2.0 / 3.0) * smooth(residual)
    for y in range(CY):
        high, low = act_parts(slope_ref, grad_ref, y)
        both = nt_dot(table_ref[...], high)
        modes_ref[y] = both[:32] + both[32:] + nt_dot(table_ref[0:32, :], low)
    position = lax.axis_index("pencil")
    forward = functools.partial(pencil_forward, modes_ref, phase_ref)
    by_parity(position, forward, own_ref, other_ref)


def combine_kernel(own_in_ref, got_in_ref, own_ref, got_ref, out_ref):
    out_ref[:, 0:64, :] = own_in_ref[...] + got_in_ref[...]
    out_ref[:, 64:128, :] = own_ref[...] + got_ref[...]


def local_kernel(pointwise_ref, slope_ref, grad_ref, out_ref):
    rows = lax.broadcasted_iota(jnp.int32, (C, LANES), 0)
    lanes = lax.broadcasted_iota(jnp.int32, (C, LANES), 1)
    repeat = jnp.where(lanes % C == rows, 1.0, 0.0).astype(BF16)
    wide = jnp.dot(pointwise_ref[...], repeat, preferred_element_type=F32)
    wide = jnp.concatenate([wide] * CX, axis=0)
    rows = lax.broadcasted_iota(jnp.int32, (LANES, LANES), 0)
    lanes = lax.broadcasted_iota(jnp.int32, (LANES, LANES), 1)
    wide = jnp.where(rows // C == lanes // C, wide, 0.0).astype(BF16)
    wide = jnp.concatenate([wide, wide], axis=1)
    for y in range(CY):
        act = jnp.concatenate(act_parts(slope_ref, grad_ref, y), axis=0)
        out_ref[y] = jnp.dot(wide, act, preferred_element_type=F32)


def slab_forward_kernel(parts_ref, table_ref, out_ref, raw_ref):
    raw = parts_ref[0, 0:64, :]
    for source in range(1, N // 2):
        raw = raw + parts_ref[source, 0:64, :]
    raw_ref[0:64, :] = raw
    raw_ref[64:128, :] = jnp.zeros((64, LANES), F32)
    for kz in range(KZ):
        out_ref[SLAB_RANK[kz], 32:40, :] = raw_ref[pl.ds(kz, 8, stride=KZ), :]
    for ky in range(2):
        for half in range(2):
            pieces = []
            for part in range(2):
                rows = pl.ds(64 + ky * 32 + part * KZ + 8 * half, 8)
                total = parts_ref[0, rows, :]
                for source in range(1, N // 2):
                    total = total + parts_ref[source, rows, :]
                pieces.append([total] + [pltpu.roll(total, 32 * d, 1) for d in range(1, 4)])
            for owner in range(N):
                result = None
                for d in range(4):
                    for part in range(2):
                        row = owner * 8 + d * 2 + part
                        term = pieces[part][d] * table_ref[row : row + 1, :]
                        result = term if result is None else result + term
                out_ref[SLAB_RANK[owner], pl.ds(ky * KZ + 8 * half, 8), :] = result


def flat_modes(block, group):
    lane_group = lax.broadcasted_iota(jnp.int32, (KZ, LANES), 1) // C
    row = lax.broadcasted_iota(jnp.int32, (KZ, LANES), 0)
    picked = jnp.where(lane_group == group, block, 0.0)
    picked = picked + pltpu.roll(picked, 64, 1)
    picked = picked + pltpu.roll(picked, 32, 1)
    tiles = [
        jnp.sum(jnp.where(row == 4 * tile + lane_group, picked, 0.0), axis=0, keepdims=True)
        for tile in range(4)
    ]
    return jnp.concatenate(tiles, axis=1)


def split_3(values):
    high = values.astype(BF16)
    rest = values - high.astype(F32)
    middle = rest.astype(BF16)
    low = (rest - middle.astype(F32)).astype(BF16)
    return high, middle, low


def minus_i(values, even_row):
    return jnp.where(even_row, pltpu.roll(values, 7, 0), -pltpu.roll(values, 1, 0))


def input_modes_at(parts_ref, table_ref):
    row = lax.broadcasted_iota(jnp.int32, (8, LANES), 0)
    group = lax.broadcasted_iota(jnp.int32, (8, LANES), 1) // C
    even_row = row % 2 == 0
    totals = [[None] * 4 for _ in range(4)]
    for source in range(N):
        values = parts_ref[SLAB_RANK[source], 32:40, :]
        turned = minus_i(values, even_row)
        for shift in range(4):
            if shift:
                real, imag = pltpu.roll(values, 32 * shift, 1), pltpu.roll(turned, 32 * shift, 1)
            else:
                real, imag = values, turned
            for q in range(4):
                r = ((q * N + source) * 4 + shift) * 2
                term = real * table_ref[r : r + 1, :] + imag * table_ref[r + 1 : r + 2, :]
                last = totals[q][shift]
                totals[q][shift] = term if last is None else last + term
    lower, upper = [], []
    for q in range(4):
        lower.append(totals[q][0] + totals[q][1] + totals[q][2] + totals[q][3])
        result = None
        for shift in range(4):
            x = (group - shift) % 4
            cos = jnp.where(x == 0, 1.0, jnp.where(x == 2, -1.0, 0.0))
            sin = jnp.where(x == 1, -1.0, jnp.where(x == 3, 1.0, 0.0))
            term = cos * totals[q][shift] + sin * minus_i(totals[q][shift], even_row)
            result = term if result is None else result + term
        upper.append(result)
    return lower + upper


def back_kernel(parts_ref, weight_ref, table_ref, modes_ref, out_ref):
    total = parts_ref[0, 0:32, :]
    for source in range(1, N):
        total = total + parts_ref[source, 0:32, :]
    modes_ref[...] = total
    rows = lax.broadcasted_iota(jnp.int32, (KZ, KZ * C), 0)
    lanes = lax.broadcasted_iota(jnp.int32, (KZ, KZ * C), 1)
    mask = jnp.where(lanes // C == rows, 1.0, 0.0).astype(BF16)
    kz = lax.broadcasted_iota(jnp.int32, (KZ, LANES), 0)
    scale = jnp.where(kz == 0, 1.0 / CELLS, 2.0 / CELLS)
    for ky in range(2):
        block = total[ky * KZ : (ky + 1) * KZ]
        products = []
        for kx in range(2):
            real, imag = flat_modes(block, 2 * kx), flat_modes(block, 2 * kx + 1)
            w_real = weight_ref[0, kx, ky].astype(F32)
            w_imag = weight_ref[1, kx, ky].astype(F32)
            products.append(w_real * real + w_imag * imag)
            products.append(w_real * imag - w_imag * real)
        high, middle, low = split_3(jnp.concatenate(products, axis=0))
        back = scale * (nt_dot(mask, high) + nt_dot(mask, middle) + nt_dot(mask, low))
        for device in range(N):
            out_ref[device, ky * KZ : (ky + 1) * KZ, :] = back
    inputs = input_modes_at(parts_ref, table_ref)
    for device in range(N):
        values = inputs[device // 2]
        if device % 2:
            values = pltpu.roll(values, 64, 1)
        out_ref[SLAB_RANK[device], 32:40, :] = values


def weight_grad_kernel(modes_ref, parts_ref, out_ref):
    rows = lax.broadcasted_iota(jnp.int32, (KZ, KZ * C), 0)
    lanes = lax.broadcasted_iota(jnp.int32, (KZ, KZ * C), 1)
    kz = sum(jnp.where(rows == rank, SLAB_ORDER[rank], 0) for rank in range(N))
    mask = jnp.where(lanes // C == kz, 1.0, 0.0).astype(BF16)
    first = lax.broadcasted_iota(jnp.int32, (1, KZ * C), 1) < C
    scale = jnp.where(first, 1.0 / CELLS, 2.0 / CELLS)
    for ky in range(2):
        grads = modes_ref[ky * KZ : (ky + 1) * KZ, :]
        spread = []
        for part in range(2):
            inputs = parts_ref[pl.ds(32 + 2 * ky + part, KZ, stride=40), :]
            high, middle, low = split_3(inputs)
            spread.append(tn_dot(high, mask) + tn_dot(middle, mask) + tn_dot(low, mask))
        for kx in range(2):
            real = scale * flat_modes(grads, 2 * kx)
            imag = scale * flat_modes(grads, 2 * kx + 1)
            in_real, in_imag = [part[kx * C : (kx + 1) * C] for part in spread]
            out_ref[0, kx, ky] = (in_real * real + in_imag * imag).astype(BF16)
            out_ref[1, kx, ky] = (in_real * imag - in_imag * real).astype(BF16)


def slab_backward_kernel(parts_ref, table_ref, out_ref):
    for ky in range(2):
        for half in range(2):
            totals = [[None] * 4, [None] * 4]
            for source in range(N):
                values = parts_ref[SLAB_RANK[source], pl.ds(ky * KZ + 8 * half, 8), :]
                for d in range(4):
                    for part in range(2):
                        row = source * 8 + d * 2 + part
                        term = values * table_ref[row : row + 1, :]
                        last = totals[part][d]
                        totals[part][d] = term if last is None else last + term
            for part in range(2):
                result = totals[part][0]
                for d in range(1, 4):
                    result = result + pltpu.roll(totals[part][d], 32 * d, 1)
                for device in range(N // 2):
                    out_ref[device, pl.ds(ky * 32 + part * KZ + 8 * half, 8), :] = result


def turn_modes(phase_ref, modes_ref, parts_refs):
    def turned(index, w_cos, w_sin, rows):
        ref = parts_refs[index // 2 % 2]
        row = (index % 2) * 32 + rows
        chip = CHIP_RANK[index // 4]
        real = ref[chip, pl.ds(row, 8), :]
        imag = ref[chip, pl.ds(row + KZ, 8), :]
        return w_cos * real - w_sin * imag, w_cos * imag + w_sin * real

    for half in range(2):
        for k in range(17):
            w_cos = phase_ref[k : k + 1, :]
            w_sin = phase_ref[17 + k : 18 + k, :]
            if k == 0:
                even = turned(0, w_cos, w_sin, 8 * half)
                odd = None
            elif k == 16:
                even = turned(16, w_cos, -w_sin, 8 * half)
                odd = [-part for part in even]
            else:
                plus = turned(k, w_cos, w_sin, 8 * half)
                minus = turned(32 - k, w_cos, -w_sin, 8 * half)
                even = [p + m for p, m in zip(plus, minus)]
                odd = [p - m for p, m in zip(plus, minus)]
            for part in range(2):
                modes_ref[half, 0, k, part] = even[part]
                if odd is not None:
                    modes_ref[half, 1, k, part] = odd[part]


def output_kernel(
    phase_ref,
    own_ref,
    other_ref,
    local_ref,
    table_ref,
    out_ref,
    modes_ref,
    rows_ref,
    flat_ref,
):
    position = lax.axis_index("pencil")
    turn = functools.partial(turn_modes, phase_ref, modes_ref)
    by_parity(position, turn, own_ref, other_ref)
    for half in range(2):
        for y in range(8):
            even = [modes_ref[half, 0, 0, 0], modes_ref[half, 0, 0, 1]]
            odd = [None, None]
            for k in range(1, 17):
                angle = 2.0 * math.pi * k * (y - 7.5) / NY
                cos, sin = math.cos(angle), math.sin(angle)
                for part in range(2):
                    even[part] = even[part] + cos * modes_ref[half, 0, k, part]
                    term = sin * modes_ref[half, 1, k, part]
                    odd[part] = term if odd[part] is None else odd[part] + term
            rows = pl.ds(8 * half, 8)
            more = pl.ds(KZ + 8 * half, 8)
            rows_ref[y, rows, :] = even[0] - odd[1]
            rows_ref[y, more, :] = even[1] + odd[0]
            rows_ref[15 - y, rows, :] = even[0] + odd[1]
            rows_ref[15 - y, more, :] = even[1] - odd[0]
    for y in range(CY):
        values = rows_ref[y]
        high = values.astype(BF16)
        low = (values - high.astype(F32)).astype(BF16)
        stacked = jnp.concatenate([high, low, high], axis=0)
        result = tn_dot(stacked, table_ref[...]) + local_ref[y]
        for x in range(CX):
            for side in range(2):
                piece = result[x * C : (x + 1) * C, side * 128 : (side + 1) * 128]
                flat_ref[side, pl.ds(x * CY + y, C, stride=PITCH), :] = piece
    for side in range(2):
        for c in range(C):
            piece = flat_ref[side, c * PITCH : c * PITCH + CX * CY].astype(BF16)
            out_ref[c, :, :, side * 128 : (side + 1) * 128] = piece.reshape(CX, CY, 128)


def call(kernel, name, out, scratch=(), scalars=(), hbm=(), us=1):
    def run(*args):
        args = [
            pltpu.with_memory_space_constraint(arg, pltpu.HBM) if i in hbm else arg
            for i, arg in enumerate(args)
        ]
        single = not isinstance(out, list)
        specs = [
            pl.BlockSpec(
                memory_space=pltpu.SMEM if i in scalars else pltpu.HBM if i in hbm else pltpu.VMEM
            )
            for i in range(len(args))
        ]
        shapes = [jax.ShapeDtypeStruct(*o) for o in ([out] if single else out)]
        result = pl.pallas_call(
            kernel,
            out_shape=shapes,
            in_specs=specs,
            out_specs=[pl.BlockSpec(memory_space=pltpu.VMEM)] * len(shapes),
            scratch_shapes=[pltpu.VMEM(*s) if isinstance(s, tuple) else s for s in scratch],
            compiler_params=pltpu.CompilerParams(vmem_limit_bytes=VMEM_LIMIT),
            cost_estimate=pl.CostEstimate(
                flops=0, transcendentals=0, bytes_accessed=int(us * BYTES_PER_US)
            ),
            name=name,
        )(*args)
        return result[0] if single else result

    return run


def shards(
    layer_input, pre_activation, coefficient, source, projection, pointwise, spectral_weight
):
    swap = [(i, i ^ 1) for i in range(N)]
    swap_odd = [(i, (i + 1 if i % 2 else i - 1) % N) for i in range(N)]
    same_core = [[2 * chip + core for chip in CHIP_ORDER] for core in range(2)]
    all_slabs = [SLAB_ORDER]
    edge = ((4, CY, NZ), F32)
    (
        field,
        edge_a,
        edge_b,
        pre_activation,
        coefficient,
        source,
        layer_input,
        proj_tile,
        phases,
        depth_forward,
    ) = call(
        field_kernel,
        "field",
        [
            ((CX, CY, NZ), F32),
            edge,
            edge,
            ((C, CX, CY, NZ), BF16),
            ((CX, CY, NZ), BF16),
            ((CX, CY, NZ), BF16),
            ((C, CX, CY, NZ), BF16),
            ((C, 128), F32),
            (PENCIL_PHASES.shape[1:], F32),
            (DEPTH_FORWARD.shape, BF16),
        ],
        scratch=[pltpu.SMEM((C,), F32), pltpu.SemaphoreType.DMA((CHUNKS + 6,))],
        hbm=(0, 1, 2, 3, 4, 5, 6),
        us=4,
    )(
        pre_activation,
        coefficient,
        source,
        projection,
        layer_input,
        jnp.asarray(PENCIL_PHASES),
        jnp.asarray(DEPTH_FORWARD),
    )
    x_a = lax.ppermute(edge_a, "slab", swap)
    x_b = lax.ppermute(edge_b, "slab", swap_odd)
    table = (SLAB_FORWARD.shape[1:], F32)
    slope, slab_forward, slab_backward, input_phases, depth_backward = call(
        slope_kernel,
        "slope",
        [
            ((2, CY * Y_PITCH, 128), F32),
            table,
            table,
            (INPUT_TABLE.shape, F32),
            (DEPTH_BACKWARD.shape, BF16),
        ],
        scratch=[pltpu.SemaphoreType.DMA((4,))],
        hbm=(2, 3, 4, 5),
        us=2,
    )(
        pre_activation,
        proj_tile,
        jnp.asarray(SLAB_FORWARD),
        jnp.asarray(SLAB_BACKWARD),
        jnp.asarray(INPUT_TABLE),
        jnp.asarray(DEPTH_BACKWARD),
    )
    half_modes = ((N // 2, 64, LANES), F32)
    own_in, other_in = call(
        input_kernel,
        "input_modes",
        [half_modes, half_modes],
        scratch=[
            ((2, C * PITCH, 128), F32),
            ((CY, 32, LANES), F32),
        ],
        us=2,
    )(phases, layer_input, depth_forward)
    got_in = lax.ppermute(other_in, "pencil", swap)
    x_a, x_b, slope, own_in, got_in = lax.optimization_barrier((x_a, x_b, slope, own_in, got_in))
    side_a, side_b = call(pack_kernel, "pack", [((32, NZ), F32), ((32, NZ), F32)])(
        field, coefficient, source, x_a, x_b
    )
    y_a = lax.ppermute(side_a, "pencil", swap)
    y_b = lax.ppermute(side_b, "pencil", swap_odd)
    own, other, grad = call(
        grad_kernel,
        "grad_modes",
        [half_modes, half_modes, ((CX, 32, NZ), F32)],
        scratch=[
            ((8, 32, NZ), F32),
            ((6, 32, NZ), F32),
            ((6, 32, NZ), F32),
            ((CY, 32, LANES), F32),
        ],
        us=3,
    )(
        phases,
        field,
        coefficient,
        source,
        x_a,
        x_b,
        y_a,
        y_b,
        slope,
        depth_forward,
    )
    got = lax.ppermute(other, "pencil", swap)
    local = call(local_kernel, "local", ((CY, LANES, NZ), F32))(pointwise, slope, grad)
    got, local = lax.optimization_barrier((got, local))
    to_pencil = call(combine_kernel, "combine", ((N // 2, 128, LANES), F32))(
        own_in, got_in, own, got
    )
    from_pencil = lax.all_to_all(
        to_pencil, "pencil", 0, 0, axis_index_groups=same_core, tiled=True
    )
    chunks = ((N, 40, LANES), F32)
    to_slab = call(slab_forward_kernel, "slab_forward", chunks, scratch=[((128, LANES), F32)])(
        from_pencil, slab_forward
    )
    from_slab = lax.all_to_all(to_slab, "slab", 0, 0, axis_index_groups=all_slabs, tiled=True)
    modes, to_slab = call(back_kernel, "back", [((32, LANES), F32), chunks])(
        from_slab, spectral_weight, input_phases
    )
    from_slab = lax.all_to_all(to_slab, "slab", 0, 0, axis_index_groups=all_slabs, tiled=True)
    weight_grad = call(weight_grad_kernel, "weight_grad", (spectral_weight.shape, BF16))(
        modes, from_slab.reshape(N * 40, LANES)
    )
    to_pencil = call(slab_backward_kernel, "slab_backward", half_modes)(from_slab, slab_backward)
    own = lax.all_to_all(to_pencil, "pencil", 0, 0, axis_index_groups=same_core, tiled=True)
    other = lax.ppermute(own, "pencil", swap)
    input_grad = call(
        output_kernel,
        "output",
        ((C, CX, CY, NZ), BF16),
        scratch=[
            ((2, 2, 17, 2, 8, LANES), F32),
            ((CY, 32, LANES), F32),
            ((2, C * PITCH, 128), F32),
        ],
    )(phases, own, other, local, depth_backward)
    return (input_grad, weight_grad)


def solution(mesh):
    return jax.shard_map(
        shards,
        mesh=mesh,
        in_specs=(
            P(None, "slab", "pencil", None),
            P(None, "slab", "pencil", None),
            P("slab", "pencil", None),
            P("slab", "pencil", None),
            P(),
            P(),
            P(None, "slab", "pencil", None, None),
        ),
        out_specs=(P(None, "slab", "pencil", None), P(None, "slab", "pencil", None, None)),
        check_vma=False,
    )
```
